32 devices in a mesh: dp: 8 (over z, x), tensor: 4 (over y, core).
Axes of the slice: x: 2, y: 2, z: 4, core: 2. Of those that a mesh axis runs over, the one named last changes fastest.
Arguments:
- tokens: bfloat16 [24576, 768], P(('dp', 'tensor')), may hold values from -6 to 6
- timesteps: int32 [192], P(('dp', 'tensor')), may hold values from 0 to 1999
- lengths: int32 [192], P('dp'), may hold values from 64 to 128, as said below
- time_inner: bfloat16 [128, 512], replicated, may hold values from -0.5 to 0.5
- time_ibias: bfloat16 [512], replicated, may hold values from -3 to 3
- time_outer: bfloat16 [512, 768], replicated, may hold values from -0.25 to 0.25
- time_obias: bfloat16 [768], replicated, may hold values from -1.75 to 1.75
- qkv_weight: bfloat16 [768, 3, 768], P(None, None, 'tensor'), may hold values from -0.21875 to 0.21875
- qv_bias: bfloat16 [2, 768], P(None, 'tensor'), may hold values from -3 to 3
- out_weight: bfloat16 [768, 768], P('tensor'), may hold values from -0.625 to 0.625
- out_bias: bfloat16 [768], replicated, may hold values from -1.75 to 1.75
- gain_first: bfloat16 [768], replicated, may hold values from 0.25 to 1.75
- shift_first: bfloat16 [768], replicated, may hold values from -1.75 to 1.75
- up_weight: bfloat16 [3072, 768], P('tensor'), may hold values from -0.21875 to 0.21875
- up_bias: bfloat16 [3072], P('tensor'), may hold values from -3 to 3
- down_weight: bfloat16 [3072, 768], P('tensor'), may hold values from -0.109375 to 0.109375
- down_bias: bfloat16 [768], replicated, may hold values from -1.75 to 1.75
- gain_second: bfloat16 [768], replicated, may hold values from 0.25 to 1.75
- shift_second: bfloat16 [768], replicated, may hold values from -1.75 to 1.75
- cotangent: bfloat16 [24576, 768], P(('dp', 'tensor')), may hold values from -6 to 6
Outputs:
- layer_out: bfloat16 [24576, 768], P(('dp', 'tensor'))
- grad_tokens: float32 [24576, 768], P(('dp', 'tensor'))
- grad_tinner: float32 [128, 512], replicated
- grad_tibias: float32 [512], replicated
- grad_touter: float32 [512, 768], replicated
- grad_tobias: float32 [768], replicated
- grad_qkv: float32 [768, 3, 768], P(None, None, 'tensor')
- grad_qvbias: float32 [2, 768], P(None, 'tensor')
- grad_wout: float32 [768, 768], P('tensor')
- grad_bout: float32 [768], replicated
- grad_gfirst: float32 [768], replicated
- grad_sfirst: float32 [768], replicated
- grad_wup: float32 [3072, 768], P('tensor')
- grad_bup: float32 [3072], P('tensor')
- grad_wdown: float32 [3072, 768], P('tensor')
- grad_bdown: float32 [768], replicated
- grad_gsecond: float32 [768], replicated
- grad_ssecond: float32 [768], replicated
The draws below stay inside these ranges and needn't reach their ends.
Inputs may be any that keep to these rules, and one draw needn't show every extreme that they name: `lengths`: each sequence has 64 or 128 tokens that are not padding; some sequence has 128.
All inputs are finite; a program needn't handle non-finite values.
Results may differ from the reference program's by a relative error of at most 0.018.
Values may be sent and summed in bfloat16 or wider, within the bound.
No kernel may reach another device: no remote copies, remote signals or barrier semaphores. Data moves between devices by JAX's collectives and lax.ppermute only.
A program may use at most 128 MiB of HBM per device.

```python
import math
import jax
import jax.numpy as jnp
from jax import lax

D = 768
HEADS = 12
FF = 3072
TIME_FEAT = 128
TIME_HID = 512
L = 128
STEPS = 2000
HEAD_DIM = 64
TOKENS = 24576
SEQS = 192


def draw_lengths(key, part):
    key = jax.random.fold_in(key, 7)
    pick_key, place_key = jax.random.split(key)
    halves = jax.random.randint(pick_key, (SEQS,), 1, 3)
    lengths = halves * (L // 2)
    chosen = jax.random.randint(place_key, (), 0, SEQS)
    return lengths.at[chosen].set(L).astype(jnp.int32)


def set_ends(values, key, low, high):
    extent = values.shape
    spot = [jax.random.randint(jax.random.fold_in(key, axis), (), 0, extent[axis]) for axis in range(len(extent))]
    values = values.at[tuple(spot)].set(low)
    longest = extent.index(max(extent))
    spot[longest] = (spot[longest] + 1) % extent[longest]
    return values.at[tuple(spot)].set(high)


def block_levels(own_key, shape, pieces, least, top_value):
    factor_of = 1.0
    for position, blocks in pieces:
        draws = jax.random.uniform(jax.random.fold_in(jax.random.fold_in(own_key, 6), position), (blocks,), jnp.float32, least / len(pieces), top_value / len(pieces))
        factor_of = factor_of * jnp.repeat(jnp.exp(draws), shape[position] // blocks).reshape((-1,) + (1,) * (len(shape) - 1 - position))
    return factor_of


def centred(stream_key, extent, scale, limit, cuts=(), kind=jnp.bfloat16):
    array = jax.random.normal(stream_key, extent, jnp.float32) * scale
    if len(cuts) > 0:
        array = block_levels(stream_key, extent, cuts, -0.22, 0.18) * array
    return jnp.clip(array, min=-limit, max=limit).astype(kind)


def setup_inputs(seed: int = 0) -> dict:
    splits = jax.random.split(jax.random.key(seed), 21)
    tokens = centred(splits[0], (TOKENS, D), 1.0, 6.0, ((0, 32),))
    timesteps = set_ends(jax.random.randint(splits[1], (SEQS,), 0, STEPS), jax.random.fold_in(splits[1], 1), 0, STEPS - 1).astype(jnp.int32)
    lengths = draw_lengths(jax.random.fold_in(splits[20], 71), 0)
    time_inner = centred(splits[3], (TIME_FEAT, TIME_HID), TIME_FEAT ** -0.5, 0.5)
    time_ibias = centred(splits[4], (TIME_HID,), 0.5, 3.0)
    time_outer = centred(splits[5], (TIME_HID, D), TIME_HID ** -0.5, 0.25)
    time_obias = centred(splits[6], (D,), 0.3, 1.75)
    qkv_weight = centred(splits[7], (D, 3, D), D ** -0.5, 0.21875, ((2, 4),))
    qv_bias = centred(splits[8], (2, D), 0.5, 3.0, ((1, 4),))
    out_weight = centred(splits[9], (D, D), (D * 16 // L) ** -0.5, 0.625, ((0, 4),))
    out_bias = centred(splits[10], (D,), 0.3, 1.75)
    gain_first = jnp.clip(1.0 + 0.15 * jax.random.normal(splits[11], (D,), jnp.float32), 0.25, 1.75).astype(jnp.bfloat16)
    shift_first = centred(splits[12], (D,), 0.3, 1.75)
    up_weight = centred(splits[13], (FF, D), D ** -0.5, 0.21875, ((0, 4),))
    up_bias = centred(splits[14], (FF,), 0.5, 3.0, ((0, 4),))
    down_weight = centred(splits[15], (FF, D), FF ** -0.5, 0.109375, ((0, 4),))
    down_bias = centred(splits[16], (D,), 0.3, 1.75)
    gain_second = jnp.clip(1.0 + 0.15 * jax.random.normal(splits[17], (D,), jnp.float32), 0.25, 1.75).astype(jnp.bfloat16)
    shift_second = centred(splits[18], (D,), 0.3, 1.75)
    cotangent = centred(splits[19], (TOKENS, D), 1.0, 6.0, ((0, 32),))
    return dict(tokens=tokens, timesteps=timesteps, lengths=lengths, time_inner=time_inner, time_ibias=time_ibias, time_outer=time_outer, time_obias=time_obias, qkv_weight=qkv_weight, qv_bias=qv_bias, out_weight=out_weight, out_bias=out_bias, gain_first=gain_first, shift_first=shift_first, up_weight=up_weight, up_bias=up_bias, down_weight=down_weight, down_bias=down_bias, gain_second=gain_second, shift_second=shift_second, cotangent=cotangent)


@jax.custom_vjp
def low(v):
    return lax.optimization_barrier(v.astype(jnp.bfloat16)).astype(jnp.float32)

@jax.custom_vjp
def low_back(v):
    return v

def low_keep(v):
    return (low(v), None)

def low_pass(kept, grad):
    return (grad,)

def back_keep(v):
    return (v, None)

def back_low(kept, grad):
    return (low(grad),)
low.defvjp(low_keep, low_pass)
low_back.defvjp(back_keep, back_low)
eps_norm = 1e-05

def matmul(left, right):
    return jnp.dot(left, right, precision=lax.Precision.HIGHEST, preferred_element_type=jnp.float32)

def layer_norm(value, gain, shift):
    centre = lax.optimization_barrier(jnp.mean(value, axis=-1, keepdims=True))
    spread = lax.optimization_barrier(jnp.mean(jnp.square(value - centre), axis=-1, keepdims=True))
    return (value - centre) * lax.rsqrt(spread + eps_norm) * gain + shift

def time_features(timesteps):
    half = TIME_FEAT // 2
    frequency = jnp.exp(-math.log(10000.0) * jnp.arange(half, dtype=jnp.float32) / half)
    angles = timesteps.astype(jnp.float32)[:, None] * frequency[None, :]
    return jnp.concatenate([jnp.cos(angles), jnp.sin(angles)], axis=1)

def attend(block):
    query, keys, values, valid = block
    scores = jnp.einsum('sqhd,skhd->shqk', query, keys, precision=lax.Precision.HIGHEST) * HEAD_DIM ** (-0.5)
    scores = jnp.where(valid[:, None, None, :], scores, -1e+30)
    scores = low_back(scores)
    top = lax.optimization_barrier(jnp.max(scores, axis=-1, keepdims=True))
    expo = jnp.exp(scores - top)
    probs = low(expo / lax.optimization_barrier(jnp.sum(expo, axis=-1, keepdims=True)))
    return jnp.einsum('shqk,skhd->sqhd', probs, values, precision=lax.Precision.HIGHEST)

def forward(params, features, valid):
    tokens, time_inner, time_ibias, time_outer, time_obias, qkv_weight, qv_bias, out_weight, out_bias, gain_first, shift_first, up_weight, up_bias, down_weight, down_bias, gain_second, shift_second = params
    hidden_time = jax.nn.silu(matmul(features, time_inner) + time_ibias)
    temb = matmul(hidden_time, time_outer) + time_obias
    start = (tokens.reshape(SEQS, L, D) + temb[:, None, :]).reshape(TOKENS, D)
    joined = matmul(low(start), qkv_weight.reshape(D, 3 * D)).reshape(TOKENS, 3, D)
    query = low(low_back(joined[:, 0] + qv_bias[0]))
    keys = low(low_back(joined[:, 1]))
    values = low(low_back(joined[:, 2] + qv_bias[1]))
    block = math.gcd(SEQS, max(1, 4096 // L))

    def blocked(value):
        return value.reshape(SEQS // block, block, L, HEADS, HEAD_DIM)
    mixed = lax.map(jax.checkpoint(attend), (blocked(query), blocked(keys), blocked(values), valid.reshape(SEQS // block, block, L)))
    mixed = low(low_back(mixed.reshape(TOKENS, D)))
    first = start + low_back(matmul(mixed, out_weight)) + out_bias
    normed = layer_norm(first, gain_first, shift_first)
    pre = low_back(matmul(low(normed), up_weight.T) + up_bias)
    act = low(jax.nn.gelu(pre, approximate=False))
    second = normed + low_back(matmul(act, down_weight)) + down_bias
    return layer_norm(second, gain_second, shift_second)

def reference(tokens, timesteps, lengths, time_inner, time_ibias, time_outer, time_obias, qkv_weight, qv_bias, out_weight, out_bias, gain_first, shift_first, up_weight, up_bias, down_weight, down_bias, gain_second, shift_second, cotangent):
    features = time_features(timesteps)
    valid = jnp.arange(L, dtype=jnp.int32)[None, :] < lengths[:, None]
    params = tuple((item.astype(jnp.float32) for item in (tokens, time_inner, time_ibias, time_outer, time_obias, qkv_weight, qv_bias, out_weight, out_bias, gain_first, shift_first, up_weight, up_bias, down_weight, down_bias, gain_second, shift_second)))

    def wrapped(inputs):
        return forward(inputs, features, valid)
    result, pullback = jax.vjp(wrapped, params)
    grads = pullback(cotangent.astype(jnp.float32))[0]
    return (result.astype(jnp.bfloat16), grads[0], grads[1], grads[2], grads[3], grads[4], grads[5], grads[6], grads[7], grads[8], grads[9], grads[10], grads[11], grads[12], grads[13], grads[14], grads[15], grads[16])
```

```python
import functools
import math

import jax
import jax.numpy as jnp
from jax import lax
from jax.experimental import pallas as pl
from jax.experimental.pallas import tpu as pltpu
from jax.sharding import PartitionSpec as P

L = 128
HD = 64
EPS = 1e-05
F32 = jnp.float32
BF = jnp.bfloat16
NN = ((1,), (0,))
NT = ((1,), (1,))
TN = ((0,), (0,))
VMEM_LIMIT = 56 * 1024 * 1024


def dot(left, right, dims):
    return lax.dot_general(left, right, (dims, ((), ())), preferred_element_type=F32)


def exact(left, right, dims):
    return lax.dot_general(
        left, right, (dims, ((), ())), precision=lax.Precision.HIGHEST, preferred_element_type=F32
    )


def call(body, outs, args, flops, scratch=(), smem=()):
    moved = sum(math.prod(o.shape) * o.dtype.itemsize for o in outs)
    moved += sum(math.prod(a.shape) * a.dtype.itemsize for a in args)
    return pl.pallas_call(
        body,
        out_shape=outs,
        in_specs=[
            pl.BlockSpec(memory_space=pltpu.SMEM if i in smem else pltpu.VMEM)
            for i in range(len(args))
        ],
        out_specs=[pl.BlockSpec(memory_space=pltpu.VMEM) for _ in outs],
        scratch_shapes=list(scratch),
        cost_estimate=pl.CostEstimate(flops=int(flops), bytes_accessed=int(moved), transcendentals=0),
        compiler_params=pltpu.CompilerParams(vmem_limit_bytes=VMEM_LIMIT),
    )(*args)


def sds(shape, dtype):
    return jax.ShapeDtypeStruct(shape, dtype)


def pieces(a, b, lo, hi):
    return [a[lo:hi, :], b[lo:hi, :]]


def head_mask(width):
    lane = lax.broadcasted_iota(jnp.int32, (1, width), 1)
    first = jnp.where(lane < width // 2, 1.0, 0.0)
    return first.astype(BF), (1.0 - first).astype(BF)


def doubled(pair, masks):
    return jnp.concatenate([pair * masks[0], pair * masks[1]], axis=0)


def joined_weight(a_ref, b_ref, w):
    parts = []
    for k in range(3):
        parts += pieces(a_ref, b_ref, k * w, (k + 1) * w)
    return jnp.concatenate(parts, axis=0)


def attn_fwd_core(x, a_ref, b_ref, len_ref, qkv_ref, p_ref, mix_ref):
    w = a_ref.shape[1] // 4
    rows = x.shape[0]
    seqs = rows // L
    wide = 2 * w
    big = joined_weight(a_ref, b_ref, w)
    base = 4 * w
    qb = (a_ref[base : base + 1, :] + b_ref[base + 1 : base + 2, :]).astype(F32)
    vb = (a_ref[base + 2 : base + 3, :] + b_ref[base + 3 : base + 4, :]).astype(F32)
    total = dot(x, big, NT)
    qkv_ref[:, :wide] = (total[:, :wide] + qb[:, :wide]).astype(BF)
    qkv_ref[:, wide : 2 * wide] = total[:, wide : 2 * wide].astype(BF)
    qkv_ref[:, 2 * wide :] = (total[:, 2 * wide :] + vb[:, :wide]).astype(BF)
    masks = head_mask(2 * HD)
    key_at = lax.broadcasted_iota(jnp.int32, (L, L), 0)
    pairs = wide // (2 * HD)

    def one(s, carry):
        at = pl.ds(pl.multiple_of(s * L, L), L)
        valid = key_at < len_ref[s]
        for pair in range(pairs):
            lo = pair * 2 * HD
            q = qkv_ref[at, lo : lo + 2 * HD]
            k = qkv_ref[at, wide + lo : wide + lo + 2 * HD]
            v = qkv_ref[at, 2 * wide + lo : 2 * wide + lo + 2 * HD]
            scores = dot(doubled(k, masks), q, NT) * HD ** (-0.5)
            lows = []
            for h in range(2):
                part = jnp.where(valid, scores[h * L : (h + 1) * L], -1e30)
                expo = jnp.exp(part - jnp.max(part, axis=0, keepdims=True))
                prob = expo * (1.0 / jnp.sum(expo, axis=0, keepdims=True))
                p_ref[s * pairs + pair, h * L : (h + 1) * L, :] = prob
                lows.append(prob.astype(BF))
            mixed = dot(jnp.concatenate(lows, axis=0), doubled(v, masks), TN)
            mix_ref[at, lo : lo + 2 * HD] = mixed.astype(BF)
        return carry

    lax.fori_loop(0, seqs, one, 0)
    out = jnp.concatenate(pieces(a_ref, b_ref, 3 * w, 4 * w), axis=0)
    return dot(mix_ref[...], out, NN)


def start_of(tok_ref, temb_ref):
    rows, width = tok_ref.shape
    seqs = rows // L
    return [
        tok_ref[s * L : (s + 1) * L, :].astype(F32) + temb_ref[s : s + 1, :] for s in range(seqs)
    ]


def attn_near_body(len_ref, tok_ref, temb_ref, a_ref, b_ref, x_ref, qkv_ref, p_ref, mix_ref, acc_ref):
    for s, rows in enumerate(start_of(tok_ref, temb_ref)):
        x_ref[s * L : (s + 1) * L, :] = rows.astype(BF)
    acc_ref[...] = attn_fwd_core(x_ref[...], a_ref, b_ref, len_ref, qkv_ref, p_ref, mix_ref)


def row_mean(value):
    return jnp.mean(value, axis=-1, keepdims=True)


def unit_of(value):
    centred = value - row_mean(value)
    rate = lax.rsqrt(row_mean(centred * centred) + EPS)
    return centred * rate, rate


def attn_far_body(
    len_ref, tok_ref, temb_ref, x_ref, a_ref, b_ref, near_ref, vec_ref,
    qkv_ref, p_ref, mix_ref, first_ref, low_ref,
):
    acc = attn_fwd_core(x_ref[...], a_ref, b_ref, len_ref, qkv_ref, p_ref, mix_ref)
    first_ref[...] = acc + near_ref[...] + vec_ref[0:1, :]
    for s, rows in enumerate(start_of(tok_ref, temb_ref)):
        at = slice(s * L, (s + 1) * L)
        first = first_ref[at, :] + rows
        first_ref[at, :] = first
        unit, _ = unit_of(first)
        low_ref[at, :] = (unit * vec_ref[1:2, :] + vec_ref[2:3, :]).astype(BF)


def gelu_pair(pre):
    cdf = 0.5 * (1.0 + lax.erf(pre * 0.7071067811865476))
    pdf = jnp.exp(-0.5 * pre * pre) * 0.3989422804014327
    return pre * cdf, cdf + pre * pdf


def mlp_fwd_core(x_ref, ups, downs, biases, act_ref, slope_ref, acc_ref):
    rows = x_ref.shape[0]
    hid = ups[0].shape[0]
    tile = 384 if hid % 384 == 0 else hid
    block = 256 if rows % 256 == 0 else rows
    first = True
    for r in range(len(ups)):
        for t in range(hid // tile):
            up = ups[r][t * tile : (t + 1) * tile, :]
            down = downs[r][t * tile : (t + 1) * tile, :]
            bias = biases[r][:, t * tile : (t + 1) * tile].astype(F32)
            lo = r * hid + t * tile
            for m in range(rows // block):
                at = slice(m * block, (m + 1) * block)
                act, slope = gelu_pair(dot(x_ref[at, :], up, NT) + bias)
                low = act.astype(BF)
                act_ref[at, lo : lo + tile] = low
                slope_ref[at, lo : lo + tile] = slope
                part = dot(low, down, NN)
                if first:
                    acc_ref[at, :] = part
                else:
                    acc_ref[at, :] += part
            first = False


def mlp_near_body(x_ref, ua, ub, da, db, ba, bb, act_ref, slope_ref, acc_ref):
    row = 4
    mlp_fwd_core(
        x_ref, (ua, ub), (da, db), (ba[row : row + 1, :], bb[row : row + 1, :]),
        act_ref, slope_ref, acc_ref,
    )


def mlp_far_body(
    x_ref, ua, ub, da, db, ba, bb, near_ref, first_ref, vec_ref, cot_ref,
    act_ref, slope_ref, out_ref, grad_ref, sums_ref, acc_ref,
):
    row = 4
    mlp_fwd_core(
        x_ref, (ua, ub), (da, db), (ba[row : row + 1, :], bb[row : row + 1, :]),
        act_ref, slope_ref, acc_ref,
    )
    rows, width = x_ref.shape
    gain1, shift1, bias = vec_ref[1:2, :], vec_ref[2:3, :], vec_ref[3:4, :]
    gain, shift = vec_ref[4:5, :], vec_ref[5:6, :]
    sums_ref[...] = jnp.zeros_like(sums_ref)
    for s in range(rows // L):
        at = slice(s * L, (s + 1) * L)
        unit1, _ = unit_of(first_ref[at, :])
        normed = unit1 * gain1 + shift1
        second = normed + acc_ref[at, :] + near_ref[at, :] + bias
        unit, rate = unit_of(second)
        out_ref[at, :] = (unit * gain + shift).astype(BF)
        grad_out = cot_ref[at, :].astype(F32)
        inner = grad_out * gain
        lower = rate * (inner - row_mean(inner) - unit * row_mean(inner * unit))
        grad_ref[at, :] = lower
        sums_ref[0:1, :] += jnp.sum(grad_out * unit, axis=0, keepdims=True)
        sums_ref[1:2, :] += jnp.sum(grad_out, axis=0, keepdims=True)
        sums_ref[2:3, :] += jnp.sum(lower, axis=0, keepdims=True)


def mlp_bwd_core(x_ref, gl, ups, downs, act_ref, slope_ref, dus, dds, bsum_ref, acc_ref):
    hid = ups[0].shape[0]
    rows = x_ref.shape[0]
    for r in (1, 0):
        lo = r * hid
        dds[r][...] = dot(act_ref[:, lo : lo + hid], gl, TN).astype(dds[r].dtype)
        gp = (dot(gl, downs[r][...], NT) * slope_ref[:, lo : lo + hid]).astype(BF)
        bsum_ref[r : r + 1, :] = jnp.sum(gp.astype(F32), axis=0, keepdims=True)
        dus[r][...] = dot(gp, x_ref[...], TN).astype(dus[r].dtype)
        part = dot(gp, ups[r][...], NN)
        if r == 1:
            acc_ref[...] = part
        else:
            acc_ref[...] += part


def mlp_bwd_far_body(
    x_ref, g_ref, ua, ub, da, db, act_ref, slope_ref,
    dua, dub, dda, ddb, bsum_ref, acc_ref,
):
    bsum_ref[...] = jnp.zeros_like(bsum_ref)
    gl = g_ref[...].astype(BF)
    mlp_bwd_core(
        x_ref, gl, (ua, ub), (da, db), act_ref, slope_ref, (dua, dub), (dda, ddb), bsum_ref, acc_ref
    )


def mlp_bwd_near_body(
    x_ref, g_ref, ua, ub, da, db, act_ref, slope_ref, far_ref, first_ref, vec_ref,
    dua, dub, dda, ddb, bsum_ref, gf_ref, sums_ref,
):
    bsum_ref[...] = jnp.zeros_like(bsum_ref)
    gl = g_ref[...].astype(BF)
    mlp_bwd_core(
        x_ref, gl, (ua, ub), (da, db), act_ref, slope_ref, (dua, dub), (dda, ddb), bsum_ref, gf_ref
    )
    rows, width = x_ref.shape
    gain = vec_ref[1:2, :]
    sums_ref[...] = jnp.zeros_like(sums_ref)
    for s in range(rows // L):
        at = slice(s * L, (s + 1) * L)
        unit, rate = unit_of(first_ref[at, :])
        upper = gf_ref[at, :] + far_ref[at, :] + g_ref[at, :]
        inner = upper * gain
        lower = rate * (inner - row_mean(inner) - unit * row_mean(inner * unit))
        gf_ref[at, :] = lower
        sums_ref[0:1, :] += jnp.sum(upper * unit, axis=0, keepdims=True)
        sums_ref[1:2, :] += jnp.sum(upper, axis=0, keepdims=True)
        sums_ref[2:3, :] += jnp.sum(lower, axis=0, keepdims=True)


def attn_bwd_core(x_ref, gl, a_ref, b_ref, qkv_ref, p_ref, mix_ref, da_ref, db_ref, bsum_ref, gm_ref, dj_ref):
    rows = x_ref.shape[0]
    seqs = rows // L
    w = a_ref.shape[1] // 4
    wide = 2 * w
    out = jnp.concatenate(pieces(a_ref, b_ref, 3 * w, 4 * w), axis=0)
    gm_ref[...] = dot(gl, out, NT).astype(BF)
    dout = dot(mix_ref[...], gl, TN)
    da_ref[3 * w : 4 * w, :] = dout[:w].astype(da_ref.dtype)
    db_ref[3 * w : 4 * w, :] = dout[w:].astype(db_ref.dtype)
    masks = head_mask(2 * HD)
    half = lax.broadcasted_iota(jnp.int32, (L, 2 * HD), 1) < HD
    pairs = wide // (2 * HD)
    scale = HD ** (-0.5)

    def one(s, carry):
        at = pl.ds(pl.multiple_of(s * L, L), L)
        for pair in range(pairs):
            lo = pair * 2 * HD
            q = qkv_ref[at, lo : lo + 2 * HD]
            k = qkv_ref[at, wide + lo : wide + lo + 2 * HD]
            v = qkv_ref[at, 2 * wide + lo : 2 * wide + lo + 2 * HD]
            go = gm_ref[at, lo : lo + 2 * HD]
            prob = p_ref[s * pairs + pair]
            dv = dot(prob.astype(BF), go, NN)
            dp = dot(doubled(v, masks), go, NT)
            lows = []
            for h in range(2):
                ph = prob[h * L : (h + 1) * L]
                dh = dp[h * L : (h + 1) * L]
                delta = jnp.sum(ph * dh, axis=0, keepdims=True)
                lows.append((ph * (dh - delta)).astype(BF))
            ds = jnp.concatenate(lows, axis=0)
            dk = dot(ds, q, NN)
            dq = dot(ds, doubled(k, masks), TN) * scale
            dj_ref[at, lo : lo + 2 * HD] = dq.astype(BF)
            dj_ref[at, wide + lo : wide + lo + 2 * HD] = (
                jnp.where(half, dk[:L], dk[L:]) * scale
            ).astype(BF)
            dj_ref[at, 2 * wide + lo : 2 * wide + lo + 2 * HD] = jnp.where(
                half, dv[:L], dv[L:]
            ).astype(BF)
        return carry

    lax.fori_loop(0, seqs, one, 0)
    dj = dj_ref[...]
    grads = dot(dj, x_ref[...], TN)
    for k in range(3):
        lo = k * wide
        da_ref[k * w : (k + 1) * w, :] = grads[lo : lo + w].astype(da_ref.dtype)
        db_ref[k * w : (k + 1) * w, :] = grads[lo + w : lo + wide].astype(db_ref.dtype)
    bsum_ref[...] = jnp.zeros_like(bsum_ref)
    bsum_ref[0:1, :] = jnp.sum(dj[:, :wide].astype(F32), axis=0, keepdims=True)
    bsum_ref[1:2, :] = jnp.sum(dj[:, 2 * wide :].astype(F32), axis=0, keepdims=True)
    return dot(dj, joined_weight(a_ref, b_ref, w), NN)


def attn_bwd_far_body(
    x_ref, g_ref, a_ref, b_ref, qkv_ref, p_ref, mix_ref,
    da_ref, db_ref, bsum_ref, acc_ref, gm_ref, dj_ref,
):
    gl = g_ref[...].astype(BF)
    acc_ref[...] = attn_bwd_core(
        x_ref, gl, a_ref, b_ref, qkv_ref, p_ref, mix_ref, da_ref, db_ref, bsum_ref, gm_ref, dj_ref
    )


def attn_bwd_near_body(
    x_ref, g_ref, a_ref, b_ref, qkv_ref, p_ref, mix_ref, far_ref,
    da_ref, db_ref, bsum_ref, gt_ref, temb_ref, gm_ref, dj_ref,
):
    gl = g_ref[...].astype(BF)
    gt_ref[...] = (
        attn_bwd_core(
            x_ref, gl, a_ref, b_ref, qkv_ref, p_ref, mix_ref, da_ref, db_ref, bsum_ref, gm_ref, dj_ref
        )
        + far_ref[...]
        + g_ref[...]
    )
    temb_ref[...] = jnp.zeros_like(temb_ref)
    for s in range(x_ref.shape[0] // L):
        temb_ref[s : s + 1, :] = jnp.sum(gt_ref[s * L : (s + 1) * L, :], axis=0, keepdims=True)


def time_features(timesteps, width):
    half = width // 2
    frequency = jnp.exp(-math.log(10000.0) * jnp.arange(half, dtype=F32) / half)
    angles = timesteps.astype(F32)[:, None] * frequency[None, :]
    return jnp.concatenate([jnp.cos(angles), jnp.sin(angles)], axis=1)


def swap(value, axis, size, bit):
    return lax.ppermute(value, axis, [(i, i ^ bit) for i in range(size)])


def halves(bit_set, mine, other):
    low = jnp.where(bit_set, other, mine)
    high = jnp.where(bit_set, mine, other)
    return low, high


def local(dp, tensor, *args):
    (
        tokens, timesteps, lengths, time_inner, time_ibias, time_outer, time_obias, qkv_weight,
        qv_bias, out_weight, out_bias, gain_first, shift_first, up_weight, up_bias, down_weight,
        down_bias, gain_second, shift_second, cotangent,
    ) = args
    rows, width = tokens.shape
    seqs = rows // L
    w = qkv_weight.shape[2]
    hid = up_weight.shape[0]
    t = lax.axis_index("tensor")
    d = lax.axis_index("dp")
    bits = [1 << i for i in range(dp.bit_length() - 1)]
    core = lambda v: swap(v, "tensor", tensor, 1)
    across = lambda v: swap(v, "tensor", tensor, 2)
    odd = (d & 1) == 1

    flat_qkv = jnp.transpose(qkv_weight, (1, 2, 0)).reshape(3 * w, width)
    pad = lambda v, lo: jnp.pad(v, (lo, width - lo - v.shape[0]))
    bias_rows = jnp.stack(
        [pad(qv_bias[0], 0), pad(qv_bias[0], w), pad(qv_bias[1], 0), pad(qv_bias[1], w), up_bias]
        + [jnp.zeros((width,), BF)] * 11
    )
    wa = jnp.concatenate([flat_qkv, out_weight, bias_rows], axis=0)
    part = 2 * w
    wa_core = core(wa)
    wa_y = across(
        jnp.concatenate(
            [jnp.where(odd, wa[part : 2 * part], wa[:part]), bias_rows], axis=0
        )
    )
    wa_x = swap(wa_y[:part], "dp", dp, 1)
    lo_part, hi_part = halves(odd, wa_y[:part], wa_x)
    wa_far = jnp.concatenate([lo_part, hi_part, wa_y[part:]], axis=0)
    wa_far2 = core(wa_far)
    up_core, down_core = core(up_weight), core(down_weight)
    ffn_y = across(jnp.where(odd, down_weight, up_weight))
    ffn_x = swap(ffn_y, "dp", dp, 1)
    up_far, down_far = halves(odd, ffn_y, ffn_x)
    up_far2, down_far2 = core(up_far), core(down_far)

    features = time_features(timesteps, time_inner.shape[0])
    touter = time_outer.astype(F32)
    tinner = time_inner.astype(F32)
    hidden_time = jax.nn.silu(exact(features, tinner, NN) + time_ibias.astype(F32))
    temb = exact(hidden_time, touter, NN) + time_obias.astype(F32)
    temb = jnp.pad(temb, ((0, 8 - seqs), (0, 0))) if seqs < 8 else temb
    own_len = lax.dynamic_slice(lengths, (t * seqs,), (seqs,))
    vecs = jnp.stack(
        [out_bias, gain_first, shift_first, down_bias, gain_second, shift_second, out_bias, out_bias]
    ).astype(F32)

    wide = 2 * w
    pairs = wide // (2 * HD)
    act_shapes = [
        sds((rows, 3 * wide), BF),
        sds((seqs * pairs, 2 * L, L), F32),
        sds((rows, wide), BF),
    ]
    full = sds((rows, width), F32)
    low_full = sds((rows, width), BF)
    attn_flops = 2 * rows * width * 4 * wide + 4 * rows * L * wide
    x, qkv_n, p_n, mix_n, acc_n = call(
        attn_near_body, [low_full] + act_shapes + [full],
        (own_len, tokens, temb, wa, wa_core), attn_flops, smem=(0,),
    )
    qkv_f, p_f, mix_f, first, normed = call(
        attn_far_body, act_shapes + [full, low_full],
        (own_len, tokens, temb, x, wa_far, wa_far2, acc_n, vecs), attn_flops, smem=(0,),
    )
    mlp_shapes = [sds((rows, 2 * hid), BF), sds((rows, 2 * hid), F32)]
    mlp_flops = 2 * rows * width * 4 * hid
    bias_of = lambda v: v[4 * w :]
    b_n, b_nc, b_f, b_fc = bias_of(wa), bias_of(wa_core), bias_of(wa_far), bias_of(wa_far2)
    act_n, slope_n, mlp_n = call(
        mlp_near_body, mlp_shapes + [full],
        (normed, up_weight, up_core, down_weight, down_core, b_n, b_nc), mlp_flops,
    )
    act_f, slope_f, layer_out, g2, sums2 = call(
        mlp_far_body, mlp_shapes + [low_full, full, sds((8, width), F32)],
        (normed, up_far, up_far2, down_far, down_far2, b_f, b_fc, mlp_n, first, vecs, cotangent),
        mlp_flops, scratch=[pltpu.VMEM((rows, width), F32)],
    )
    dw_shapes = [sds((hid, width), F32), sds((hid, width), BF)] * 2
    duf, duf2, ddf, ddf2, bup_f, gn_f = call(
        mlp_bwd_far_body, dw_shapes + [sds((8, hid), F32), full],
        (normed, g2, up_far, up_far2, down_far, down_far2, act_f, slope_f), 2 * mlp_flops,
    )
    f_far = jnp.concatenate([duf + core(duf2), ddf + core(ddf2)], axis=0).astype(BF)
    f_y = across(f_far)
    dun, dun2, ddn, ddn2, bup_n, g1, sums1 = call(
        mlp_bwd_near_body, dw_shapes + [sds((8, hid), F32), full, sds((8, width), F32)],
        (normed, g2, up_weight, up_core, down_weight, down_core, act_n, slope_n, gn_f, first, vecs),
        2 * mlp_flops,
    )
    f_own = jnp.concatenate([dun + core(dun2), ddn + core(ddn2)], axis=0) + f_y
    da_shapes = [sds((4 * w, width), F32), sds((4 * w, width), BF), sds((8, wide), F32)]
    bwd_scratch = [pltpu.VMEM((rows, wide), BF), pltpu.VMEM((rows, 3 * wide), BF)]
    daf, daf2, qvb_f, gin_f = call(
        attn_bwd_far_body, da_shapes + [full],
        (x, g1, wa_far, wa_far2, qkv_f, p_f, mix_f), 2 * attn_flops, scratch=bwd_scratch,
    )
    a_y = across((daf + core(daf2)).astype(BF))
    dan, dan2, qvb_n, grad_tokens, gtemb = call(
        attn_bwd_near_body, da_shapes + [full, sds((8, width), F32)],
        (x, g1, wa, wa_core, qkv_n, p_n, mix_n, gin_f), 2 * attn_flops, scratch=bwd_scratch,
    )
    a_own = dan + core(dan2) + a_y

    def reduce_dp(value):
        for bit in bits:
            h = value.shape[0] // 2
            up = (d & bit) != 0
            send = jnp.where(up, value[:h], value[h:]).astype(BF)
            keep = jnp.where(up, value[h:], value[:h])
            value = keep + swap(send, "dp", dp, bit).astype(F32)
        value = value.astype(BF)
        for bit in bits[::-1]:
            other = swap(value, "dp", dp, bit)
            low, high = halves((d & bit) != 0, value, other)
            value = jnp.concatenate([low, high], axis=0)
        return value.astype(F32)

    f_all = reduce_dp(f_own)
    a_all = reduce_dp(a_own)

    slot = jnp.arange(tensor, dtype=jnp.int32)
    qv_row = lambda s, at: jnp.concatenate([s[0, at * w : (at + 1) * w], s[1, at * w : (at + 1) * w]])
    rel = [
        (bup_n[0], qv_row(qvb_n, 0)), (bup_n[1], qv_row(qvb_n, 1)),
        (bup_f[0], qv_row(qvb_f, 0)), (bup_f[1], qv_row(qvb_f, 1)),
    ]
    bup_rows = 0.0
    qv_rows = 0.0
    for r, (bu, qv) in enumerate(rel):
        here = (slot == (t ^ r))[:, None]
        bup_rows = bup_rows + jnp.where(here, bu[None, :], 0.0)
        qv_rows = qv_rows + jnp.where(here, jnp.pad(qv, (0, width - 2 * w))[None, :], 0.0)
    small = jnp.concatenate([sums2[:3], sums1[:3], bup_rows, qv_rows], axis=0)
    gath = gtemb[:seqs]
    hops = [("tensor", tensor, 1), ("tensor", tensor, 2)] + [("dp", dp, bit) for bit in bits]
    for axis, size, bit in hops:
        n = small.shape[0]
        other = swap(jnp.concatenate([small, gath], axis=0), axis, size, bit)
        small = small + other[:n]
        me = t if axis == "tensor" else d
        low, high = halves((me & bit) != 0, gath, other[n:])
        gath = jnp.concatenate([low, high], axis=0)
    all_steps = lax.all_gather(timesteps, ("dp", "tensor"), axis=0, tiled=True)
    feats = time_features(all_steps, time_inner.shape[0])
    pre = exact(feats, tinner, NN) + time_ibias.astype(F32)
    act_t, silu_back = jax.vjp(jax.nn.silu, pre)
    grad_touter = exact(act_t, gath, TN)
    grad_tobias = jnp.sum(gath, axis=0)
    grad_hidden = silu_back(exact(gath, touter, NT))[0]
    grad_tinner = exact(feats, grad_hidden, TN)
    grad_tibias = jnp.sum(grad_hidden, axis=0)

    grad_qkv = jnp.transpose(a_all[: 3 * w].reshape(3, w, width), (2, 0, 1))
    own_bup = lax.dynamic_slice(small, (6 + t, 0), (1, width))[0]
    own_qv = lax.dynamic_slice(small, (6 + tensor + t, 0), (1, width))[0, : 2 * w].reshape(2, w)
    return (
        layer_out,
        grad_tokens,
        grad_tinner,
        grad_tibias,
        grad_touter,
        grad_tobias,
        grad_qkv,
        own_qv,
        a_all[3 * w :],
        small[5],
        small[3],
        small[4],
        f_all[:hid],
        own_bup,
        f_all[hid:],
        small[2],
        small[0],
        small[1],
    )


def solution(mesh):
    both = ("dp", "tensor")
    placed = (
        P(both, None), P(both), P("dp"), P(), P(), P(), P(), P(None, None, "tensor"),
        P(None, "tensor"), P("tensor", None), P(), P(), P(), P("tensor", None), P("tensor"),
        P("tensor", None), P(), P(), P(), P(both, None),
    )
    return jax.shard_map(
        functools.partial(local, mesh.shape["dp"], mesh.shape["tensor"]),
        mesh=mesh,
        in_specs=placed,
        out_specs=(
            P(both, None), P(both, None), P(), P(), P(), P(), P(None, None, "tensor"),
            P(None, "tensor"), P("tensor", None), P(), P(), P(), P("tensor", None), P("tensor"),
            P("tensor", None), P(), P(), P(),
        ),
        check_vma=False,
    )
```

```python
import functools
import math

import jax
import jax.numpy as jnp
from jax import lax
from jax.experimental import pallas as pl
from jax.experimental.pallas import tpu as pltpu
from jax.sharding import PartitionSpec as P

L = 128
HD = 64
EPS = 1e-05
F32 = jnp.float32
BF = jnp.bfloat16
NN = ((1,), (0,))
NT = ((1,), (1,))
TN = ((0,), (0,))
VMEM_LIMIT = 60 * 1024 * 1024
BIG = 64 * 1024


def dot(left, right, dims):
    return lax.dot_general(left, right, (dims, ((), ())), preferred_element_type=F32)


def exact(left, right, dims):
    return lax.dot_general(
        left, right, (dims, ((), ())), precision=lax.Precision.HIGHEST, preferred_element_type=F32
    )


class Loaded:
    def __init__(self, ref, copies=(), queue=None):
        self.ref, self.copies, self.queue = ref, list(copies), queue

    def __call__(self):
        if self.copies:
            while self.queue[0] and self not in self.queue[1]:
                advance(self.queue)
            for copy in self.copies:
                copy.wait()
            self.copies = []
            advance(self.queue)
        return self.ref


def advance(queue):
    if queue[0]:
        item = queue[0].pop(0)
        for copy in item.copies:
            copy.start()
        queue[1].append(item)


class Stored:
    def __init__(self, ref, copy=None):
        self.ref, self.copy, self.started = ref, copy, False

    def put(self):
        if self.copy is not None and not self.started:
            self.started = True
            self.copy.start()


def call(body, outs, args, flops, scratch=(), smem=(), place=None, window=4):
    place = place or {}
    size = lambda v: math.prod(v.shape) * v.dtype.itemsize
    moved = sum(size(v) for v in list(outs) + list(args))
    big_in = [i for i, v in enumerate(args) if i not in smem and size(v) >= BIG]
    held = [i for i in big_in if i not in place]
    big_out = [i for i, v in enumerate(outs) if size(v) >= BIG]
    n_in, n_out = len(args), len(outs)
    def kernel(*refs):
        ins = [Loaded(r) for r in refs[:n_in]]
        res = [Stored(r) for r in refs[n_in : n_in + n_out]]
        rest = refs[n_in + n_out :]
        held_in, rest = rest[: len(held)], rest[len(held) :]
        held_out, rest = rest[: len(big_out)], rest[len(big_out) :]
        extra, (sem_in, sem_out) = rest[:-2], rest[-2:]
        queue = ([], [])
        sem = 0
        for i in big_in:
            if i in place:
                dst, pairs = place[i](refs, extra)
            else:
                dst = held_in[held.index(i)]
                pairs = [(refs[i], dst)]
            copies = []
            for one, two in pairs:
                copies.append(pltpu.make_async_copy(one, two, sem_in.at[sem]))
                sem += 1
            ins[i] = Loaded(dst, copies, queue)
            queue[0].append(ins[i])
        for _ in range(window):
            advance(queue)
        for k, i in enumerate(big_out):
            copy = pltpu.make_async_copy(held_out[k], refs[n_in + i], sem_out.at[k])
            res[i] = Stored(held_out[k], copy)
        body(ins, res, extra)
        for item in ins:
            item()
        for item in res:
            item.put()
        for item in res:
            if item.copy is not None:
                item.copy.wait()

    def spec(i, big):
        if i in big:
            return pl.BlockSpec(memory_space=pl.ANY)
        return pl.BlockSpec(memory_space=pltpu.VMEM)

    return pl.pallas_call(
        kernel,
        out_shape=outs,
        in_specs=[
            pl.BlockSpec(memory_space=pltpu.SMEM) if i in smem else spec(i, big_in)
            for i in range(n_in)
        ],
        out_specs=[spec(i, big_out) for i in range(n_out)],
        scratch_shapes=[pltpu.VMEM(args[i].shape, args[i].dtype) for i in held]
        + [pltpu.VMEM(outs[i].shape, outs[i].dtype) for i in big_out]
        + list(scratch)
        + [pltpu.SemaphoreType.DMA((len(big_in) + 3 * len(place) + 1,)), pltpu.SemaphoreType.DMA((max(1, len(big_out)),))],
        cost_estimate=pl.CostEstimate(flops=int(flops), bytes_accessed=int(moved), transcendentals=0),
        compiler_params=pltpu.CompilerParams(vmem_limit_bytes=VMEM_LIMIT),
    )(*args)


def sds(shape, dtype):
    return jax.ShapeDtypeStruct(shape, dtype)


def head_mask(width):
    lane = lax.broadcasted_iota(jnp.int32, (1, width), 1)
    first = jnp.where(lane < width // 2, 1.0, 0.0)
    return first.astype(BF), (1.0 - first).astype(BF)


def doubled(pair, masks):
    return jnp.concatenate([pair * masks[0], pair * masks[1]], axis=0)


def far_places(j_at, first, scratch):
    def place_of(s, k):
        def pairs(refs, extra):
            dst = extra[scratch + s]
            n = dst.shape[0] // 4
            row = pl.multiple_of((refs[j_at][0] ^ k) * n, n)
            return dst, [(refs[first + 4 * s + k], dst.at[pl.ds(row, n), :])]

        return pairs

    return {first + 4 * s + k: place_of(s, k) for s in range(2) for k in range(4)}


class Whole:
    def __init__(self, parts):
        self.parts, self.ref = parts, parts[0].ref

    def __call__(self):
        for part in self.parts:
            part()
        return self.ref


class Rows:
    def __init__(self, item, lo, n):
        self.item, self.ref = item, item.ref.at[pl.ds(lo, n), :]

    def __call__(self):
        self.item()
        return self.ref


def side_by_side(a_ref, b_ref, row, w):
    a = a_ref[...].astype(F32)
    b = b_ref[...].astype(F32)
    return (a + pltpu.roll(b, w, 1))[row : row + 1, : 2 * w]


def joined(weights, w):
    return jnp.concatenate([q[k * w : (k + 1) * w, :] for k in range(3) for q in weights], axis=0)


def attn_fwd_core(x, weights, outs, biases, len_ref, qkv_ref, p_ref, mix_ref, stored):
    w = outs[0].ref.shape[0]
    rows = x.shape[0]
    seqs = rows // L
    wide = 2 * w
    total = dot(x, joined([q() for q in weights], w), NT)
    qkv_ref[:, :wide] = (total[:, :wide] + side_by_side(*biases, 0, w)).astype(BF)
    qkv_ref[:, wide : 2 * wide] = total[:, wide : 2 * wide].astype(BF)
    qkv_ref[:, 2 * wide :] = (total[:, 2 * wide :] + side_by_side(*biases, 1, w)).astype(BF)
    masks = head_mask(2 * HD)
    key_at = lax.broadcasted_iota(jnp.int32, (L, L), 0)
    pairs = wide // (2 * HD)

    def one(s, carry):
        at = pl.ds(pl.multiple_of(s * L, L), L)
        valid = key_at < len_ref[s]
        for pair in range(pairs):
            lo = pair * 2 * HD
            q = qkv_ref[at, lo : lo + 2 * HD]
            k = qkv_ref[at, wide + lo : wide + lo + 2 * HD]
            v = qkv_ref[at, 2 * wide + lo : 2 * wide + lo + 2 * HD]
            scores = dot(doubled(k, masks), q, NT) * HD ** (-0.5)
            lows = []
            for h in range(2):
                part = jnp.where(valid, scores[h * L : (h + 1) * L], -1e30)
                expo = jnp.exp(part - jnp.max(part, axis=0, keepdims=True))
                prob = expo * (1.0 / jnp.sum(expo, axis=0, keepdims=True))
                p_ref[s * pairs + pair, h * L : (h + 1) * L, :] = prob
                lows.append(prob.astype(BF))
            mixed = dot(jnp.concatenate(lows, axis=0), doubled(v, masks), TN)
            mix_ref[at, lo : lo + 2 * HD] = mixed.astype(BF)
        return carry

    lax.fori_loop(0, seqs, one, 0)
    stored()
    return dot(mix_ref[...], jnp.concatenate([o()[...] for o in outs], axis=0), NN)


def start_of(tok_ref, temb_ref):
    rows, width = tok_ref.shape
    seqs = rows // L
    return [
        tok_ref[s * L : (s + 1) * L, :].astype(F32) + temb_ref[s : s + 1, :] for s in range(seqs)
    ]


def attn_near_body(ins, res, extra):
    len_r, tok, temb, qa, qb, ba, bb, oa, ob = ins
    x, qkv, p, mix, acc = res
    for s, rows in enumerate(start_of(tok(), temb())):
        x.ref[s * L : (s + 1) * L, :] = rows.astype(BF)
    acc.ref[...] = attn_fwd_core(
        x.ref[...], (qa, qb), (oa, ob), (ba(), bb()), len_r(), qkv.ref, p.ref, mix.ref,
        lambda: [r.put() for r in (qkv, p, mix)],
    )


def far_weights(pieces):
    both = (Whole(pieces[:4]), Whole(pieces[4:]))
    w = both[0].ref.shape[0] // 4
    return both, tuple(Rows(f, 3 * w, w) for f in both)


def row_mean(value):
    return jnp.mean(value, axis=-1, keepdims=True)


def unit_of(value):
    centred = value - row_mean(value)
    rate = lax.rsqrt(row_mean(centred * centred) + EPS)
    return centred * rate, rate


def attn_far_body(ins, res, extra):
    len_r, j, x, *pieces, ba, bb, near, tok, temb, ob_v, g_v, s_v = ins
    qkv, p, mix, first_o, low = res
    weights, outs = far_weights(pieces)
    acc = attn_fwd_core(
        x()[...], weights, outs, (ba(), bb()), len_r(), qkv.ref, p.ref, mix.ref,
        lambda: [r.put() for r in (qkv, p, mix)],
    )
    out_bias, gain, shift = (vector(v) for v in (ob_v, g_v, s_v))
    first_ref = first_o.ref
    first_ref[...] = acc + near()[...] + out_bias
    for s, rows in enumerate(start_of(tok(), temb())):
        at = slice(s * L, (s + 1) * L)
        first = first_ref[at, :] + rows
        first_ref[at, :] = first
        unit, _ = unit_of(first)
        low.ref[at, :] = (unit * gain + shift).astype(BF)


def vector(item):
    return item()[...].astype(F32).reshape(1, -1)


def gelu_pair(pre):
    cdf = 0.5 * (1.0 + lax.erf(pre * 0.7071067811865476))
    pdf = jnp.exp(-0.5 * pre * pre) * 0.3989422804014327
    return pre * cdf, cdf + pre * pdf


def mlp_fwd_core(x_ref, ups, downs, biases, act_ref, slope_ref, acc_ref, done):
    rows = x_ref.shape[0]
    hid = ups[0].ref.shape[0]
    tile = 384 if hid % 384 == 0 else hid
    block = 256 if rows % 256 == 0 else rows
    first = True
    for r in range(len(ups)):
        for t in range(hid // tile):
            up = ups[r]()[t * tile : (t + 1) * tile, :]
            down = downs[r]()[t * tile : (t + 1) * tile, :]
            bias = biases[r][:, t * tile : (t + 1) * tile].astype(F32)
            for m in range(rows // block):
                at = slice(m * block, (m + 1) * block)
                act, slope = gelu_pair(dot(x_ref[at, :], up, NT) + bias)
                low = act.astype(BF)
                cols = slice(t * tile, (t + 1) * tile)
                act_ref[r][at, cols] = low
                slope_ref[r][at, cols] = slope
                part = dot(low, down, NN)
                if first:
                    acc_ref[at, :] = part
                else:
                    acc_ref[at, :] += part
            first = False
        done(r)


def mlp_near_body(ins, res, extra):
    x, ua, ub, da, db, ba, bb = ins
    act_a, act_b, slope_a, slope_b, acc = res

    def done(r):
        (act_a, act_b)[r].put()
        (slope_a, slope_b)[r].put()

    mlp_fwd_core(
        x(), (ua, ub), (da, db), (ba()[2:3, :], bb()[2:3, :]), (act_a.ref, act_b.ref),
        (slope_a.ref, slope_b.ref), acc.ref, done,
    )


def mlp_far_body(ins, res, extra):
    j, x, *pieces, ba, bb, near, first, cot, g1_v, s1_v, b_v, g2_v, s2_v = ins
    fa, fb = Whole(pieces[:4]), Whole(pieces[4:])
    dub, ddb, dua, dda, bsb, bsa, out, grad, sums, gn = res
    _, _, act_a, act_b, slope_a, slope_b, acc_ref = extra
    hid = fa.ref.shape[0] // 2
    ups = tuple(Rows(f, 0, hid) for f in (fa, fb))
    downs = tuple(Rows(f, hid, hid) for f in (fa, fb))
    mlp_fwd_core(
        x(), ups, downs, (ba()[2:3, :], bb()[2:3, :]), (act_a, act_b), (slope_a, slope_b), acc_ref,
        lambda r: None,
    )
    rows, width = x().shape
    first_ref, near_ref, cot_ref, sums_ref = first(), near(), cot(), sums.ref
    gain1, shift1, bias, gain, shift = [vector(v) for v in (g1_v, s1_v, b_v, g2_v, s2_v)]
    sums_ref[...] = jnp.zeros_like(sums_ref)
    for s in range(rows // L):
        at = slice(s * L, (s + 1) * L)
        unit1, _ = unit_of(first_ref[at, :])
        normed = unit1 * gain1 + shift1
        second = normed + acc_ref[at, :] + near_ref[at, :] + bias
        unit, rate = unit_of(second)
        out.ref[at, :] = (unit * gain + shift).astype(BF)
        grad_out = cot_ref[at, :].astype(F32)
        inner = grad_out * gain
        lower = rate * (inner - row_mean(inner) - unit * row_mean(inner * unit))
        grad.ref[at, :] = lower
        sums_ref[0:1, :] += jnp.sum(grad_out * unit, axis=0, keepdims=True)
        sums_ref[1:2, :] += jnp.sum(grad_out, axis=0, keepdims=True)
        sums_ref[2:3, :] += jnp.sum(lower, axis=0, keepdims=True)
    out.put()
    gl = grad.ref[...].astype(BF)
    held = [Loaded(r) for r in (act_a, act_b, slope_a, slope_b)]
    gn.ref[...] = mlp_bwd_slice(x, gl, ups[1], downs[1], held[1], held[3], dub, ddb, bsb)
    gn.ref[...] += mlp_bwd_slice(x, gl, ups[0], downs[0], held[0], held[2], dua, dda, bsa)


def mlp_bwd_slice(x, gl, up, down, act, slope, du, dd, bsum):
    dd.ref[...] = dot(act()[...], gl, TN).astype(dd.ref.dtype)
    dd.put()
    gp = (dot(gl, down()[...], NT) * slope()[...]).astype(BF)
    bsum.ref[...] = jnp.sum(gp.astype(F32), axis=0, keepdims=True)
    du.ref[...] = dot(gp, x()[...], TN).astype(du.ref.dtype)
    du.put()
    return dot(gp, up()[...], NN)


def mlp_bwd_near_body(ins, res, extra):
    g, act_b, db, slope_b, x, ub, act_a, da, slope_a, ua, far, first, g_v = ins
    dub, ddb, dua, dda, bsb, bsa, gf, sums = res
    gl = g()[...].astype(BF)
    gf_ref, sums_ref = gf.ref, sums.ref
    gf_ref[...] = mlp_bwd_slice(x, gl, ub, db, act_b, slope_b, dub, ddb, bsb)
    gf_ref[...] += mlp_bwd_slice(x, gl, ua, da, act_a, slope_a, dua, dda, bsa)
    rows = x().shape[0]
    far_ref, first_ref, g_ref = far(), first(), g()
    gain = vector(g_v)
    sums_ref[...] = jnp.zeros_like(sums_ref)
    for s in range(rows // L):
        at = slice(s * L, (s + 1) * L)
        unit, rate = unit_of(first_ref[at, :])
        upper = gf_ref[at, :] + far_ref[at, :] + g_ref[at, :]
        inner = upper * gain
        lower = rate * (inner - row_mean(inner) - unit * row_mean(inner * unit))
        gf_ref[at, :] = lower
        sums_ref[0:1, :] += jnp.sum(upper * unit, axis=0, keepdims=True)
        sums_ref[1:2, :] += jnp.sum(upper, axis=0, keepdims=True)
        sums_ref[2:3, :] += jnp.sum(lower, axis=0, keepdims=True)


def attn_bwd_core(x, gl, weights, outs, qkv, p, mix, da, db, bsum_ref, gm_ref, dj_ref):
    rows = gl.shape[0]
    seqs = rows // L
    w = outs[0].ref.shape[0]
    wide = 2 * w
    gm_ref[...] = dot(gl, jnp.concatenate([o()[...] for o in outs], axis=0), NT).astype(BF)
    dout = dot(mix()[...], gl, TN)
    da.ref[3 * w : 4 * w, :] = dout[:w].astype(da.ref.dtype)
    db.ref[3 * w : 4 * w, :] = dout[w:].astype(db.ref.dtype)
    masks = head_mask(2 * HD)
    half = lax.broadcasted_iota(jnp.int32, (L, 2 * HD), 1) < HD
    pairs = wide // (2 * HD)
    scale = HD ** (-0.5)
    qkv_ref, p_ref = qkv(), p()

    def one(s, carry):
        at = pl.ds(pl.multiple_of(s * L, L), L)
        for pair in range(pairs):
            lo = pair * 2 * HD
            q = qkv_ref[at, lo : lo + 2 * HD]
            k = qkv_ref[at, wide + lo : wide + lo + 2 * HD]
            v = qkv_ref[at, 2 * wide + lo : 2 * wide + lo + 2 * HD]
            go = gm_ref[at, lo : lo + 2 * HD]
            prob = p_ref[s * pairs + pair]
            dv = dot(prob.astype(BF), go, NN)
            dp = dot(doubled(v, masks), go, NT)
            lows = []
            for h in range(2):
                ph = prob[h * L : (h + 1) * L]
                dh = dp[h * L : (h + 1) * L]
                delta = jnp.sum(ph * dh, axis=0, keepdims=True)
                lows.append((ph * (dh - delta)).astype(BF))
            ds = jnp.concatenate(lows, axis=0)
            dk = dot(ds, q, NN)
            dq = dot(ds, doubled(k, masks), TN) * scale
            dj_ref[at, lo : lo + 2 * HD] = dq.astype(BF)
            dj_ref[at, wide + lo : wide + lo + 2 * HD] = (
                jnp.where(half, dk[:L], dk[L:]) * scale
            ).astype(BF)
            dj_ref[at, 2 * wide + lo : 2 * wide + lo + 2 * HD] = jnp.where(
                half, dv[:L], dv[L:]
            ).astype(BF)
        return carry

    lax.fori_loop(0, seqs, one, 0)
    dj = dj_ref[...]
    grads = dot(dj, x()[...], TN)
    for k in range(3):
        lo = k * wide
        da.ref[k * w : (k + 1) * w, :] = grads[lo : lo + w].astype(da.ref.dtype)
        db.ref[k * w : (k + 1) * w, :] = grads[lo + w : lo + wide].astype(db.ref.dtype)
    db.put()
    da.put()
    bsum_ref[...] = jnp.zeros_like(bsum_ref)
    bsum_ref[0:1, :] = jnp.sum(dj[:, :wide].astype(F32), axis=0, keepdims=True)
    bsum_ref[1:2, :] = jnp.sum(dj[:, 2 * wide :].astype(F32), axis=0, keepdims=True)
    return dot(dj, joined([q() for q in weights], w), NN)


def attn_bwd_far_body(ins, res, extra):
    j, g, *pieces, mix, qkv, p, x = ins
    db, da, bsum, acc = res
    _, _, gm_ref, dj_ref = extra
    weights, outs = far_weights(pieces)
    gl = g()[...].astype(BF)
    acc.ref[...] = attn_bwd_core(
        x, gl, weights, outs, qkv, p, mix, da, db, bsum.ref, gm_ref, dj_ref
    )


def attn_bwd_near_body(ins, res, extra):
    t, g, oa, ob, mix, qkv, p, x, qa, qb, far, sums2, sums1, b0, b1, b2, b3, far_bsum, steps = ins
    db, da, gt, pack = res
    gm_ref, dj_ref, bsum_ref = extra
    bsum = Loaded(bsum_ref)
    gl = g()[...].astype(BF)
    gt.ref[...] = (
        attn_bwd_core(
            x, gl, (qa, qb), (oa, ob), qkv, p, mix, da, db, bsum.ref, gm_ref, dj_ref
        )
        + far()[...]
        + g()[...]
    )
    gt.put()
    pack_ref = pack.ref
    pack_ref[...] = jnp.zeros_like(pack_ref)
    pack_ref[0:3, :] = sums2()[0:3, :]
    pack_ref[3:6, :] = sums1()[0:3, :]
    wide = far_bsum.ref.shape[1]
    for r, bias in enumerate((b0, b1, b2, b3)):
        at = t()[0] ^ r
        pack_ref[pl.ds(8 + at, 1), :] = bias()[...]
        sums = (bsum_ref if r < 2 else far_bsum())[...]
        if r % 2:
            sums = pltpu.roll(sums, wide - wide // 2, 1)
        for k in range(2):
            pack_ref[pl.ds(12 + 4 * k + at, 1), :wide] = sums[k : k + 1, :]
    for s in range(gl.shape[0] // L):
        pack_ref[24 + s : 25 + s, :] = jnp.sum(gt.ref[s * L : (s + 1) * L, :], axis=0, keepdims=True)
    pack_ref[31:32, :] = steps()[...]


def halves_at(bit, n):
    keep = pl.multiple_of(bit * n, n)
    send = pl.multiple_of((1 - bit) * n, n)
    return pl.ds(keep, n), pl.ds(send, n)


def cut(refs, bit, keep, send, scale=1):
    n = keep.ref.shape[0]
    for at, out in zip(halves_at(bit, n), (keep, send)):
        total = refs[0][at, :].astype(F32)
        for ref in refs[1:]:
            total = total + ref[at, :].astype(F32)
        out.ref[...] = total.astype(out.ref.dtype)


def pair_sum(one, two, at, out):
    out.ref[...] = (one[at, :].astype(F32) + two[at, :].astype(F32)).astype(out.ref.dtype)


def glue_first_body(ins, res, extra):
    bits, dd, dd2, du, du2 = ins
    d_keep, d_send, u_keep, u_send = res
    cut((dd(), dd2()), bits()[0], d_keep, d_send)
    d_send.put()
    cut((du(), du2()), bits()[1], u_keep, u_send)


def glue_second_body(ins, res, extra):
    bits, dn, dn2, un, un2, df, df_x, uf, uf_z = ins
    dn_keep, un_keep, df_keep, uf_keep, x_send, z_send = res
    n = dn_keep.ref.shape[0]
    first = lambda out: Stored(out.ref.at[pl.ds(0, n), :])
    rest = lambda out: Stored(out.ref.at[pl.ds(n, n // 2), :])
    cut((dn(), dn2()), bits()[0], dn_keep, first(x_send))
    cut((un(), un2()), bits()[1], un_keep, first(z_send))
    cut((df(), df_x()), bits()[1], df_keep, rest(z_send))
    cut((uf(), uf_z()), bits()[0], uf_keep, rest(x_send))


def glue_third_body(ins, res, extra):
    bits, da, da2, dn, un, df, uf, x_got, z_got = ins
    a_lo, a_hi, dn_keep, dn_send, un_keep, un_send, df_keep, uf_keep, f_send = res
    n = a_lo.ref.shape[0]
    pair_sum(da(), da2(), slice(0, n), a_lo)
    a_lo.put()
    pair_sum(da(), da2(), slice(n, 2 * n), a_hi)
    a_hi.put()
    n = dn.ref.shape[0]
    first = lambda item: item().at[pl.ds(0, n), :]
    rest = lambda item: item().at[pl.ds(n, n // 2), :]
    cut((dn(), first(x_got)), bits()[1], dn_keep, dn_send)
    cut((un(), first(z_got)), bits()[0], un_keep, un_send)
    k = df_keep.ref.shape[0]
    part = lambda i: Stored(f_send.ref.at[pl.ds(i * k, k), :])
    cut((df(), rest(z_got)), bits()[2], df_keep, part(0))
    cut((uf(), rest(x_got)), bits()[2], uf_keep, part(1))


def glue_fourth_body(ins, res, extra):
    bits, dn, dn_z, un, un_x, df, uf, f_got = ins
    keep, send, f_sum = res
    n = df.ref.shape[0]
    part = lambda out, i: Stored(out.ref.at[pl.ds(i * n, n), :])
    cut((dn(), dn_z()), bits()[2], part(keep, 0), part(send, 0))
    cut((un(), un_x()), bits()[2], part(keep, 1), part(send, 1))
    got = f_got()
    for i, item in enumerate((df, uf)):
        rows = slice(i * n, (i + 1) * n)
        f_sum.ref[rows, :] = (item()[...] + got[rows, :].astype(F32)).astype(f_sum.ref.dtype)


def quarter_of(bits, m):
    return (bits[0] ^ (m & 1)) * 2 + (bits[1] ^ (m >> 1))


def glue_fifth_body(ins, res, extra):
    bits, da, da2, lo, hi = ins
    n = res[0].ref.shape[0]
    a, b, lo_ref, hi_ref = da(), da2(), lo(), hi()
    for m in (1, 2, 3, 0):
        out = res[m]
        at = quarter_of(bits(), m)
        rows = pl.ds(pl.multiple_of(at * n, n), n)
        part = pl.ds(pl.multiple_of((at & 1) * n, n), n)
        total = a[rows, :] + b[rows, :].astype(F32)

        @pl.when(at < 2)
        def _():
            out.ref[...] = (total + lo_ref[part, :].astype(F32)).astype(out.ref.dtype)

        @pl.when(at >= 2)
        def _():
            out.ref[...] = (total + hi_ref[part, :].astype(F32)).astype(out.ref.dtype)

        out.put()


def join_body(ins, res, extra):
    bits, d_own, d_x, u_own, u_z, *quarters = ins
    d_out, u_out, q_out, o_out = res
    n = d_own.ref.shape[0]
    for own, other, out, bit in ((d_own, d_x, d_out, 0), (u_own, u_z, u_out, 1)):
        for item, at in zip((own, other), halves_at(bits()[bit], n)):
            out.ref[at, :] = item()[...].astype(F32)
        out.put()
    n = quarters[0].ref.shape[0]
    for m, item in enumerate(quarters):
        at = quarter_of(bits(), m)
        value = item()[...].astype(F32)

        @pl.when(at < 3)
        def _():
            q_out.ref[pl.ds(pl.multiple_of(at * n, n), n), :] = value

        @pl.when(at == 3)
        def _():
            o_out.ref[...] = value


def last_body(ins, res, extra):
    t, feats, inner, ibias, outer, grad, small = ins
    g_inner, g_ibias, g_outer, g_obias, *vectors, own_bup, own_q, own_v = res
    outer_w = outer()[...].astype(F32)
    pre = exact(feats()[...], inner()[...].astype(F32), NN) + vector(ibias)
    gate = 1.0 / (1.0 + jnp.exp(-pre))
    g = grad()[...]
    g_outer.ref[...] = exact(pre * gate, g, TN)
    g_outer.put()
    g_obias.ref[...] = jnp.sum(g, axis=0)
    hidden = exact(g, outer_w, NT) * (gate * (1.0 + pre * (1.0 - gate)))
    g_inner.ref[...] = exact(feats()[...], hidden, TN)
    g_ibias.ref[...] = jnp.sum(hidden, axis=0)
    small_ref = small()
    for i, out in enumerate(vectors):
        out.ref[...] = small_ref[i, :]
    own_bup.ref[...] = small_ref[pl.ds(8 + t()[0], 1), :].reshape(own_bup.ref.shape)
    for k, out in enumerate((own_q, own_v)):
        out.ref[...] = small_ref[pl.ds(12 + 4 * k + t()[0], 1), :]


def time_features(timesteps, width):
    half = width // 2
    frequency = jnp.exp(-math.log(10000.0) * jnp.arange(half, dtype=F32) / half)
    angles = timesteps.astype(F32)[:, None] * frequency[None, :]
    return jnp.concatenate([jnp.cos(angles), jnp.sin(angles)], axis=1)


def swap(value, axis, size, bit):
    return lax.ppermute(value, axis, [(i, i ^ bit) for i in range(size)])


def tie(value, *others):
    return lax.optimization_barrier((value,) + others)[0]


def halves(bit_set, mine, other):
    low = jnp.where(bit_set, other, mine)
    high = jnp.where(bit_set, mine, other)
    return low, high


def tie(value, *others):
    return lax.optimization_barrier((value,) + others)[0]


def sync(*values):
    return lax.optimization_barrier(values)


def local(dp, tensor, *args):
    (
        tokens, timesteps, lengths, time_inner, time_ibias, time_outer, time_obias, qkv_weight,
        qv_bias, out_weight, out_bias, gain_first, shift_first, up_weight, up_bias, down_weight,
        down_bias, gain_second, shift_second, cotangent,
    ) = args
    rows, width = tokens.shape
    seqs = rows // L
    w = qkv_weight.shape[2]
    hid = up_weight.shape[0]
    t = lax.axis_index("tensor")
    d = lax.axis_index("dp")
    high = list(range(3, dp.bit_length() - 1))
    core = lambda v: swap(v, "tensor", tensor, 1)
    across = lambda v: swap(v, "tensor", tensor, 2)

    j0 = (d & 1) == 1
    j1 = ((d >> 1) & 1) == 1
    own_j = (d & 3)[None]
    own_bits = jnp.stack([d & 1, (d >> 1) & 1, (d >> 2) & 1])
    flat_qkv = jnp.transpose(qkv_weight, (1, 2, 0)).reshape(3 * w, width)
    part_a = [flat_qkv[:w], flat_qkv[w : 2 * w], flat_qkv[2 * w :], out_weight]
    h2 = hid // 2
    part_f = [up_weight[:h2], up_weight[h2:], down_weight[:h2], down_weight[h2:]]

    def pick(parts, j0, j1):
        return jnp.where(j1, jnp.where(j0, parts[3], parts[2]), jnp.where(j0, parts[1], parts[0]))

    def spread(got):
        return [swap(got, "dp", dp, m) for m in (1, 2)]

    a_y = across(pick(part_a, j0, j1))
    qkv_core, out_core = core(flat_qkv), core(out_weight)
    bias = jnp.concatenate(
        [
            jnp.pad(qv_bias, ((0, 0), (0, width - w))),
            jnp.pad(up_bias[None], ((0, 13), (0, 0))),
        ],
        axis=0,
    )
    bias_core, bias_y = core(bias), across(bias)

    features = time_features(timesteps, time_inner.shape[0])
    hidden_time = jax.nn.silu(
        exact(features, time_inner.astype(F32), NN) + time_ibias.astype(F32)
    )
    temb = exact(hidden_time, time_outer.astype(F32), NN) + time_obias.astype(F32)
    temb = jnp.pad(temb, ((0, 8 - seqs), (0, 0))) if seqs < 8 else temb
    own_len = lax.dynamic_slice(lengths, (t * seqs,), (seqs,))

    send_a, send_f, a_y, temb = sync(
        pick(part_a, ~j0, ~j1), pick(part_f, j0, j1), a_y, temb
    )
    a_others = spread(a_y)
    a_others.append(across(send_a))
    f_y = across(send_f)
    wide = 2 * w
    pairs = wide // (2 * HD)
    act_shapes = [
        sds((rows, 3 * wide), BF),
        sds((seqs * pairs, 2 * L, L), F32),
        sds((rows, wide), BF),
    ]
    full = sds((rows, width), F32)
    low_full = sds((rows, width), BF)
    attn_flops = 2 * rows * width * 4 * wide + 4 * rows * L * wide
    x, qkv_n, p_n, mix_n, acc_n = call(
        attn_near_body, [low_full] + act_shapes + [full],
        (own_len, tokens, temb, flat_qkv, qkv_core, bias, bias_core, out_weight, out_core),
        attn_flops, smem=(0,),
    )
    acc_n, bias_y, f_y, *far_a1 = sync(acc_n, bias_y, f_y, a_y, *a_others)
    far_a2 = [core(v) for v in far_a1]
    bias_y2 = core(bias_y)
    f_others = spread(f_y)
    f_others.append(across(tie(pick(part_f, ~j0, ~j1), f_y)))
    up_core, down_core = core(up_weight), core(down_weight)
    wt = pltpu.VMEM((4 * w, width), BF)
    qkv_f, p_f, mix_f, first, normed = call(
        attn_far_body, act_shapes + [full, low_full],
        (
            own_len, own_j, x, *far_a1, *far_a2, bias_y, bias_y2, acc_n,
            tokens, temb, out_bias, gain_first, shift_first,
        ),
        attn_flops, smem=(0, 1), scratch=[wt, wt], place=far_places(1, 3, 0),
    )
    normed, up_core, down_core, *far_f1 = sync(normed, up_core, down_core, f_y, *f_others)
    far_f2 = [core(v) for v in far_f1]
    up_core, down_core = up_core, down_core
    mlp_flops = 2 * rows * width * 4 * hid
    act_na, act_nb, slope_na, slope_nb, mlp_n = call(
        mlp_near_body,
        [sds((rows, hid), BF)] * 2 + [sds((rows, hid), F32)] * 2 + [full],
        (normed, up_weight, up_core, down_weight, down_core, bias, bias_core), mlp_flops,
    )
    mlp_n, *far_f2 = sync(mlp_n, *far_f2)
    mat = pltpu.VMEM((2 * hid, width), BF)
    dw_far = sds((hid, width), BF)
    dw_own = sds((hid, width), F32)
    bsum = sds((1, hid), F32)
    dws = [dw_far, dw_far, dw_own, dw_own, bsum, bsum]
    sums_shape = sds((8, width), F32)
    duf2, ddf2, duf, ddf, bup_f2, bup_f, layer_out, g2, sums2, gn_f = call(
        mlp_far_body, dws + [low_full, full, sums_shape, full],
        (
            own_j, normed, *far_f1, *far_f2, bias_y, bias_y2, mlp_n,
            first, cotangent, gain_first, shift_first, down_bias, gain_second, shift_second,
        ),
        3 * mlp_flops, smem=(0,),
        scratch=[
            mat, mat, pltpu.VMEM((rows, hid), BF), pltpu.VMEM((rows, hid), BF),
            pltpu.VMEM((rows, hid), F32), pltpu.VMEM((rows, hid), F32),
            pltpu.VMEM((rows, width), F32),
        ],
        place=far_places(0, 2, 0),
    )
    f32 = lambda v: v.astype(F32)

    part = lambda k, dtype: sds((hid // k, width), dtype)

    def glue(body, outs, args):
        return call(body, outs, (own_bits,) + args, 1, smem=(0,), window=16)

    df_keep, df_send, uf_keep, uf_send = glue(
        glue_first_body, [part(2, F32), part(2, BF), part(2, F32), part(2, BF)],
        (ddf, core(ddf2), duf, core(duf2)),
    )
    g2n, df_keep, df_send, uf_keep, uf_send = sync(g2, df_keep, df_send, uf_keep, uf_send)
    along = lambda v, m: swap(v, "dp", dp, m)
    df_x = along(df_send, 1)
    uf_z = along(uf_send, 2)
    dun2, ddn2, dun, ddn, bup_n2, bup_n, g1, sums1 = call(
        mlp_bwd_near_body, dws + [full, sums_shape],
        (
            g2n, act_nb, down_core, slope_nb, normed, up_core, act_na, down_weight, slope_na,
            up_weight, gn_f, first, gain_first,
        ),
        2 * mlp_flops,
    )
    dun2, ddn2, g1, df_x, uf_z = sync(dun2, ddn2, g1, df_x, uf_z)
    both = sds((hid // 2 + hid // 4, width), BF)
    dn_keep, un_keep, df_keep, uf_keep, x_send, z_send = glue(
        glue_second_body, [part(2, F32), part(2, F32), part(4, F32), part(4, F32), both, both],
        (ddn, core(ddn2), dun, core(dun2), df_keep, df_x, uf_keep, uf_z),
    )
    g1, dn_keep, un_keep, df_keep, uf_keep, x_send, z_send = sync(
        g1, dn_keep, un_keep, df_keep, uf_keep, x_send, z_send
    )
    x_got = along(x_send, 1)
    z_got = along(z_send, 2)
    da_shapes = [sds((4 * w, width), BF), sds((4 * w, width), F32), sds((8, wide), F32)]
    bwd_scratch = [pltpu.VMEM((rows, wide), BF), pltpu.VMEM((rows, 3 * wide), BF)]
    daf2, daf, qvb_f, gin_f = call(
        attn_bwd_far_body, da_shapes + [full],
        (own_j, g1, *far_a1, *far_a2, mix_f, qkv_f, p_f, x), 2 * attn_flops,
        smem=(0,), scratch=[wt, wt] + bwd_scratch, place=far_places(0, 2, 0),
    )
    daf2, gin_f, x_got, z_got = sync(daf2, gin_f, x_got, z_got)
    qpart = lambda k, dtype: sds((4 * w // k, width), dtype)
    a_lo, a_hi, dn_keep, dn_send, un_keep, un_send, df_keep, uf_keep, f_send = glue(
        glue_third_body,
        [
            qpart(2, BF), qpart(2, BF), part(4, F32), part(4, BF), part(4, F32), part(4, BF),
            part(8, F32), part(8, F32), part(4, BF),
        ],
        (daf, core(daf2), dn_keep, un_keep, df_keep, uf_keep, x_got, z_got),
    )
    g1, a_lo, a_hi, dn_keep, dn_send, un_keep, un_send, df_keep, uf_keep, f_send = sync(
        g1, a_lo, a_hi, dn_keep, dn_send, un_keep, un_send, df_keep, uf_keep, f_send
    )
    a_lo = across(a_lo)
    dn_z = along(dn_send, 2)
    un_x = along(un_send, 1)
    f_got = along(f_send, 4)
    steps_row = jnp.pad(timesteps.astype(F32), (0, width - seqs))[None, :]
    dan2, dan, grad_tokens, pack = call(
        attn_bwd_near_body, da_shapes[:2] + [full, sds((32, width), F32)],
        (
            t[None], g1, out_weight, out_core, mix_n, qkv_n, p_n, x, flat_qkv, qkv_core, gin_f,
            sums2, sums1, bup_n, bup_n2, bup_f, bup_f2, qvb_f, steps_row,
        ),
        2 * attn_flops, smem=(0,), scratch=bwd_scratch + [pltpu.VMEM((8, wide), F32)],
    )
    dan2, pack, a_hi, a_lo, dn_z, un_x, f_got = sync(dan2, pack, a_hi, a_lo, dn_z, un_x, f_got)

    cat = lambda *v: jnp.concatenate(v, axis=0)
    near_a2, pack_c = core(dan2), core(pack)
    a_hi = across(a_hi)
    du_keep, du_send, f_sum = glue(
        glue_fourth_body, [part(4, F32), part(4, BF), part(4, BF if not high else F32)],
        (dn_keep, dn_z, un_keep, un_x, df_keep, uf_keep, f_got),
    )

    def halve(value, which):
        n = value.shape[0] // 2
        at = jnp.where(((d >> which) & 1) == 1, n, 0)
        keep = lax.dynamic_slice_in_dim(value, at, n, 0)
        return keep, lax.dynamic_slice_in_dim(value, n - at, n, 0).astype(BF)

    def high_sum(value):
        for which in high:
            keep, send = halve(value, which)
            value = keep + f32(along(send, 1 << which))
        return value

    def join_bit(value, which, other=None):
        other = along(value, 1 << which) if other is None else other
        return cat(*halves(((d >> which) & 1) == 1, value, other))

    def high_join(value):
        for which in high[::-1]:
            value = join_bit(value, which)
        return value

    two = lambda f, v: cat(f(v[: v.shape[0] // 2]), f(v[v.shape[0] // 2 :]))
    du_z = along(du_send, 4)
    du_y = across(two(high_sum, f_sum).astype(BF) if high else f_sum)
    near_a2, pack_c, a_hi, du_z, du_y = sync(near_a2, pack_c, a_hi, du_z, du_y)

    du = two(high_sum, du_keep + f32(du_z)) + f32(du_y)
    du = two(high_join, du.astype(BF))
    small = pack[:24] + pack_c[:24]
    gath = cat(*halves((t & 1) == 1, pack[24:], pack_c[24:]))
    got_y = across(cat(small, gath))
    du_z = along(du, 4)
    quarters = glue(
        glue_fifth_body, [qpart(4, F32)] + [qpart(4, BF)] * 3, (dan, near_a2, a_lo, a_hi)
    )
    got = [along(quarters[m], m) for m in (1, 2, 3)]
    got_y, du, du_z, *got = sync(got_y, du, du_z, *got)

    state = [small + got_y[:24], cat(*halves((t & 2) == 2, gath, got_y[24:]))]

    def small_hop(which):
        small, gath = state
        other = along(cat(small, gath), 1 << which)
        state[:] = [small + other[:24], join_bit(gath, which, other[24:])]

    a_keep, a_send = halve(quarters[0] + sum(f32(v) for v in got), 2)
    a_z = along(a_send, 4)
    n = du.shape[0] // 2
    d_own, u_own = join_bit(du[:n], 2, du_z[:n]), join_bit(du[n:], 2, du_z[n:])
    d_z, u_x = along(d_own, 2), along(u_own, 1)
    small_hop(0)
    a_keep, a_z, d_own, u_own, d_z, u_x, *state[:] = sync(
        a_keep, a_z, d_own, u_own, d_z, u_x, *state
    )
    a_end = high_join(high_sum(a_keep + f32(a_z)).astype(BF))
    a_z = along(a_end, 4)
    d_own, u_own = join_bit(d_own, 1, d_z), join_bit(u_own, 0, u_x)
    d_x, u_z = along(d_own, 1), along(u_own, 2)
    small_hop(1)
    a_end, a_z, d_own, u_own, d_x, u_z, *state[:] = sync(
        a_end, a_z, d_own, u_own, d_x, u_z, *state
    )
    a_end = join_bit(a_end, 2, a_z)
    a_got = [along(a_end, m) for m in (1, 2, 3)]
    small_hop(2)
    for which in high:
        small_hop(which)

    small, gath = state
    gath = gath.reshape(dp, tensor, 8, width)
    feats = time_features(gath[:, :, 7, :seqs].reshape(-1), time_inner.shape[0])
    line = sds((width,), F32)
    row = sds((1, width), F32)
    (
        grad_tinner, grad_tibias, grad_touter, grad_tobias, gsecond, ssecond, bdown, gfirst, sfirst,
        bout, own_bup, own_q, own_v,
    ) = call(
        last_body,
        [sds(time_inner.shape, F32), sds(time_ibias.shape, F32), sds(time_outer.shape, F32)]
        + [line] * 8 + [row] * 2,
        (
            t[None], feats, time_inner, time_ibias, time_outer,
            gath[:, :, :seqs].reshape(-1, width), small,
        ),
        1, smem=(0,), window=8,
    )
    d_all, u_all, q_all, o_all = call(
        join_body, [part(1, F32)] * 2 + [sds((3 * w, width), F32), sds((w, width), F32)],
        (own_bits, d_own, d_x, u_own, u_z, a_end, *a_got), 1, smem=(0,), window=16,
    )

    grad_qkv = jnp.transpose(q_all.reshape(3, w, width), (2, 0, 1))
    return (
        layer_out,
        grad_tokens,
        grad_tinner,
        grad_tibias,
        grad_touter,
        grad_tobias,
        grad_qkv,
        jnp.concatenate([own_q[:, :w], own_v[:, :w]], axis=0),
        o_all,
        bout,
        gfirst,
        sfirst,
        u_all,
        own_bup,
        d_all,
        bdown,
        gsecond,
        ssecond,
    )


def solution(mesh):
    both = ("dp", "tensor")
    placed = (
        P(both, None), P(both), P("dp"), P(), P(), P(), P(), P(None, None, "tensor"),
        P(None, "tensor"), P("tensor", None), P(), P(), P(), P("tensor", None), P("tensor"),
        P("tensor", None), P(), P(), P(), P(both, None),
    )
    return jax.shard_map(
        functools.partial(local, mesh.shape["dp"], mesh.shape["tensor"]),
        mesh=mesh,
        in_specs=placed,
        out_specs=(
            P(both, None), P(both, None), P(), P(), P(), P(), P(None, None, "tensor"),
            P(None, "tensor"), P("tensor", None), P(), P(), P(), P("tensor", None), P("tensor"),
            P("tensor", None), P(), P(), P(),
        ),
        check_vma=False,
    )
```

```python
import functools
import math

import jax
import jax.numpy as jnp
from jax import lax
from jax.experimental import pallas as pl
from jax.experimental.pallas import tpu as pltpu
from jax.sharding import PartitionSpec as P

L = 128
HD = 64
EPS = 1e-05
F32 = jnp.float32
BF = jnp.bfloat16
NN = ((1,), (0,))
NT = ((1,), (1,))
TN = ((0,), (0,))
LOW = 62
BIG = 64 * 1024
CHUNKS = 8


def dot(left, right, dims):
    return lax.dot_general(left, right, (dims, ((), ())), preferred_element_type=F32)


def exact(left, right, dims):
    return lax.dot_general(
        left, right, (dims, ((), ())), precision=lax.Precision.HIGHEST, preferred_element_type=F32
    )


class Loaded:
    def __init__(self, ref, copies=(), queue=None):
        self.ref, self.copies, self.queue = ref, list(copies), queue

    def __call__(self):
        if self.copies:
            while self.queue[0] and self not in self.queue[1]:
                advance(self.queue)
            for copy in self.copies:
                copy.wait()
            self.copies = []
            advance(self.queue)
        return self.ref


def advance(queue):
    if queue[0]:
        item = queue[0].pop(0)
        for copy in item.copies:
            copy.start()
        queue[1].append(item)


class Stored:
    def __init__(self, ref, dst=None, sems=None):
        self.ref, self.dst, self.sems = ref, dst, sems
        self.copies, self.whole = [], False

    def put(self, lo=None, n=None):
        if self.dst is None or self.whole:
            return
        self.whole = lo is None
        src, dst = self.ref, self.dst
        if lo is not None:
            src, dst = src.at[pl.ds(lo, n)], dst.at[pl.ds(lo, n)]
        copy = pltpu.make_async_copy(src, dst, self.sems[len(self.copies)])
        copy.start()
        self.copies.append(copy)

    def finish(self):
        if not self.copies:
            self.put()
        for copy in self.copies:
            copy.wait()


class PartOf:
    def __init__(self, out, lo, n):
        self.out, self.lo, self.n = out, lo, n
        self.ref = out.ref.at[pl.ds(lo, n), :]

    def put(self):
        self.out.put(self.lo, self.n)


def call(body, outs, args, flops, scratch=(), smem=(), place=None, window=4, limit=62):
    place = place or {}
    size = lambda v: math.prod(v.shape) * v.dtype.itemsize
    moved = sum(size(v) for v in list(outs) + list(args))
    big_in = [i for i, v in enumerate(args) if i not in smem and size(v) >= BIG]
    held = [i for i in big_in if i not in place]
    big_out = [i for i, v in enumerate(outs) if size(v) >= BIG]
    n_in, n_out = len(args), len(outs)
    def kernel(*refs):
        ins = [Loaded(r) for r in refs[:n_in]]
        res = [Stored(r) for r in refs[n_in : n_in + n_out]]
        rest = refs[n_in + n_out :]
        held_in, rest = rest[: len(held)], rest[len(held) :]
        held_out, rest = rest[: len(big_out)], rest[len(big_out) :]
        extra, (sem_in, sem_out) = rest[:-2], rest[-2:]
        queue = ([], [])
        sem = 0
        for i in big_in:
            if i in place:
                dst, pairs = place[i](refs, extra)
            else:
                dst = held_in[held.index(i)]
                pairs = [(refs[i], dst)]
            copies = []
            for one, two in pairs:
                copies.append(pltpu.make_async_copy(one, two, sem_in.at[sem]))
                sem += 1
            ins[i] = Loaded(dst, copies, queue)
            queue[0].append(ins[i])
        for _ in range(window):
            advance(queue)
        for k, i in enumerate(big_out):
            sems = [sem_out.at[k * CHUNKS + c] for c in range(CHUNKS)]
            res[i] = Stored(held_out[k], refs[n_in + i], sems)
        body(ins, res, extra)
        for item in ins:
            item()
        for item in res:
            item.finish()

    def spec(i, big):
        if i in big:
            return pl.BlockSpec(memory_space=pl.ANY)
        return pl.BlockSpec(memory_space=pltpu.VMEM)

    return pl.pallas_call(
        kernel,
        out_shape=outs,
        in_specs=[
            pl.BlockSpec(memory_space=pltpu.SMEM) if i in smem else spec(i, big_in)
            for i in range(n_in)
        ],
        out_specs=[spec(i, big_out) for i in range(n_out)],
        scratch_shapes=[pltpu.VMEM(args[i].shape, args[i].dtype) for i in held]
        + [pltpu.VMEM(outs[i].shape, outs[i].dtype) for i in big_out]
        + list(scratch)
        + [pltpu.SemaphoreType.DMA((len(big_in) + 3 * len(place) + 1,)), pltpu.SemaphoreType.DMA((max(1, len(big_out)) * CHUNKS,))],
        cost_estimate=pl.CostEstimate(flops=int(flops), bytes_accessed=int(moved), transcendentals=0),
        compiler_params=pltpu.CompilerParams(vmem_limit_bytes=limit * 1024 * 1024),
    )(*args)


def sds(shape, dtype):
    return jax.ShapeDtypeStruct(shape, dtype)


def head_mask(width):
    lane = lax.broadcasted_iota(jnp.int32, (1, width), 1)
    first = jnp.where(lane < width // 2, 1.0, 0.0)
    return first.astype(BF), (1.0 - first).astype(BF)


def doubled(pair, masks):
    return jnp.concatenate([pair * masks[0], pair * masks[1]], axis=0)


def far_places(j_at, first, scratch):
    def place_of(s, k):
        def pairs(refs, extra):
            dst = extra[scratch + s]
            n = dst.shape[0] // 4
            row = pl.multiple_of((refs[j_at][0] ^ k) * n, n)
            return dst, [(refs[first + 4 * s + k], dst.at[pl.ds(row, n), :])]

        return pairs

    return {first + 4 * s + k: place_of(s, k) for s in range(2) for k in range(4)}


class Whole:
    def __init__(self, parts, ref=None):
        self.parts, self.ref = parts, parts[0].ref if ref is None else ref

    def __call__(self):
        for part in self.parts:
            part()
        return self.ref


class Rows:
    def __init__(self, item, lo, n):
        self.item, self.ref = item, item.ref.at[pl.ds(lo, n), :]

    def __call__(self):
        self.item()
        return self.ref


def side_by_side(a_ref, b_ref, row, w):
    a = a_ref[...].astype(F32)
    b = b_ref[...].astype(F32)
    return (a + pltpu.roll(b, w, 1))[row : row + 1, : 2 * w]


def joined(weights, w):
    return jnp.concatenate([q[k * w : (k + 1) * w, :] for k in range(3) for q in weights], axis=0)


def attn_fwd_core(x, weights, outs, biases, len_ref, qkv_ref, p_ref, mix_ref, stored):
    w = outs[0].ref.shape[0]
    rows = x.shape[0]
    seqs = rows // L
    wide = 2 * w
    total = dot(x, joined([q() for q in weights], w), NT)
    qkv_ref[:, :wide] = (total[:, :wide] + side_by_side(*biases, 0, w)).astype(BF)
    qkv_ref[:, wide : 2 * wide] = total[:, wide : 2 * wide].astype(BF)
    qkv_ref[:, 2 * wide :] = (total[:, 2 * wide :] + side_by_side(*biases, 1, w)).astype(BF)
    stored[0].put()
    masks = head_mask(2 * HD)
    key_at = lax.broadcasted_iota(jnp.int32, (L, L), 0)
    pairs = wide // (2 * HD)
    for s in range(seqs):
        at = slice(s * L, (s + 1) * L)
        valid = key_at < len_ref[s]
        for pair in range(pairs):
            lo = pair * 2 * HD
            q = qkv_ref[at, lo : lo + 2 * HD]
            k = qkv_ref[at, wide + lo : wide + lo + 2 * HD]
            v = qkv_ref[at, 2 * wide + lo : 2 * wide + lo + 2 * HD]
            scores = dot(doubled(k, masks), q, NT) * HD ** (-0.5)
            lows = []
            for h in range(2):
                part = jnp.where(valid, scores[h * L : (h + 1) * L], -1e30)
                expo = jnp.exp(part - jnp.max(part, axis=0, keepdims=True))
                prob = expo * (1.0 / jnp.sum(expo, axis=0, keepdims=True))
                p_ref[s * pairs + pair, h * L : (h + 1) * L, :] = prob
                lows.append(prob.astype(BF))
            mixed = dot(jnp.concatenate(lows, axis=0), doubled(v, masks), TN)
            mix_ref[at, lo : lo + 2 * HD] = mixed.astype(BF)
        stored[1].put(s * pairs, pairs)
    stored[2].put()
    return jnp.concatenate([o()[...] for o in outs], axis=0)


def start_of(tok_ref, temb_ref):
    rows, width = tok_ref.shape
    seqs = rows // L
    return [
        tok_ref[s * L : (s + 1) * L, :].astype(F32) + temb_ref[s : s + 1, :] for s in range(seqs)
    ]


def blocks_of(rows):
    n = rows // 3 if rows % (3 * L) == 0 else rows
    return [(slice(lo, lo + n), lo, n) for lo in range(0, rows, n)]


def attn_near_body(ins, res, extra):
    len_r, tok, temb, qa, qb, ba, bb, oa, ob = ins
    x, qkv, p, mix, acc = res
    for s, rows in enumerate(start_of(tok(), temb())):
        x.ref[s * L : (s + 1) * L, :] = rows.astype(BF)
    x.put()
    out = attn_fwd_core(
        x.ref[...], (qa, qb), (oa, ob), (ba(), bb()), len_r(), qkv.ref, p.ref, mix.ref, (qkv, p, mix)
    )
    for at, lo, n in blocks_of(mix.ref.shape[0]):
        acc.ref[at, :] = dot(mix.ref[at, :], out, NN)
        acc.put(lo, n)


def far_weights(pieces):
    both = (Whole(pieces[:4]), Whole(pieces[4:]))
    w = both[0].ref.shape[0] // 4
    return both, tuple(Rows(f, 3 * w, w) for f in both)


def row_mean(value):
    return jnp.mean(value, axis=-1, keepdims=True)


def unit_of(value):
    centred = value - row_mean(value)
    rate = lax.rsqrt(row_mean(centred * centred) + EPS)
    return centred * rate, rate


def attn_far_body(ins, res, extra):
    len_r, j, x, *pieces, ba, bb, near, tok, temb, ob_v, g_v, s_v = ins
    qkv, p, mix, first_o, low = res
    weights, outs = far_weights(pieces)
    out = attn_fwd_core(
        x()[...], weights, outs, (ba(), bb()), len_r(), qkv.ref, p.ref, mix.ref, (qkv, p, mix)
    )
    out_bias, gain, shift = (vector(v) for v in (ob_v, g_v, s_v))
    first_ref = first_o.ref
    near_ref, starts = near(), start_of(tok(), temb())
    for rows, lo, n in blocks_of(mix.ref.shape[0]):
        first_ref[rows, :] = dot(mix.ref[rows, :], out, NN) + near_ref[rows, :] + out_bias
        for s in range(lo // L, (lo + n) // L):
            at = slice(s * L, (s + 1) * L)
            first = first_ref[at, :] + starts[s]
            first_ref[at, :] = first
            unit, _ = unit_of(first)
            low.ref[at, :] = (unit * gain + shift).astype(BF)
        first_o.put(lo, n)
        low.put(lo, n)


def vector(item):
    return item()[...].astype(F32).reshape(1, -1)


def gelu_pair(pre):
    cdf = 0.5 * (1.0 + lax.erf(pre * 0.7071067811865476))
    pdf = jnp.exp(-0.5 * pre * pre) * 0.3989422804014327
    return pre * cdf, cdf + pre * pdf


def mlp_fwd_core(x_ref, ups, downs, biases, act_ref, slope_ref, acc_ref, done=None):
    rows = x_ref.shape[0]
    hid = ups[0].ref.shape[0]
    block = 256 if rows % 256 == 0 else rows
    for r in range(len(ups)):
        cols = slice(r * hid, (r + 1) * hid)
        up = ups[r]()[...]
        down = downs[r]() if downs is not None else None
        bias = biases[r].astype(F32)
        for m in range(rows // block):
            at = slice(m * block, (m + 1) * block)
            act, slope = gelu_pair(dot(x_ref[at, :], up, NT) + bias)
            low = act.astype(BF)
            if act_ref is not None:
                act_ref[at, cols] = low
                slope_ref[at, cols] = slope
            if acc_ref is None:
                continue
            part = dot(low, down[...], NN)
            if r == 0:
                acc_ref[at, :] = part
            else:
                acc_ref[at, :] += part
            if done is not None and r == len(ups) - 1:
                done(m * block, block)


def mlp_near_body(ins, res, extra):
    x, ua, ub, da, db, ba, bb = ins
    (acc,) = res
    mlp_fwd_core(
        x(), (ua, ub), (da, db), (ba()[2:3, :], bb()[2:3, :]), None, None, acc.ref, acc.put
    )


def mlp_far_body(ins, res, extra):
    j, x, *pieces, ba, bb, near, first, cot, g1_v, s1_v, b_v, g2_v, s2_v = ins
    fa, fb = Whole(pieces[:4]), Whole(pieces[4:])
    dub, ddb, dua, dda, bsb, bsa, out, low, sums, grad = res
    _, _, up_ref, down_ref, act_ref, slope_ref, acc_ref = extra
    hid = fa.ref.shape[0] // 2
    ups = tuple(Rows(f, 0, hid) for f in (fa, fb))
    downs = tuple(Rows(f, hid, hid) for f in (fa, fb))
    mlp_fwd_core(
        x(), ups, downs, (ba()[2:3, :], bb()[2:3, :]), act_ref, slope_ref, acc_ref
    )
    rows, width = x().shape
    first_ref, near_ref, cot_ref, sums_ref = first(), near(), cot(), sums.ref
    gain1, shift1, bias, gain, shift = [vector(v) for v in (g1_v, s1_v, b_v, g2_v, s2_v)]
    sums_ref[...] = jnp.zeros_like(sums_ref)
    for s in range(rows // L):
        at = slice(s * L, (s + 1) * L)
        unit1, _ = unit_of(first_ref[at, :])
        normed = unit1 * gain1 + shift1
        second = normed + acc_ref[at, :] + near_ref[at, :] + bias
        unit, rate = unit_of(second)
        out.ref[at, :] = (unit * gain + shift).astype(BF)
        grad_out = cot_ref[at, :].astype(F32)
        inner = grad_out * gain
        lower = rate * (inner - row_mean(inner) - unit * row_mean(inner * unit))
        grad.ref[at, :] = lower
        low.ref[at, :] = lower.astype(BF)
        sums_ref[0:1, :] += jnp.sum(grad_out * unit, axis=0, keepdims=True)
        sums_ref[1:2, :] += jnp.sum(grad_out, axis=0, keepdims=True)
        sums_ref[2:3, :] += jnp.sum(lower, axis=0, keepdims=True)
    out.put()
    low.put()
    for r in range(2):
        at = slice(r * hid, (r + 1) * hid)
        up_ref[at, :] = ups[r]()[...]
        down_ref[at, :] = downs[r]()[...]
    grad.ref[...] += mlp_bwd_core(
        x, low.ref, lambda: up_ref, lambda: down_ref, lambda: act_ref, lambda: slope_ref,
        (dua, dub), (dda, ddb), (bsa, bsb),
    )


def mlp_bwd_core(x, gl_ref, up, down, act, slope, dus, dds, bsums):
    hid = dus[0].ref.shape[0]
    total = dot(act()[...], gl_ref[...], TN)
    for r in (1, 0):
        dds[r].ref[...] = total[r * hid : (r + 1) * hid].astype(dds[r].ref.dtype)
        dds[r].put()
    gp = (dot(gl_ref[...], down()[...], NT) * slope()[...]).astype(BF)
    total = dot(gp, x()[...], TN)
    for r in (1, 0):
        dus[r].ref[...] = total[r * hid : (r + 1) * hid].astype(dus[r].ref.dtype)
        dus[r].put()
    sums = jnp.sum(gp.astype(F32), axis=0, keepdims=True)
    for r in range(2):
        bsums[r].ref[...] = sums[:, r * hid : (r + 1) * hid]
    return dot(gp, up()[...], NN)


def mlp_bwd_near_body(ins, res, extra):
    x, ua, ub, low, da, db, prev, first, g_v, ba, bb = ins
    up_ref, down_ref, act_ref, slope_ref = extra
    dub, ddb, dua, dda, bsb, bsa, gf, gl, sums = res
    gf_ref, sums_ref = gf.ref, sums.ref
    mlp_fwd_core(
        x(), (ua, ub), None, (ba()[2:3, :], bb()[2:3, :]), act_ref, slope_ref, None
    )
    gf_ref[...] = mlp_bwd_core(
        x, low(), lambda: up_ref, Whole((da, db), down_ref), lambda: act_ref, lambda: slope_ref,
        (dua, dub), (dda, ddb), (bsa, bsb),
    )
    rows = x().shape[0]
    prev_ref, first_ref = prev(), first()
    gain = vector(g_v)
    sums_ref[...] = jnp.zeros_like(sums_ref)
    for s in range(rows // L):
        at = slice(s * L, (s + 1) * L)
        unit, rate = unit_of(first_ref[at, :])
        upper = gf_ref[at, :] + prev_ref[at, :]
        inner = upper * gain
        lower = rate * (inner - row_mean(inner) - unit * row_mean(inner * unit))
        gf_ref[at, :] = lower
        gl.ref[at, :] = lower.astype(BF)
        gl.put(s * L, L)
        gf.put(s * L, L)
        sums_ref[0:1, :] += jnp.sum(upper * unit, axis=0, keepdims=True)
        sums_ref[1:2, :] += jnp.sum(upper, axis=0, keepdims=True)
        sums_ref[2:3, :] += jnp.sum(lower, axis=0, keepdims=True)


def near_places(first, scratch):
    def place_of(s):
        def pairs(refs, extra):
            n = extra[scratch].shape[0] // 2
            dst = extra[scratch].at[pl.ds(s * n, n), :]
            return dst, [(refs[first + s], dst)]

        return pairs

    return {first + s: place_of(s) for s in range(2)}


def attn_bwd_core(x, gl, weights, outs, qkv, p, mix, da, db, bsum_ref, gm_ref, dj_ref):
    rows = gl.shape[0]
    seqs = rows // L
    w = outs[0].ref.shape[0]
    wide = 2 * w
    gm_ref[...] = dot(gl, jnp.concatenate([o()[...] for o in outs], axis=0), NT).astype(BF)
    dout = dot(mix()[...], gl, TN)
    da.ref[3 * w : 4 * w, :] = dout[:w].astype(da.ref.dtype)
    db.ref[3 * w : 4 * w, :] = dout[w:].astype(db.ref.dtype)
    masks = head_mask(2 * HD)
    half = lax.broadcasted_iota(jnp.int32, (L, 2 * HD), 1) < HD
    pairs = wide // (2 * HD)
    scale = HD ** (-0.5)
    qkv_ref, p_ref = qkv(), p()

    for s in range(seqs):
        at = slice(s * L, (s + 1) * L)
        for pair in range(pairs):
            lo = pair * 2 * HD
            q = qkv_ref[at, lo : lo + 2 * HD]
            k = qkv_ref[at, wide + lo : wide + lo + 2 * HD]
            v = qkv_ref[at, 2 * wide + lo : 2 * wide + lo + 2 * HD]
            go = gm_ref[at, lo : lo + 2 * HD]
            prob = p_ref[s * pairs + pair]
            dv = dot(prob.astype(BF), go, NN)
            dp = dot(doubled(v, masks), go, NT)
            lows = []
            for h in range(2):
                ph = prob[h * L : (h + 1) * L]
                dh = dp[h * L : (h + 1) * L]
                delta = jnp.sum(ph * dh, axis=0, keepdims=True)
                lows.append((ph * (dh - delta)).astype(BF))
            ds = jnp.concatenate(lows, axis=0)
            dk = dot(ds, q, NN)
            dq = dot(ds, doubled(k, masks), TN) * scale
            dj_ref[at, lo : lo + 2 * HD] = dq.astype(BF)
            dj_ref[at, wide + lo : wide + lo + 2 * HD] = (
                jnp.where(half, dk[:L], dk[L:]) * scale
            ).astype(BF)
            dj_ref[at, 2 * wide + lo : 2 * wide + lo + 2 * HD] = jnp.where(
                half, dv[:L], dv[L:]
            ).astype(BF)

    dj = dj_ref[...]
    grads = dot(dj, x()[...], TN)
    for k in range(3):
        lo = k * wide
        da.ref[k * w : (k + 1) * w, :] = grads[lo : lo + w].astype(da.ref.dtype)
        db.ref[k * w : (k + 1) * w, :] = grads[lo + w : lo + wide].astype(db.ref.dtype)
    db.put()
    da.put()
    bsum_ref[...] = jnp.zeros_like(bsum_ref)
    bsum_ref[0:1, :] = jnp.sum(dj[:, :wide].astype(F32), axis=0, keepdims=True)
    bsum_ref[1:2, :] = jnp.sum(dj[:, 2 * wide :].astype(F32), axis=0, keepdims=True)
    return dj, joined([q() for q in weights], w)


def attn_bwd_far_body(ins, res, extra):
    j, g, *pieces, mix, qkv, p, x = ins
    db, da, bsum, acc = res
    _, _, gm_ref, dj_ref = extra
    weights, outs = far_weights(pieces)
    dj, big = attn_bwd_core(
        x, g()[...], weights, outs, qkv, p, mix, da, db, bsum.ref, gm_ref, dj_ref
    )
    for at, lo, n in blocks_of(dj.shape[0]):
        acc.ref[at, :] = dot(dj[at, :], big, NN)
        acc.put(lo, n)


def attn_bwd_near_body(ins, res, extra):
    t, g, oa, ob, mix, qkv, p, x, qa, qb, far, g_full, sums2, sums1, b0, b1, b2, b3, far_bsum, steps = ins
    db, da, gt, pack = res
    gm_ref, dj_ref, bsum_ref = extra
    bsum = Loaded(bsum_ref)
    gl = g()[...]
    dj, big = attn_bwd_core(
        x, gl, (qa, qb), (oa, ob), qkv, p, mix, da, db, bsum.ref, gm_ref, dj_ref
    )
    far_ref, full_ref = far(), g_full()
    for at, lo, n in blocks_of(gl.shape[0]):
        gt.ref[at, :] = dot(dj[at, :], big, NN) + far_ref[at, :] + full_ref[at, :]
        gt.put(lo, n)
    pack_ref = pack.ref
    pack_ref[...] = jnp.zeros_like(pack_ref)
    pack_ref[0:3, :] = sums2()[0:3, :]
    pack_ref[3:6, :] = sums1()[0:3, :]
    wide = far_bsum.ref.shape[1]
    for r, bias in enumerate((b0, b1, b2, b3)):
        at = t()[0] ^ r
        pack_ref[pl.ds(8 + at, 1), :] = bias()[...]
        sums = (bsum_ref if r < 2 else far_bsum())[...]
        if r % 2:
            sums = pltpu.roll(sums, wide - wide // 2, 1)
        for k in range(2):
            pack_ref[pl.ds(12 + 4 * k + at, 1), :wide] = sums[k : k + 1, :]
    for s in range(gl.shape[0] // L):
        pack_ref[24 + s : 25 + s, :] = jnp.sum(gt.ref[s * L : (s + 1) * L, :], axis=0, keepdims=True)
    pack_ref[31:32, :] = steps()[...]


def halves_at(bit, n):
    keep = pl.multiple_of(bit * n, n)
    send = pl.multiple_of((1 - bit) * n, n)
    return pl.ds(keep, n), pl.ds(send, n)


def cut(refs, bit, keep, send, scale=1):
    n = keep.ref.shape[0]
    for at, out in zip(halves_at(bit, n), (keep, send)):
        total = refs[0][at, :].astype(F32)
        for ref in refs[1:]:
            total = total + ref[at, :].astype(F32)
        out.ref[...] = total.astype(out.ref.dtype)
        out.put()


def pair_sum(one, two, at, out):
    out.ref[...] = (one[at, :].astype(F32) + two[at, :].astype(F32)).astype(out.ref.dtype)


def glue_first_body(ins, res, extra):
    bits, dd, dd2, du, du2 = ins
    d_keep, d_send, u_keep, u_send = res
    cut((dd(), dd2()), bits()[0], d_keep, d_send)
    d_send.put()
    cut((du(), du2()), bits()[1], u_keep, u_send)


def glue_second_body(ins, res, extra):
    bits, dn, dn2, un, un2, df, df_x, uf, uf_z = ins
    dn_keep, x_send, un_keep, un_send, df_send, uf_keep = res
    n = dn_keep.ref.shape[0]
    cut((dn(), dn2()), bits()[0], dn_keep, PartOf(x_send, 0, n))
    cut((un(), un2()), bits()[1], un_keep, un_send)
    pair_sum(df(), df_x(), slice(0, n), df_send)
    df_send.put()
    cut((uf(), uf_z()), bits()[0], uf_keep, PartOf(x_send, n, n // 2))


def glue_third_body(ins, res, extra):
    bits, da, da2, dn, x_got, df_y, un, un_z, uf = ins
    y_send, a_hi, dn_keep, dn_send, un_keep, un_send = res
    n = a_hi.ref.shape[0]
    pair_sum(da(), da2(), slice(n, 2 * n), a_hi)
    a_hi.put()
    out = PartOf(y_send, 0, n)
    pair_sum(da(), da2(), slice(0, n), out)
    out.put()
    n = dn.ref.shape[0]
    cut((dn(), x_got().at[pl.ds(0, n), :], df_y()), bits()[1], dn_keep, dn_send)
    cut((un(), un_z()), bits()[0], un_keep, un_send)
    k = uf.ref.shape[0]
    out = PartOf(y_send, a_hi.ref.shape[0], k)
    pair_sum(uf(), x_got().at[pl.ds(n, k), :], slice(0, k), out)
    out.put()


def glue_fourth_body(ins, res, extra):
    bits, dn, dn_z, un, un_x, y_got = ins
    keep, send = res
    n = keep.ref.shape[0] // 2
    cut((dn(), dn_z()), bits()[2], PartOf(keep, 0, n), PartOf(send, 0, n))
    far = y_got().at[pl.ds(y_got.ref.shape[0] - 2 * n, 2 * n), :]
    cut((un(), un_x(), far), bits()[2], PartOf(keep, n, n), PartOf(send, n, n))


def quarter_of(bits, m):
    return (bits[0] ^ (m & 1)) * 2 + (bits[1] ^ (m >> 1))


def glue_fifth_body(ins, res, extra):
    bits, da, da2, lo, hi = ins
    n = res[0].ref.shape[0]
    a, b, lo_ref, hi_ref = da(), da2(), lo(), hi()
    for m in (1, 2, 3, 0):
        out = res[m]
        at = quarter_of(bits(), m)
        rows = pl.ds(pl.multiple_of(at * n, n), n)
        part = pl.ds(pl.multiple_of((at & 1) * n, n), n)
        total = a[rows, :] + b[rows, :].astype(F32)

        @pl.when(at < 2)
        def _():
            out.ref[...] = (total + lo_ref[part, :].astype(F32)).astype(out.ref.dtype)

        @pl.when(at >= 2)
        def _():
            out.ref[...] = (total + hi_ref[part, :].astype(F32)).astype(out.ref.dtype)

        out.put()


def join_body(ins, res, extra):
    bits, d_own, d_x, u_own, u_z, *quarters = ins
    d_out, u_out, q_out, o_out = res
    n = d_own.ref.shape[0]
    for own, other, out, bit in ((d_own, d_x, d_out, 0), (u_own, u_z, u_out, 1)):
        for item, at in zip((own, other), halves_at(bits()[bit], n)):
            out.ref[at, :] = item()[...].astype(F32)
        out.put()
    n = quarters[0].ref.shape[0]
    for m, item in enumerate(quarters):
        at = quarter_of(bits(), m)
        value = item()[...].astype(F32)

        @pl.when(at < 3)
        def _():
            q_out.ref[pl.ds(pl.multiple_of(at * n, n), n), :] = value

        @pl.when(at == 3)
        def _():
            o_out.ref[...] = value


def last_body(ins, res, extra):
    t, feats, inner, ibias, outer, grad, small = ins
    g_inner, g_ibias, g_outer, g_obias, *vectors, own_bup, own_q, own_v = res
    outer_w = outer()[...].astype(F32)
    pre = exact(feats()[...], inner()[...].astype(F32), NN) + vector(ibias)
    gate = 1.0 / (1.0 + jnp.exp(-pre))
    g = grad()[...]
    g_outer.ref[...] = exact(pre * gate, g, TN)
    g_outer.put()
    g_obias.ref[...] = jnp.sum(g, axis=0)
    hidden = exact(g, outer_w, NT) * (gate * (1.0 + pre * (1.0 - gate)))
    g_inner.ref[...] = exact(feats()[...], hidden, TN)
    g_ibias.ref[...] = jnp.sum(hidden, axis=0)
    small_ref = small()
    for i, out in enumerate(vectors):
        out.ref[...] = small_ref[i, :]
    own_bup.ref[...] = small_ref[pl.ds(8 + t()[0], 1), :].reshape(own_bup.ref.shape)
    for k, out in enumerate((own_q, own_v)):
        out.ref[...] = small_ref[pl.ds(12 + 4 * k + t()[0], 1), :]


def time_features(timesteps, width):
    half = width // 2
    frequency = jnp.exp(-math.log(10000.0) * jnp.arange(half, dtype=F32) / half)
    angles = timesteps.astype(F32)[:, None] * frequency[None, :]
    return jnp.concatenate([jnp.cos(angles), jnp.sin(angles)], axis=1)


def swap(value, axis, size, bit):
    return lax.ppermute(value, axis, [(i, i ^ bit) for i in range(size)])


def tie(value, *others):
    return lax.optimization_barrier((value,) + others)[0]


def halves(bit_set, mine, other):
    low = jnp.where(bit_set, other, mine)
    high = jnp.where(bit_set, mine, other)
    return low, high


def tie(value, *others):
    return lax.optimization_barrier((value,) + others)[0]


def sync(*values):
    return lax.optimization_barrier(values)


def local(dp, tensor, *args):
    (
        tokens, timesteps, lengths, time_inner, time_ibias, time_outer, time_obias, qkv_weight,
        qv_bias, out_weight, out_bias, gain_first, shift_first, up_weight, up_bias, down_weight,
        down_bias, gain_second, shift_second, cotangent,
    ) = args
    rows, width = tokens.shape
    seqs = rows // L
    w = qkv_weight.shape[2]
    hid = up_weight.shape[0]
    t = lax.axis_index("tensor")
    d = lax.axis_index("dp")
    high = list(range(3, dp.bit_length() - 1))
    core = lambda v: swap(v, "tensor", tensor, 1)
    across = lambda v: swap(v, "tensor", tensor, 2)

    j0 = (d & 1) == 1
    j1 = ((d >> 1) & 1) == 1
    own_j = (d & 3)[None]
    own_bits = jnp.stack([d & 1, (d >> 1) & 1, (d >> 2) & 1])
    flat_qkv = jnp.transpose(qkv_weight, (1, 2, 0)).reshape(3 * w, width)
    part_a = [flat_qkv[:w], flat_qkv[w : 2 * w], flat_qkv[2 * w :], out_weight]
    h2 = hid // 2
    part_f = [up_weight[:h2], up_weight[h2:], down_weight[:h2], down_weight[h2:]]

    def pick(parts, j0, j1):
        return jnp.where(j1, jnp.where(j0, parts[3], parts[2]), jnp.where(j0, parts[1], parts[0]))

    def spread(got):
        return [swap(got, "dp", dp, m) for m in (1, 2)]

    a_y = across(pick(part_a, j0, j1))
    qkv_core, out_core = core(flat_qkv), core(out_weight)
    bias = jnp.concatenate(
        [
            jnp.pad(qv_bias, ((0, 0), (0, width - w))),
            jnp.pad(up_bias[None], ((0, 13), (0, 0))),
        ],
        axis=0,
    )
    bias_core, bias_y = core(bias), across(bias)

    features = time_features(timesteps, time_inner.shape[0])
    hidden_time = jax.nn.silu(
        exact(features, time_inner.astype(F32), NN) + time_ibias.astype(F32)
    )
    temb = exact(hidden_time, time_outer.astype(F32), NN) + time_obias.astype(F32)
    temb = jnp.pad(temb, ((0, 8 - seqs), (0, 0))) if seqs < 8 else temb
    own_len = lax.dynamic_slice(lengths, (t * seqs,), (seqs,))

    send_a, send_f, a_y, temb, bias_y, bias_core = sync(
        pick(part_a, ~j0, ~j1), pick(part_f, j0, j1), a_y, temb, bias_y, bias_core
    )
    bias_y2 = core(bias_y)
    a_others = spread(a_y)
    a_others.append(across(send_a))
    f_y = across(send_f)
    wide = 2 * w
    pairs = wide // (2 * HD)
    act_shapes = [
        sds((rows, 3 * wide), BF),
        sds((seqs * pairs, 2 * L, L), F32),
        sds((rows, wide), BF),
    ]
    full = sds((rows, width), F32)
    low_full = sds((rows, width), BF)
    attn_flops = 2 * rows * width * 4 * wide + 4 * rows * L * wide
    x, qkv_n, p_n, mix_n, acc_n = call(
        attn_near_body, [low_full] + act_shapes + [full],
        (own_len, tokens, temb, flat_qkv, qkv_core, bias, bias_core, out_weight, out_core),
        attn_flops, smem=(0,),
    )
    acc_n, bias_y2, f_y, *far_a1 = sync(acc_n, bias_y2, f_y, a_y, *a_others)
    far_a2 = [core(v) for v in far_a1]
    send_f, f_y, acc_n, up_own, down_own, *far_a2 = sync(
        pick(part_f, ~j0, ~j1), f_y, acc_n, up_weight, down_weight, *far_a2
    )
    f_others = spread(f_y)
    f_others.append(across(send_f))
    up_core, down_core = core(up_own), core(down_own)
    wt = pltpu.VMEM((4 * w, width), BF)
    qkv_f, p_f, mix_f, first, normed = call(
        attn_far_body, act_shapes + [full, low_full],
        (
            own_len, own_j, x, *far_a1, *far_a2, bias_y, bias_y2, acc_n,
            tokens, temb, out_bias, gain_first, shift_first,
        ),
        attn_flops, smem=(0, 1), scratch=[wt, wt], place=far_places(1, 3, 0),
    )
    normed, up_core, down_core, *far_f1 = sync(normed, up_core, down_core, f_y, *f_others)
    far_f2 = [core(v) for v in far_f1]
    up_core, down_core = up_core, down_core
    mlp_flops = 2 * rows * width * 4 * hid
    (mlp_n,) = call(
        mlp_near_body, [full],
        (normed, up_weight, up_core, down_weight, down_core, bias, bias_core), mlp_flops,
    )
    mlp_n, *far_f2 = sync(mlp_n, *far_f2)
    mat = pltpu.VMEM((2 * hid, width), BF)
    dw_far = sds((hid, width), BF)
    dw_own = sds((hid, width), F32)
    bsum = sds((1, hid), F32)
    dws = [dw_far, dw_far, dw_own, dw_own, bsum, bsum]
    sums_shape = sds((8, width), F32)
    duf2, ddf2, duf, ddf, bup_f2, bup_f, layer_out, g2_low, sums2, g2 = call(
        mlp_far_body, dws + [low_full, low_full, sums_shape, full],
        (
            own_j, normed, *far_f1, *far_f2, bias_y, bias_y2, mlp_n,
            first, cotangent, gain_first, shift_first, down_bias, gain_second, shift_second,
        ),
        3 * mlp_flops, smem=(0,),
        scratch=[
            mat, mat, mat, mat, pltpu.VMEM((rows, 2 * hid), BF), pltpu.VMEM((rows, 2 * hid), F32),
            pltpu.VMEM((rows, width), F32),
        ],
        place=far_places(0, 2, 0),
    )
    f32 = lambda v: v.astype(F32)

    part = lambda k, dtype: sds((hid // k, width), dtype)

    def glue(body, outs, args):
        return call(body, outs, (own_bits,) + args, 1, smem=(0,), limit=LOW)

    df_keep, df_send, uf_keep, uf_send = glue(
        glue_first_body, [part(2, F32), part(2, BF), part(2, F32), part(2, BF)],
        (ddf, core(ddf2), duf, core(duf2)),
    )
    g2_low, df_keep, df_send, uf_keep, uf_send = sync(g2_low, df_keep, df_send, uf_keep, uf_send)
    along = lambda v, m: swap(v, "dp", dp, m)
    df_x = along(df_send, 1)
    uf_z = along(uf_send, 2)
    dun2, ddn2, dun, ddn, bup_n2, bup_n, g1, g1_low, sums1 = call(
        mlp_bwd_near_body, dws + [full, low_full, sums_shape],
        (
            normed, up_weight, up_core, g2_low, down_weight, down_core, g2, first, gain_first, bias,
            bias_core,
        ),
        2 * mlp_flops, limit=LOW, place={**near_places(1, 0), **near_places(4, 1)},
        scratch=[mat, mat, pltpu.VMEM((rows, 2 * hid), BF), pltpu.VMEM((rows, 2 * hid), F32)],
    )
    dun2, ddn2, df_x, uf_z = sync(dun2, ddn2, df_x, uf_z)
    both = sds((hid // 2 + hid // 4, width), BF)
    dn_keep, x_send, un_keep, un_send, df_send, uf_keep = glue(
        glue_second_body, [part(2, F32), both, part(2, F32), part(2, BF), part(2, BF), part(4, F32)],
        (ddn, core(ddn2), dun, core(dun2), df_keep, df_x, uf_keep, uf_z),
    )
    g1_low, dn_keep, x_send, un_keep, un_send, df_send, uf_keep = sync(
        g1_low, dn_keep, x_send, un_keep, un_send, df_send, uf_keep
    )
    x_got = along(x_send, 1)
    un_z = along(un_send, 2)
    df_y = across(df_send)
    da_shapes = [sds((4 * w, width), BF), sds((4 * w, width), F32), sds((8, wide), F32)]
    bwd_scratch = [pltpu.VMEM((rows, wide), BF), pltpu.VMEM((rows, 3 * wide), BF)]
    daf2, daf, qvb_f, gin_f = call(
        attn_bwd_far_body, da_shapes + [full],
        (own_j, g1_low, *far_a1, *far_a2, mix_f, qkv_f, p_f, x), 2 * attn_flops, limit=LOW,
        smem=(0,), scratch=[wt, wt] + bwd_scratch, place=far_places(0, 2, 0),
    )
    daf2, gin_f, x_got, un_z, df_y = sync(daf2, gin_f, x_got, un_z, df_y)
    qpart = lambda k, dtype: sds((4 * w // k, width), dtype)
    y_send, a_hi, dn_keep, dn_send, un_keep, un_send = glue(
        glue_third_body,
        [sds((2 * w + hid // 4, width), BF), qpart(2, BF)] + [part(4, F32), part(4, BF)] * 2,
        (daf, core(daf2), dn_keep, x_got, df_y, un_keep, un_z, uf_keep),
    )
    g1_low, y_send, a_hi, dn_keep, dn_send, un_keep, un_send = sync(
        g1_low, y_send, a_hi, dn_keep, dn_send, un_keep, un_send
    )
    y_got = across(y_send)
    a_hi = across(a_hi)
    dn_z = along(dn_send, 2)
    un_x = along(un_send, 1)
    steps_row = jnp.pad(timesteps.astype(F32), (0, width - seqs))[None, :]
    dan2, dan, grad_tokens, pack = call(
        attn_bwd_near_body, da_shapes[:2] + [full, sds((32, width), F32)],
        (
            t[None], g1_low, out_weight, out_core, mix_n, qkv_n, p_n, x, flat_qkv, qkv_core, gin_f, g1,
            sums2, sums1, bup_n, bup_n2, bup_f, bup_f2, qvb_f, steps_row,
        ),
        2 * attn_flops, limit=LOW, smem=(0,), scratch=bwd_scratch + [pltpu.VMEM((8, wide), F32)],
    )
    dan2, pack, y_got, dn_z, un_x = sync(dan2, pack, y_got, dn_z, un_x)

    cat = lambda *v: jnp.concatenate(v, axis=0)
    near_a2, pack_c = core(dan2), core(pack)
    du_keep, du_send = glue(
        glue_fourth_body, [part(4, F32), part(4, BF)], (dn_keep, dn_z, un_keep, un_x, y_got)
    )

    def halve(value, which):
        n = value.shape[0] // 2
        at = jnp.where(((d >> which) & 1) == 1, n, 0)
        keep = lax.dynamic_slice_in_dim(value, at, n, 0)
        return keep, lax.dynamic_slice_in_dim(value, n - at, n, 0).astype(BF)

    def high_sum(value):
        for which in high:
            keep, send = halve(value, which)
            value = keep + f32(along(send, 1 << which))
        return value

    def join_bit(value, which, other=None):
        other = along(value, 1 << which) if other is None else other
        return cat(*halves(((d >> which) & 1) == 1, value, other))

    def high_join(value):
        for which in high[::-1]:
            value = join_bit(value, which)
        return value

    two = lambda f, v: cat(f(v[: v.shape[0] // 2]), f(v[v.shape[0] // 2 :]))
    du_z = along(du_send, 4)
    pack, pack_c = sync(pack, pack_c)
    small = pack[:24] + pack_c[:24]
    gath = cat(*halves((t & 1) == 1, pack[24:], pack_c[24:]))
    got_y = across(cat(small, gath))
    near_a2, got_y, a_hi, du_z = sync(near_a2, got_y, a_hi, du_z)

    du = two(high_sum, du_keep + f32(du_z))
    du = two(high_join, du.astype(BF))
    du_z = along(du, 4)
    state = [small + got_y[:24], cat(*halves((t & 2) == 2, gath, got_y[24:]))]

    def small_hop(which):
        small, gath = state
        other = along(cat(small, gath), 1 << which)
        state[:] = [small + other[:24], join_bit(gath, which, other[24:])]

    quarters = glue(
        glue_fifth_body, [qpart(4, F32)] + [qpart(4, BF)] * 3, (dan, near_a2, y_got, a_hi)
    )
    got = [along(quarters[m], m) for m in (1, 2, 3)]
    small_hop(2)
    du, du_z, *rest = sync(du, du_z, *state, *got)
    state[:], got = rest[:2], rest[2:]
    a_keep, a_send = halve(quarters[0] + sum(f32(v) for v in got), 2)
    a_z = along(a_send, 4)
    n = du.shape[0] // 2
    d_own, u_own = join_bit(du[:n], 2, du_z[:n]), join_bit(du[n:], 2, du_z[n:])
    d_z, u_x = along(d_own, 2), along(u_own, 1)
    small_hop(0)
    a_keep, a_z, d_own, u_own, d_z, u_x, *state[:] = sync(
        a_keep, a_z, d_own, u_own, d_z, u_x, *state
    )
    a_end = high_join(high_sum(a_keep + f32(a_z)).astype(BF))
    a_z = along(a_end, 4)
    d_own, u_own = join_bit(d_own, 1, d_z), join_bit(u_own, 0, u_x)
    d_x, u_z = along(d_own, 1), along(u_own, 2)
    small_hop(1)
    for which in high:
        small_hop(which)
    a_end, a_z, *state[:] = sync(a_end, a_z, *state)
    a_end = join_bit(a_end, 2, a_z)
    a_got = [along(a_end, m) for m in (1, 2, 3)]

    small, gath = state
    gath = gath.reshape(dp, tensor, 8, width)
    feats = time_features(gath[:, :, 7, :seqs].reshape(-1), time_inner.shape[0])
    line = sds((width,), F32)
    row = sds((1, width), F32)
    (
        grad_tinner, grad_tibias, grad_touter, grad_tobias, gsecond, ssecond, bdown, gfirst, sfirst,
        bout, own_bup, own_q, own_v,
    ) = call(
        last_body,
        [sds(time_inner.shape, F32), sds(time_ibias.shape, F32), sds(time_outer.shape, F32)]
        + [line] * 8 + [row] * 2,
        (
            t[None], feats, time_inner, time_ibias, time_outer,
            gath[:, :, :seqs].reshape(-1, width), small,
        ),
        1, smem=(0,), window=8, limit=LOW,
    )
    a_end, d_x, u_z, grad_touter, *a_got = sync(a_end, d_x, u_z, grad_touter, *a_got)
    d_all, u_all, q_all, o_all = call(
        join_body, [part(1, F32)] * 2 + [sds((3 * w, width), F32), sds((w, width), F32)],
        (own_bits, d_own, d_x, u_own, u_z, a_end, *a_got), 1, smem=(0,), window=16,
    )

    grad_qkv = jnp.transpose(q_all.reshape(3, w, width), (2, 0, 1))
    return (
        layer_out,
        grad_tokens,
        grad_tinner,
        grad_tibias,
        grad_touter,
        grad_tobias,
        grad_qkv,
        jnp.concatenate([own_q[:, :w], own_v[:, :w]], axis=0),
        o_all,
        bout,
        gfirst,
        sfirst,
        u_all,
        own_bup,
        d_all,
        bdown,
        gsecond,
        ssecond,
    )


def solution(mesh):
    both = ("dp", "tensor")
    placed = (
        P(both, None), P(both), P("dp"), P(), P(), P(), P(), P(None, None, "tensor"),
        P(None, "tensor"), P("tensor", None), P(), P(), P(), P("tensor", None), P("tensor"),
        P("tensor", None), P(), P(), P(), P(both, None),
    )
    return jax.shard_map(
        functools.partial(local, mesh.shape["dp"], mesh.shape["tensor"]),
        mesh=mesh,
        in_specs=placed,
        out_specs=(
            P(both, None), P(both, None), P(), P(), P(), P(), P(None, None, "tensor"),
            P(None, "tensor"), P("tensor", None), P(), P(), P(), P("tensor", None), P("tensor"),
            P("tensor", None), P(), P(), P(),
        ),
        check_vma=False,
    )
```

```python
import functools
import math

import jax
import jax.numpy as jnp
from jax import lax
from jax.experimental import pallas as pl
from jax.experimental.pallas import tpu as pltpu
from jax.sharding import PartitionSpec as P

L = 128
HD = 64
EPS = 1e-05
F32 = jnp.float32
BF = jnp.bfloat16
NN = ((1,), (0,))
NT = ((1,), (1,))
TN = ((0,), (0,))
LOW = 62
BIG = 64 * 1024
CHUNKS = 8


def dot(left, right, dims):
    return lax.dot_general(left, right, (dims, ((), ())), preferred_element_type=F32)


def exact(left, right, dims):
    return lax.dot_general(
        left, right, (dims, ((), ())), precision=lax.Precision.HIGHEST, preferred_element_type=F32
    )


class Loaded:
    def __init__(self, ref, copies=(), queue=None):
        self.ref, self.copies, self.queue = ref, list(copies), queue

    def __call__(self):
        if self.copies:
            while self.queue[0] and self not in self.queue[1]:
                advance(self.queue)
            for copy in self.copies:
                copy.wait()
            self.copies = []
            advance(self.queue)
        return self.ref


def advance(queue):
    if queue[0]:
        item = queue[0].pop(0)
        for copy in item.copies:
            copy.start()
        queue[1].append(item)


class Stored:
    def __init__(self, ref, dst=None, sems=None):
        self.ref, self.dst, self.sems = ref, dst, sems
        self.copies, self.whole = [], False

    def put(self, lo=None, n=None):
        if self.dst is None or self.whole:
            return
        self.whole = lo is None
        src, dst = self.ref, self.dst
        if lo is not None:
            src, dst = src.at[pl.ds(lo, n)], dst.at[pl.ds(lo, n)]
        copy = pltpu.make_async_copy(src, dst, self.sems[len(self.copies)])
        copy.start()
        self.copies.append(copy)

    def finish(self):
        if not self.copies:
            self.put()
        for copy in self.copies:
            copy.wait()


class PartOf:
    def __init__(self, out, lo, n):
        self.out, self.lo, self.n = out, lo, n
        self.ref = out.ref.at[pl.ds(lo, n), :]

    def put(self):
        self.out.put(self.lo, self.n)


def call(body, outs, args, flops, scratch=(), smem=(), place=None, window=4, limit=62):
    place = place or {}
    size = lambda v: math.prod(v.shape) * v.dtype.itemsize
    moved = sum(size(v) for v in list(outs) + list(args))
    big_in = [i for i, v in enumerate(args) if i not in smem and size(v) >= BIG]
    held = [i for i in big_in if i not in place]
    big_out = [i for i, v in enumerate(outs) if size(v) >= BIG]
    n_in, n_out = len(args), len(outs)
    def kernel(*refs):
        ins = [Loaded(r) for r in refs[:n_in]]
        res = [Stored(r) for r in refs[n_in : n_in + n_out]]
        rest = refs[n_in + n_out :]
        held_in, rest = rest[: len(held)], rest[len(held) :]
        held_out, rest = rest[: len(big_out)], rest[len(big_out) :]
        extra, (sem_in, sem_out) = rest[:-2], rest[-2:]
        queue = ([], [])
        sem = 0
        for i in big_in:
            if i in place:
                dst, pairs = place[i](refs, extra)
            else:
                dst = held_in[held.index(i)]
                pairs = [(refs[i], dst)]
            copies = []
            for one, two in pairs:
                copies.append(pltpu.make_async_copy(one, two, sem_in.at[sem]))
                sem += 1
            ins[i] = Loaded(dst, copies, queue)
            queue[0].append(ins[i])
        for _ in range(window):
            advance(queue)
        for k, i in enumerate(big_out):
            sems = [sem_out.at[k * CHUNKS + c] for c in range(CHUNKS)]
            res[i] = Stored(held_out[k], refs[n_in + i], sems)
        body(ins, res, extra)
        for item in ins:
            item()
        for item in res:
            item.finish()

    def spec(i, big):
        if i in big:
            return pl.BlockSpec(memory_space=pl.ANY)
        return pl.BlockSpec(memory_space=pltpu.VMEM)

    return pl.pallas_call(
        kernel,
        out_shape=outs,
        in_specs=[
            pl.BlockSpec(memory_space=pltpu.SMEM) if i in smem else spec(i, big_in)
            for i in range(n_in)
        ],
        out_specs=[spec(i, big_out) for i in range(n_out)],
        scratch_shapes=[pltpu.VMEM(args[i].shape, args[i].dtype) for i in held]
        + [pltpu.VMEM(outs[i].shape, outs[i].dtype) for i in big_out]
        + list(scratch)
        + [pltpu.SemaphoreType.DMA((len(big_in) + 3 * len(place) + 1,)), pltpu.SemaphoreType.DMA((max(1, len(big_out)) * CHUNKS,))],
        cost_estimate=pl.CostEstimate(flops=int(flops), bytes_accessed=int(moved), transcendentals=0),
        compiler_params=pltpu.CompilerParams(vmem_limit_bytes=limit * 1024 * 1024),
    )(*args)


def sds(shape, dtype):
    return jax.ShapeDtypeStruct(shape, dtype)


def head_mask(width):
    lane = lax.broadcasted_iota(jnp.int32, (1, width), 1)
    first = jnp.where(lane < width // 2, 1.0, 0.0)
    return first.astype(BF), (1.0 - first).astype(BF)


def doubled(pair, masks):
    return jnp.concatenate([pair * masks[0], pair * masks[1]], axis=0)


def far_places(j_at, first, scratch):
    def place_of(s, k):
        def pairs(refs, extra):
            dst = extra[scratch + s]
            n = dst.shape[0] // 4
            row = pl.multiple_of((refs[j_at][0] ^ k) * n, n)
            return dst, [(refs[first + 4 * s + k], dst.at[pl.ds(row, n), :])]

        return pairs

    return {first + 4 * s + k: place_of(s, k) for s in range(2) for k in range(4)}


class Whole:
    def __init__(self, parts, ref=None):
        self.parts, self.ref = parts, parts[0].ref if ref is None else ref

    def __call__(self):
        for part in self.parts:
            part()
        return self.ref


class Rows:
    def __init__(self, item, lo, n):
        self.item, self.ref = item, item.ref.at[pl.ds(lo, n), :]

    def __call__(self):
        self.item()
        return self.ref


def side_by_side(a_ref, b_ref, row, w):
    a = a_ref[...].astype(F32)
    b = b_ref[...].astype(F32)
    return (a + pltpu.roll(b, w, 1))[row : row + 1, : 2 * w]


def joined(weights, w):
    return jnp.concatenate([q[k * w : (k + 1) * w, :] for k in range(3) for q in weights], axis=0)


def attn_fwd_core(x, weights, outs, biases, len_ref, qkv_ref, p_ref, mix_ref, stored):
    w = outs[0].ref.shape[0]
    rows = x.shape[0]
    seqs = rows // L
    wide = 2 * w
    total = dot(x, joined([q() for q in weights], w), NT)
    qkv_ref[:, :wide] = (total[:, :wide] + side_by_side(*biases, 0, w)).astype(BF)
    qkv_ref[:, wide : 2 * wide] = total[:, wide : 2 * wide].astype(BF)
    qkv_ref[:, 2 * wide :] = (total[:, 2 * wide :] + side_by_side(*biases, 1, w)).astype(BF)
    stored[0].put()
    masks = head_mask(2 * HD)
    key_at = lax.broadcasted_iota(jnp.int32, (L, L), 0)
    pairs = wide // (2 * HD)
    for s in range(seqs):
        at = slice(s * L, (s + 1) * L)
        valid = key_at < len_ref[s]
        for pair in range(pairs):
            lo = pair * 2 * HD
            q = qkv_ref[at, lo : lo + 2 * HD]
            k = qkv_ref[at, wide + lo : wide + lo + 2 * HD]
            v = qkv_ref[at, 2 * wide + lo : 2 * wide + lo + 2 * HD]
            scores = dot(doubled(k, masks), q, NT) * HD ** (-0.5)
            lows = []
            for h in range(2):
                part = jnp.where(valid, scores[h * L : (h + 1) * L], -1e30)
                expo = jnp.exp(part - jnp.max(part, axis=0, keepdims=True))
                prob = expo * (1.0 / jnp.sum(expo, axis=0, keepdims=True))
                p_ref[s * pairs + pair, h * L : (h + 1) * L, :] = prob
                lows.append(prob.astype(BF))
            mixed = dot(jnp.concatenate(lows, axis=0), doubled(v, masks), TN)
            mix_ref[at, lo : lo + 2 * HD] = mixed.astype(BF)
        stored[1].put(s * pairs, pairs)
    stored[2].put()
    return jnp.concatenate([o()[...] for o in outs], axis=0)


def start_of(tok_ref, temb_ref):
    rows, width = tok_ref.shape
    seqs = rows // L
    return [
        tok_ref[s * L : (s + 1) * L, :].astype(F32) + temb_ref[s : s + 1, :] for s in range(seqs)
    ]


def blocks_of(rows):
    n = rows // 3 if rows % (3 * L) == 0 else rows
    return [(slice(lo, lo + n), lo, n) for lo in range(0, rows, n)]


def attn_near_body(ins, res, extra):
    len_r, tok, temb, qa, qb, ba, bb, oa, ob = ins
    x, qkv, p, mix, acc = res
    for s, rows in enumerate(start_of(tok(), temb())):
        x.ref[s * L : (s + 1) * L, :] = rows.astype(BF)
    x.put()
    out = attn_fwd_core(
        x.ref[...], (qa, qb), (oa, ob), (ba(), bb()), len_r(), qkv.ref, p.ref, mix.ref, (qkv, p, mix)
    )
    for at, lo, n in blocks_of(mix.ref.shape[0]):
        acc.ref[at, :] = dot(mix.ref[at, :], out, NN)
        acc.put(lo, n)


def far_weights(pieces):
    both = (Whole(pieces[:4]), Whole(pieces[4:]))
    w = both[0].ref.shape[0] // 4
    return both, tuple(Rows(f, 3 * w, w) for f in both)


def row_mean(value):
    return jnp.mean(value, axis=-1, keepdims=True)


def unit_of(value):
    centred = value - row_mean(value)
    rate = lax.rsqrt(row_mean(centred * centred) + EPS)
    return centred * rate, rate


def attn_far_body(ins, res, extra):
    len_r, j, x, *pieces, ba, bb, near, tok, temb, ob_v, g_v, s_v = ins
    qkv, p, mix, first_o, low = res
    weights, outs = far_weights(pieces)
    out = attn_fwd_core(
        x()[...], weights, outs, (ba(), bb()), len_r(), qkv.ref, p.ref, mix.ref, (qkv, p, mix)
    )
    out_bias, gain, shift = (vector(v) for v in (ob_v, g_v, s_v))
    first_ref = first_o.ref
    near_ref, starts = near(), start_of(tok(), temb())
    for rows, lo, n in blocks_of(mix.ref.shape[0]):
        first_ref[rows, :] = dot(mix.ref[rows, :], out, NN) + near_ref[rows, :] + out_bias
        for s in range(lo // L, (lo + n) // L):
            at = slice(s * L, (s + 1) * L)
            first = first_ref[at, :] + starts[s]
            first_ref[at, :] = first
            unit, _ = unit_of(first)
            low.ref[at, :] = (unit * gain + shift).astype(BF)
        first_o.put(lo, n)
        low.put(lo, n)


def vector(item):
    return item()[...].astype(F32).reshape(1, -1)


def gelu_pair(pre):
    cdf = 0.5 * (1.0 + lax.erf(pre * 0.7071067811865476))
    pdf = jnp.exp(-0.5 * pre * pre) * 0.3989422804014327
    return pre * cdf, cdf + pre * pdf


def mlp_fwd_core(x_ref, ups, downs, biases, act_ref, slope_ref, acc_ref, done=None):
    rows = x_ref.shape[0]
    hid = ups[0].ref.shape[0]
    block = 256 if rows % 256 == 0 else rows
    for r in range(len(ups)):
        cols = slice(r * hid, (r + 1) * hid)
        up = ups[r]()[...]
        down = downs[r]() if downs is not None else None
        bias = biases[r].astype(F32)
        for m in range(rows // block):
            at = slice(m * block, (m + 1) * block)
            act, slope = gelu_pair(dot(x_ref[at, :], up, NT) + bias)
            low = act.astype(BF)
            if act_ref is not None:
                act_ref[at, cols] = low
                slope_ref[at, cols] = slope
            if acc_ref is None:
                continue
            part = dot(low, down[...], NN)
            if r == 0:
                acc_ref[at, :] = part
            else:
                acc_ref[at, :] += part
            if done is not None and r == len(ups) - 1:
                done(m * block, block)


def mlp_near_body(ins, res, extra):
    x, ua, ub, da, db, ba, bb = ins
    (acc,) = res
    mlp_fwd_core(
        x(), (ua, ub), (da, db), (ba()[2:3, :], bb()[2:3, :]), None, None, acc.ref, acc.put
    )


def mlp_far_body(ins, res, extra):
    j, x, *pieces, ba, bb, near, first, cot, g1_v, s1_v, b_v, g2_v, s2_v = ins
    fa, fb = Whole(pieces[:4]), Whole(pieces[4:])
    dub, ddb, dua, dda, bsb, bsa, out, low, sums, grad = res
    _, _, up_ref, down_ref, act_ref, slope_ref, acc_ref = extra
    hid = fa.ref.shape[0] // 2
    ups = tuple(Rows(f, 0, hid) for f in (fa, fb))
    downs = tuple(Rows(f, hid, hid) for f in (fa, fb))
    mlp_fwd_core(
        x(), ups, downs, (ba()[2:3, :], bb()[2:3, :]), act_ref, slope_ref, acc_ref
    )
    rows, width = x().shape
    first_ref, near_ref, cot_ref, sums_ref = first(), near(), cot(), sums.ref
    gain1, shift1, bias, gain, shift = [vector(v) for v in (g1_v, s1_v, b_v, g2_v, s2_v)]
    sums_ref[...] = jnp.zeros_like(sums_ref)
    for s in range(rows // L):
        at = slice(s * L, (s + 1) * L)
        unit1, _ = unit_of(first_ref[at, :])
        normed = unit1 * gain1 + shift1
        second = normed + acc_ref[at, :] + near_ref[at, :] + bias
        unit, rate = unit_of(second)
        out.ref[at, :] = (unit * gain + shift).astype(BF)
        grad_out = cot_ref[at, :].astype(F32)
        inner = grad_out * gain
        lower = rate * (inner - row_mean(inner) - unit * row_mean(inner * unit))
        grad.ref[at, :] = lower
        low.ref[at, :] = lower.astype(BF)
        sums_ref[0:1, :] += jnp.sum(grad_out * unit, axis=0, keepdims=True)
        sums_ref[1:2, :] += jnp.sum(grad_out, axis=0, keepdims=True)
        sums_ref[2:3, :] += jnp.sum(lower, axis=0, keepdims=True)
    out.put()
    low.put()
    for r in range(2):
        at = slice(r * hid, (r + 1) * hid)
        up_ref[at, :] = ups[r]()[...]
        down_ref[at, :] = downs[r]()[...]
    grad.ref[...] += mlp_bwd_core(
        x, low.ref, lambda: up_ref, lambda: down_ref, lambda: act_ref, lambda: slope_ref,
        (dua, dub), (dda, ddb), (bsa, bsb),
    )


def mlp_bwd_core(x, gl_ref, up, down, act, slope, dus, dds, bsums):
    hid = dus[0].ref.shape[0]
    total = dot(act()[...], gl_ref[...], TN)
    for r in (1, 0):
        dds[r].ref[...] = total[r * hid : (r + 1) * hid].astype(dds[r].ref.dtype)
        dds[r].put()
    gp = (dot(gl_ref[...], down()[...], NT) * slope()[...]).astype(BF)
    total = dot(gp, x()[...], TN)
    for r in (1, 0):
        dus[r].ref[...] = total[r * hid : (r + 1) * hid].astype(dus[r].ref.dtype)
        dus[r].put()
    sums = jnp.sum(gp.astype(F32), axis=0, keepdims=True)
    for r in range(2):
        bsums[r].ref[...] = sums[:, r * hid : (r + 1) * hid]
    return dot(gp, up()[...], NN)


def mlp_bwd_near_body(ins, res, extra):
    x, ua, ub, low, da, db, prev, first, g_v, ba, bb = ins
    up_ref, down_ref, act_ref, slope_ref = extra
    dub, ddb, dua, dda, bsb, bsa, gf, gl, sums = res
    gf_ref, sums_ref = gf.ref, sums.ref
    mlp_fwd_core(
        x(), (ua, ub), None, (ba()[2:3, :], bb()[2:3, :]), act_ref, slope_ref, None
    )
    gf_ref[...] = mlp_bwd_core(
        x, low(), lambda: up_ref, Whole((da, db), down_ref), lambda: act_ref, lambda: slope_ref,
        (dua, dub), (dda, ddb), (bsa, bsb),
    )
    rows = x().shape[0]
    prev_ref, first_ref = prev(), first()
    gain = vector(g_v)
    sums_ref[...] = jnp.zeros_like(sums_ref)
    for s in range(rows // L):
        at = slice(s * L, (s + 1) * L)
        unit, rate = unit_of(first_ref[at, :])
        upper = gf_ref[at, :] + prev_ref[at, :]
        inner = upper * gain
        lower = rate * (inner - row_mean(inner) - unit * row_mean(inner * unit))
        gf_ref[at, :] = lower
        gl.ref[at, :] = lower.astype(BF)
        gl.put(s * L, L)
        gf.put(s * L, L)
        sums_ref[0:1, :] += jnp.sum(upper * unit, axis=0, keepdims=True)
        sums_ref[1:2, :] += jnp.sum(upper, axis=0, keepdims=True)
        sums_ref[2:3, :] += jnp.sum(lower, axis=0, keepdims=True)


def near_places(first, scratch):
    def place_of(s):
        def pairs(refs, extra):
            n = extra[scratch].shape[0] // 2
            dst = extra[scratch].at[pl.ds(s * n, n), :]
            return dst, [(refs[first + s], dst)]

        return pairs

    return {first + s: place_of(s) for s in range(2)}


def attn_bwd_core(x, gl, weights, outs, qkv, p, mix, da, db, bsum_ref, gm_ref, dj_ref):
    rows = gl.shape[0]
    seqs = rows // L
    w = outs[0].ref.shape[0]
    wide = 2 * w
    gm_ref[...] = dot(gl, jnp.concatenate([o()[...] for o in outs], axis=0), NT).astype(BF)
    dout = dot(mix()[...], gl, TN)
    da.ref[3 * w : 4 * w, :] = dout[:w].astype(da.ref.dtype)
    db.ref[3 * w : 4 * w, :] = dout[w:].astype(db.ref.dtype)
    masks = head_mask(2 * HD)
    half = lax.broadcasted_iota(jnp.int32, (L, 2 * HD), 1) < HD
    pairs = wide // (2 * HD)
    scale = HD ** (-0.5)
    qkv_ref, p_ref = qkv(), p()

    for s in range(seqs):
        at = slice(s * L, (s + 1) * L)
        for pair in range(pairs):
            lo = pair * 2 * HD
            q = qkv_ref[at, lo : lo + 2 * HD]
            k = qkv_ref[at, wide + lo : wide + lo + 2 * HD]
            v = qkv_ref[at, 2 * wide + lo : 2 * wide + lo + 2 * HD]
            go = gm_ref[at, lo : lo + 2 * HD]
            prob = p_ref[s * pairs + pair]
            dv = dot(prob.astype(BF), go, NN)
            dp = dot(doubled(v, masks), go, NT)
            lows = []
            for h in range(2):
                ph = prob[h * L : (h + 1) * L]
                dh = dp[h * L : (h + 1) * L]
                delta = jnp.sum(ph * dh, axis=0, keepdims=True)
                lows.append((ph * (dh - delta)).astype(BF))
            ds = jnp.concatenate(lows, axis=0)
            dk = dot(ds, q, NN)
            dq = dot(ds, doubled(k, masks), TN) * scale
            dj_ref[at, lo : lo + 2 * HD] = dq.astype(BF)
            dj_ref[at, wide + lo : wide + lo + 2 * HD] = (
                jnp.where(half, dk[:L], dk[L:]) * scale
            ).astype(BF)
            dj_ref[at, 2 * wide + lo : 2 * wide + lo + 2 * HD] = jnp.where(
                half, dv[:L], dv[L:]
            ).astype(BF)

    dj = dj_ref[...]
    grads = dot(dj, x()[...], TN)
    for k in range(3):
        lo = k * wide
        da.ref[k * w : (k + 1) * w, :] = grads[lo : lo + w].astype(da.ref.dtype)
        db.ref[k * w : (k + 1) * w, :] = grads[lo + w : lo + wide].astype(db.ref.dtype)
    db.put()
    da.put()
    bsum_ref[...] = jnp.zeros_like(bsum_ref)
    bsum_ref[0:1, :] = jnp.sum(dj[:, :wide].astype(F32), axis=0, keepdims=True)
    bsum_ref[1:2, :] = jnp.sum(dj[:, 2 * wide :].astype(F32), axis=0, keepdims=True)
    return dj, joined([q() for q in weights], w)


def attn_bwd_far_body(ins, res, extra):
    j, g, *pieces, mix, qkv, p, x = ins
    db, da, bsum, acc = res
    _, _, gm_ref, dj_ref = extra
    weights, outs = far_weights(pieces)
    dj, big = attn_bwd_core(
        x, g()[...], weights, outs, qkv, p, mix, da, db, bsum.ref, gm_ref, dj_ref
    )
    for at, lo, n in blocks_of(dj.shape[0]):
        acc.ref[at, :] = dot(dj[at, :], big, NN)
        acc.put(lo, n)


def attn_bwd_near_body(ins, res, extra):
    t, g, oa, ob, mix, qkv, p, x, qa, qb, far, g_full, sums2, sums1, b0, b1, b2, b3, far_bsum, steps = ins
    db, da, gt, pack = res
    gm_ref, dj_ref, bsum_ref = extra
    bsum = Loaded(bsum_ref)
    gl = g()[...]
    dj, big = attn_bwd_core(
        x, gl, (qa, qb), (oa, ob), qkv, p, mix, da, db, bsum.ref, gm_ref, dj_ref
    )
    far_ref, full_ref = far(), g_full()
    for at, lo, n in blocks_of(gl.shape[0]):
        gt.ref[at, :] = dot(dj[at, :], big, NN) + far_ref[at, :] + full_ref[at, :]
        gt.put(lo, n)
    pack_ref = pack.ref
    pack_ref[...] = jnp.zeros_like(pack_ref)
    pack_ref[0:3, :] = sums2()[0:3, :]
    pack_ref[3:6, :] = sums1()[0:3, :]
    wide = far_bsum.ref.shape[1]
    for r, bias in enumerate((b0, b1, b2, b3)):
        at = t()[0] ^ r
        pack_ref[pl.ds(8 + at, 1), :] = bias()[...]
        sums = (bsum_ref if r < 2 else far_bsum())[...]
        if r % 2:
            sums = pltpu.roll(sums, wide - wide // 2, 1)
        for k in range(2):
            pack_ref[pl.ds(12 + 4 * k + at, 1), :wide] = sums[k : k + 1, :]
    for s in range(gl.shape[0] // L):
        pack_ref[24 + s : 25 + s, :] = jnp.sum(gt.ref[s * L : (s + 1) * L, :], axis=0, keepdims=True)
    pack_ref[31:32, :] = steps()[...]


def halves_at(bit, n):
    keep = pl.multiple_of(bit * n, n)
    send = pl.multiple_of((1 - bit) * n, n)
    return pl.ds(keep, n), pl.ds(send, n)


def cut(refs, bit, keep, send, scale=1):
    n = keep.ref.shape[0]
    for at, out in zip(halves_at(bit, n), (keep, send)):
        total = refs[0][at, :].astype(F32)
        for ref in refs[1:]:
            total = total + ref[at, :].astype(F32)
        out.ref[...] = total.astype(out.ref.dtype)
        out.put()


def pair_sum(one, two, at, out):
    out.ref[...] = (one[at, :].astype(F32) + two[at, :].astype(F32)).astype(out.ref.dtype)


def glue_first_body(ins, res, extra):
    bits, dd, dd2, du, du2 = ins
    d_keep, d_send, u_keep, u_send = res
    cut((dd(), dd2()), bits()[0], d_keep, d_send)
    d_send.put()
    cut((du(), du2()), bits()[1], u_keep, u_send)


def glue_far_body(ins, res, extra):
    bits, df, df_x, uf, uf_z = ins
    df_send, uf_send, uf_keep = res
    pair_sum(df(), df_x(), slice(0, df.ref.shape[0]), df_send)
    df_send.put()
    cut((uf(), uf_z()), bits()[0], uf_keep, uf_send)


def glue_second_body(ins, res, extra):
    bits, dn, dn2, un, un2 = ins
    dn_keep, dn_send, un_keep, un_send = res
    cut((dn(), dn2()), bits()[0], dn_keep, dn_send)
    cut((un(), un2()), bits()[1], un_keep, un_send)


def glue_near_body(ins, res, extra):
    bits, dn, dn_x, df_y, un, un_z, uf, uf_x = ins
    dn_keep, dn_send, un_keep, un_send, uf_sum = res
    cut((dn(), dn_x(), df_y()), bits()[1], dn_keep, dn_send)
    cut((un(), un_z()), bits()[0], un_keep, un_send)
    pair_sum(uf(), uf_x(), slice(0, uf.ref.shape[0]), uf_sum)


def glue_third_body(ins, res, extra):
    bits, da, da2 = ins
    n = res[0].ref.shape[0]
    for k, out in enumerate(res):
        pair_sum(da(), da2(), slice(k * n, (k + 1) * n), out)
        out.put()


def glue_fourth_body(ins, res, extra):
    bits, dn, dn_z, un, un_x, uf_y = ins
    keep, send = res
    n = keep.ref.shape[0] // 2
    cut((dn(), dn_z()), bits()[2], PartOf(keep, 0, n), PartOf(send, 0, n))
    cut((un(), un_x(), uf_y()), bits()[2], PartOf(keep, n, n), PartOf(send, n, n))


def quarter_of(bits, m):
    return (bits[0] ^ (m & 1)) * 2 + (bits[1] ^ (m >> 1))


def glue_fifth_body(which):
    def body(ins, res, extra):
        bits, da, da2, far = ins
        n = res[0].ref.shape[0]
        a, b, far_ref = da(), da2(), far()
        for m in (1, 2, 3, 0):
            out = res[m]
            at = quarter_of(bits(), m)
            rows = pl.ds(pl.multiple_of(which * 4 * n + at * n, n), n)
            part = pl.ds(pl.multiple_of(at * n, n), n)
            total = a[rows, :] + b[rows, :].astype(F32) + far_ref[part, :].astype(F32)
            out.ref[...] = total.astype(out.ref.dtype)
            out.put()

    return body


def join_body(ins, res, extra):
    bits, d_own, d_x, u_own, u_z, *quarters = ins
    d_out, u_out, q_out, o_out = res
    n = d_own.ref.shape[0]
    for own, other, out, bit in ((d_own, d_x, d_out, 0), (u_own, u_z, u_out, 1)):
        for item, at in zip((own, other), halves_at(bits()[bit], n)):
            out.ref[at, :] = item()[...].astype(F32)
        out.put()
    n = quarters[0].ref.shape[0]
    for m, item in enumerate(quarters):
        at = quarter_of(bits(), m)
        half = n // 2
        ref = item()
        q_out.ref[pl.ds(pl.multiple_of(at * half, half), half), :] = ref[:half, :].astype(F32)
        value = ref[half:, :].astype(F32)

        @pl.when(at < 2)
        def _():
            q_out.ref[pl.ds(pl.multiple_of(4 * half + at * half, half), half), :] = value

        @pl.when(at >= 2)
        def _():
            o_out.ref[pl.ds(pl.multiple_of((at - 2) * half, half), half), :] = value


def last_body(ins, res, extra):
    t, feats, inner, ibias, outer, grad, small = ins
    g_inner, g_ibias, g_outer, g_obias, *vectors, own_bup, own_q, own_v = res
    outer_w = outer()[...].astype(F32)
    pre = exact(feats()[...], inner()[...].astype(F32), NN) + vector(ibias)
    gate = 1.0 / (1.0 + jnp.exp(-pre))
    g = grad()[...]
    g_outer.ref[...] = exact(pre * gate, g, TN)
    g_outer.put()
    g_obias.ref[...] = jnp.sum(g, axis=0)
    hidden = exact(g, outer_w, NT) * (gate * (1.0 + pre * (1.0 - gate)))
    g_inner.ref[...] = exact(feats()[...], hidden, TN)
    g_ibias.ref[...] = jnp.sum(hidden, axis=0)
    small_ref = small()
    for i, out in enumerate(vectors):
        out.ref[...] = small_ref[i, :]
    own_bup.ref[...] = small_ref[pl.ds(8 + t()[0], 1), :].reshape(own_bup.ref.shape)
    for k, out in enumerate((own_q, own_v)):
        out.ref[...] = small_ref[pl.ds(12 + 4 * k + t()[0], 1), :]


def time_features(timesteps, width):
    half = width // 2
    frequency = jnp.exp(-math.log(10000.0) * jnp.arange(half, dtype=F32) / half)
    angles = timesteps.astype(F32)[:, None] * frequency[None, :]
    return jnp.concatenate([jnp.cos(angles), jnp.sin(angles)], axis=1)


def swap(value, axis, size, bit):
    return lax.ppermute(value, axis, [(i, i ^ bit) for i in range(size)])


def tie(value, *others):
    return lax.optimization_barrier((value,) + others)[0]


def halves(bit_set, mine, other):
    low = jnp.where(bit_set, other, mine)
    high = jnp.where(bit_set, mine, other)
    return low, high


def tie(value, *others):
    return lax.optimization_barrier((value,) + others)[0]


def sync(*values):
    return lax.optimization_barrier(values)


def local(dp, tensor, *args):
    (
        tokens, timesteps, lengths, time_inner, time_ibias, time_outer, time_obias, qkv_weight,
        qv_bias, out_weight, out_bias, gain_first, shift_first, up_weight, up_bias, down_weight,
        down_bias, gain_second, shift_second, cotangent,
    ) = args
    rows, width = tokens.shape
    seqs = rows // L
    w = qkv_weight.shape[2]
    hid = up_weight.shape[0]
    t = lax.axis_index("tensor")
    d = lax.axis_index("dp")
    high = list(range(3, dp.bit_length() - 1))
    core = lambda v: swap(v, "tensor", tensor, 1)
    across = lambda v: swap(v, "tensor", tensor, 2)

    j0 = (d & 1) == 1
    j1 = ((d >> 1) & 1) == 1
    own_j = (d & 3)[None]
    own_bits = jnp.stack([d & 1, (d >> 1) & 1, (d >> 2) & 1])
    flat_qkv = jnp.transpose(qkv_weight, (1, 2, 0)).reshape(3 * w, width)
    part_a = [flat_qkv[:w], flat_qkv[w : 2 * w], flat_qkv[2 * w :], out_weight]
    h2 = hid // 2
    part_f = [up_weight[:h2], up_weight[h2:], down_weight[:h2], down_weight[h2:]]

    def pick(parts, j0, j1):
        return jnp.where(j1, jnp.where(j0, parts[3], parts[2]), jnp.where(j0, parts[1], parts[0]))

    def spread(got):
        return [swap(got, "dp", dp, m) for m in (1, 2)]

    a_y = across(pick(part_a, j0, j1))
    qkv_core, out_core = core(flat_qkv), core(out_weight)
    bias = jnp.concatenate(
        [
            jnp.pad(qv_bias, ((0, 0), (0, width - w))),
            jnp.pad(up_bias[None], ((0, 13), (0, 0))),
        ],
        axis=0,
    )
    bias_core, bias_y = core(bias), across(bias)

    features = time_features(timesteps, time_inner.shape[0])
    hidden_time = jax.nn.silu(
        exact(features, time_inner.astype(F32), NN) + time_ibias.astype(F32)
    )
    temb = exact(hidden_time, time_outer.astype(F32), NN) + time_obias.astype(F32)
    temb = jnp.pad(temb, ((0, 8 - seqs), (0, 0))) if seqs < 8 else temb
    own_len = lax.dynamic_slice(lengths, (t * seqs,), (seqs,))

    a_y2 = across(pick(part_a, ~j0, ~j1))
    a_others = spread(a_y)
    send_f, a_y2, temb, bias_y, bias_core = sync(
        pick(part_f, j0, j1), a_y2, temb, bias_y, bias_core
    )
    a_others.append(a_y2)
    bias_y2 = core(bias_y)
    f_y = across(send_f)
    wide = 2 * w
    pairs = wide // (2 * HD)
    act_shapes = [
        sds((rows, 3 * wide), BF),
        sds((seqs * pairs, 2 * L, L), F32),
        sds((rows, wide), BF),
    ]
    full = sds((rows, width), F32)
    low_full = sds((rows, width), BF)
    attn_flops = 2 * rows * width * 4 * wide + 4 * rows * L * wide
    x, qkv_n, p_n, mix_n, acc_n = call(
        attn_near_body, [low_full] + act_shapes + [full],
        (own_len, tokens, temb, flat_qkv, qkv_core, bias, bias_core, out_weight, out_core),
        attn_flops, smem=(0,),
    )
    acc_n, bias_y2, f_y, *far_a1 = sync(acc_n, bias_y2, f_y, a_y, *a_others)
    far_a2 = [core(v) for v in far_a1]
    send_f, f_y, acc_n, up_own, down_own, *far_a2 = sync(
        pick(part_f, ~j0, ~j1), f_y, acc_n, up_weight, down_weight, *far_a2
    )
    f_others = spread(f_y)
    f_others.append(across(send_f))
    up_core, down_core = core(up_own), core(down_own)
    wt = pltpu.VMEM((4 * w, width), BF)
    qkv_f, p_f, mix_f, first, normed = call(
        attn_far_body, act_shapes + [full, low_full],
        (
            own_len, own_j, x, *far_a1, *far_a2, bias_y, bias_y2, acc_n,
            tokens, temb, out_bias, gain_first, shift_first,
        ),
        attn_flops, smem=(0, 1), scratch=[wt, wt], place=far_places(1, 3, 0),
    )
    normed, up_core, down_core, *far_f1 = sync(normed, up_core, down_core, f_y, *f_others)
    far_f2 = [core(v) for v in far_f1]
    up_core, down_core = up_core, down_core
    mlp_flops = 2 * rows * width * 4 * hid
    (mlp_n,) = call(
        mlp_near_body, [full],
        (normed, up_weight, up_core, down_weight, down_core, bias, bias_core), mlp_flops,
    )
    mlp_n, *far_f2 = sync(mlp_n, *far_f2)
    mat = pltpu.VMEM((2 * hid, width), BF)
    dw_far = sds((hid, width), BF)
    dw_own = sds((hid, width), F32)
    bsum = sds((1, hid), F32)
    dws = [dw_far, dw_far, dw_own, dw_own, bsum, bsum]
    sums_shape = sds((8, width), F32)
    duf2, ddf2, duf, ddf, bup_f2, bup_f, layer_out, g2_low, sums2, g2 = call(
        mlp_far_body, dws + [low_full, low_full, sums_shape, full],
        (
            own_j, normed, *far_f1, *far_f2, bias_y, bias_y2, mlp_n,
            first, cotangent, gain_first, shift_first, down_bias, gain_second, shift_second,
        ),
        3 * mlp_flops, smem=(0,),
        scratch=[
            mat, mat, mat, mat, pltpu.VMEM((rows, 2 * hid), BF), pltpu.VMEM((rows, 2 * hid), F32),
            pltpu.VMEM((rows, width), F32),
        ],
        place=far_places(0, 2, 0),
    )
    f32 = lambda v: v.astype(F32)

    part = lambda k, dtype: sds((hid // k, width), dtype)

    def glue(body, outs, args):
        return call(body, outs, (own_bits,) + args, 1, smem=(0,), limit=LOW)

    df_keep, df_send, uf_keep, uf_send = glue(
        glue_first_body, [part(2, F32), part(2, BF), part(2, F32), part(2, BF)],
        (ddf, core(ddf2), duf, core(duf2)),
    )
    g2_low, df_keep, df_send, uf_keep, uf_send = sync(g2_low, df_keep, df_send, uf_keep, uf_send)
    along = lambda v, m: swap(v, "dp", dp, m)
    df_x = along(df_send, 1)
    uf_z = along(uf_send, 2)
    dun2, ddn2, dun, ddn, bup_n2, bup_n, g1, g1_low, sums1 = call(
        mlp_bwd_near_body, dws + [full, low_full, sums_shape],
        (
            normed, up_weight, up_core, g2_low, down_weight, down_core, g2, first, gain_first, bias,
            bias_core,
        ),
        2 * mlp_flops, limit=LOW, place={**near_places(1, 0), **near_places(4, 1)},
        scratch=[mat, mat, pltpu.VMEM((rows, 2 * hid), BF), pltpu.VMEM((rows, 2 * hid), F32)],
    )
    dun2, ddn2, df_x, uf_z = sync(dun2, ddn2, df_x, uf_z)
    near2 = core(ddn2), core(dun2)
    df_send, uf_send, uf_keep = glue(
        glue_far_body, [part(2, BF), part(4, BF), part(4, F32)], (df_keep, df_x, uf_keep, uf_z)
    )
    dn_keep, dn_send, un_keep, un_send = glue(
        glue_second_body, [part(2, F32), part(2, BF)] * 2, (ddn, near2[0], dun, near2[1])
    )
    g1_low, dn_keep, dn_send, un_keep, un_send, df_send, uf_keep, uf_send = sync(
        g1_low, dn_keep, dn_send, un_keep, un_send, df_send, uf_keep, uf_send
    )
    dn_x, uf_x = along(dn_send, 1), along(uf_send, 1)
    un_z = along(un_send, 2)
    df_y = across(df_send)
    da_shapes = [sds((4 * w, width), BF), sds((4 * w, width), F32), sds((8, wide), F32)]
    bwd_scratch = [pltpu.VMEM((rows, wide), BF), pltpu.VMEM((rows, 3 * wide), BF)]
    daf2, daf, qvb_f, gin_f = call(
        attn_bwd_far_body, da_shapes + [full],
        (own_j, g1_low, *far_a1, *far_a2, mix_f, qkv_f, p_f, x), 2 * attn_flops, limit=LOW,
        smem=(0,), scratch=[wt, wt] + bwd_scratch, place=far_places(0, 2, 0),
    )
    daf2, gin_f, dn_x, uf_x, un_z, df_y = sync(daf2, gin_f, dn_x, uf_x, un_z, df_y)
    qpart = lambda k, dtype: sds((4 * w // k, width), dtype)
    far_a2nd = core(daf2)
    dn_keep, dn_send, un_keep, un_send, uf_sum = glue(
        glue_near_body, [part(4, F32), part(4, BF)] * 2 + [part(4, BF)],
        (dn_keep, dn_x, df_y, un_keep, un_z, uf_keep, uf_x),
    )
    a_lo, a_hi = glue(glue_third_body, [qpart(2, BF)] * 2, (daf, far_a2nd))
    g1_low, a_lo, a_hi, dn_keep, dn_send, un_keep, un_send, uf_sum = sync(
        g1_low, a_lo, a_hi, dn_keep, dn_send, un_keep, un_send, uf_sum
    )
    a_lo = across(a_lo)
    uf_y = across(uf_sum)
    a_hi = across(a_hi)
    dn_z = along(dn_send, 2)
    un_x = along(un_send, 1)
    steps_row = jnp.pad(timesteps.astype(F32), (0, width - seqs))[None, :]
    dan2, dan, grad_tokens, pack = call(
        attn_bwd_near_body, da_shapes[:2] + [full, sds((32, width), F32)],
        (
            t[None], g1_low, out_weight, out_core, mix_n, qkv_n, p_n, x, flat_qkv, qkv_core, gin_f, g1,
            sums2, sums1, bup_n, bup_n2, bup_f, bup_f2, qvb_f, steps_row,
        ),
        2 * attn_flops, limit=LOW, smem=(0,), scratch=bwd_scratch + [pltpu.VMEM((8, wide), F32)],
    )
    dan2, pack, a_lo, uf_y, dn_z, un_x = sync(dan2, pack, a_lo, uf_y, dn_z, un_x)

    cat = lambda *v: jnp.concatenate(v, axis=0)
    near_a2, pack_c = core(dan2), core(pack)
    du_keep, du_send = glue(
        glue_fourth_body, [part(4, F32), part(4, BF)], (dn_keep, dn_z, un_keep, un_x, uf_y)
    )

    def halve(value, which):
        n = value.shape[0] // 2
        at = jnp.where(((d >> which) & 1) == 1, n, 0)
        keep = lax.dynamic_slice_in_dim(value, at, n, 0)
        return keep, lax.dynamic_slice_in_dim(value, n - at, n, 0).astype(BF)

    def high_sum(value):
        for which in high:
            keep, send = halve(value, which)
            value = keep + f32(along(send, 1 << which))
        return value

    def join_bit(value, which, other=None):
        other = along(value, 1 << which) if other is None else other
        return cat(*halves(((d >> which) & 1) == 1, value, other))

    def high_join(value):
        for which in high[::-1]:
            value = join_bit(value, which)
        return value

    two = lambda f, v: cat(f(v[: v.shape[0] // 2]), f(v[v.shape[0] // 2 :]))
    du_z = along(du_send, 4)
    cut_half = lambda which, far: glue(
        glue_fifth_body(which), [qpart(8, F32)] + [qpart(8, BF)] * 3, (dan, near_a2, far)
    )
    pack, pack_c = sync(pack, pack_c)
    state = [pack[:24] + pack_c[:24], cat(*halves((t & 1) == 1, pack[24:], pack_c[24:]))]

    def small_hop(which):
        small, gath = state
        other = along(cat(small, gath), 1 << which)
        state[:] = [small + other[:24], join_bit(gath, which, other[24:])]

    small_hop(2)
    q_lo = cut_half(0, a_lo)
    got_lo = [along(q_lo[m], m) for m in (1, 2, 3)]
    near_a2, a_hi, du_z, *state[:] = sync(near_a2, a_hi, du_z, *state)

    du = two(high_sum, du_keep + f32(du_z))
    du = two(high_join, du.astype(BF))
    du_z = along(du, 4)
    q_hi = cut_half(1, a_hi)
    got_hi = [along(q_hi[m], m) for m in (1, 2, 3)]
    small_hop(0)
    du, du_z, *rest = sync(du, du_z, *state, *got_hi, *got_lo)
    state[:], got_hi, got_lo = rest[:2], rest[2:5], rest[5:]

    lo_keep, lo_send = halve(q_lo[0] + sum(f32(v) for v in got_lo), 2)
    hi_keep, hi_send = halve(q_hi[0] + sum(f32(v) for v in got_hi), 2)
    a_z = along(cat(lo_send, hi_send), 4)
    a_keep = cat(lo_keep, hi_keep)
    n = du.shape[0] // 2
    d_own, u_own = join_bit(du[:n], 2, du_z[:n]), join_bit(du[n:], 2, du_z[n:])
    d_z, u_x = along(d_own, 2), along(u_own, 1)
    small_hop(1)
    a_keep, a_z, d_own, u_own, d_z, u_x, *state[:] = sync(
        a_keep, a_z, d_own, u_own, d_z, u_x, *state
    )
    a_end = two(high_join, two(high_sum, a_keep + f32(a_z)).astype(BF))
    a_z = along(a_end, 4)
    d_own, u_own = join_bit(d_own, 1, d_z), join_bit(u_own, 0, u_x)
    d_x = along(d_own, 1)
    for which in high:
        small_hop(which)
    a_end, a_z, u_own, *state[:] = sync(a_end, a_z, u_own, *state)
    u_z = along(u_own, 2)
    other = across(cat(*state))
    state[:] = [state[0] + other[:24], cat(*halves((t & 2) == 2, state[1], other[24:]))]
    n = a_end.shape[0] // 2
    a_end = cat(join_bit(a_end[:n], 2, a_z[:n]), join_bit(a_end[n:], 2, a_z[n:]))
    a_got = [along(a_end, m) for m in (1, 2, 3)]

    small, gath = state
    gath = gath.reshape(dp, tensor, 8, width)
    feats = time_features(gath[:, :, 7, :seqs].reshape(-1), time_inner.shape[0])
    line = sds((width,), F32)
    row = sds((1, width), F32)
    (
        grad_tinner, grad_tibias, grad_touter, grad_tobias, gsecond, ssecond, bdown, gfirst, sfirst,
        bout, own_bup, own_q, own_v,
    ) = call(
        last_body,
        [sds(time_inner.shape, F32), sds(time_ibias.shape, F32), sds(time_outer.shape, F32)]
        + [line] * 8 + [row] * 2,
        (
            t[None], feats, time_inner, time_ibias, time_outer,
            gath[:, :, :seqs].reshape(-1, width), small,
        ),
        1, smem=(0,), window=8, limit=LOW,
    )
    a_end, d_x, u_z, grad_touter, *a_got = sync(a_end, d_x, u_z, grad_touter, *a_got)
    d_all, u_all, q_all, o_all = call(
        join_body, [part(1, F32)] * 2 + [sds((3 * w, width), F32), sds((w, width), F32)],
        (own_bits, d_own, d_x, u_own, u_z, a_end, *a_got), 1, smem=(0,), window=16,
    )

    grad_qkv = jnp.transpose(q_all.reshape(3, w, width), (2, 0, 1))
    return (
        layer_out,
        grad_tokens,
        grad_tinner,
        grad_tibias,
        grad_touter,
        grad_tobias,
        grad_qkv,
        jnp.concatenate([own_q[:, :w], own_v[:, :w]], axis=0),
        o_all,
        bout,
        gfirst,
        sfirst,
        u_all,
        own_bup,
        d_all,
        bdown,
        gsecond,
        ssecond,
    )


def solution(mesh):
    both = ("dp", "tensor")
    placed = (
        P(both, None), P(both), P("dp"), P(), P(), P(), P(), P(None, None, "tensor"),
        P(None, "tensor"), P("tensor", None), P(), P(), P(), P("tensor", None), P("tensor"),
        P("tensor", None), P(), P(), P(), P(both, None),
    )
    return jax.shard_map(
        functools.partial(local, mesh.shape["dp"], mesh.shape["tensor"]),
        mesh=mesh,
        in_specs=placed,
        out_specs=(
            P(both, None), P(both, None), P(), P(), P(), P(), P(None, None, "tensor"),
            P(None, "tensor"), P("tensor", None), P(), P(), P(), P("tensor", None), P("tensor"),
            P("tensor", None), P(), P(), P(),
        ),
        check_vma=False,
    )
```

```python
import functools
import math

import jax
import jax.numpy as jnp
from jax import lax
from jax.experimental import pallas as pl
from jax.experimental.pallas import tpu as pltpu
from jax.sharding import PartitionSpec as P

L = 128
HD = 64
EPS = 1e-05
F32 = jnp.float32
BF = jnp.bfloat16
NN = ((1,), (0,))
NT = ((1,), (1,))
TN = ((0,), (0,))
LOW = 63
BIG = 64 * 1024
CHUNKS = 8


def dot(left, right, dims):
    return lax.dot_general(left, right, (dims, ((), ())), preferred_element_type=F32)


def exact(left, right, dims):
    return lax.dot_general(
        left, right, (dims, ((), ())), precision=lax.Precision.HIGHEST, preferred_element_type=F32
    )


class Loaded:
    def __init__(self, ref, copies=(), queue=None):
        self.ref, self.copies, self.queue = ref, list(copies), queue

    def __call__(self):
        if self.copies:
            while self.queue[0] and self not in self.queue[1]:
                advance(self.queue)
            for copy in self.copies:
                copy.wait()
            self.copies = []
            advance(self.queue)
        return self.ref


def advance(queue):
    if queue[0]:
        item = queue[0].pop(0)
        for copy in item.copies:
            copy.start()
        queue[1].append(item)


class Stored:
    def __init__(self, ref, dst=None, sems=None):
        self.ref, self.dst, self.sems = ref, dst, sems
        self.copies, self.whole = [], False

    def put(self, lo=None, n=None):
        if self.dst is None or self.whole:
            return
        self.whole = lo is None
        src, dst = self.ref, self.dst
        if lo is not None:
            src, dst = src.at[pl.ds(lo, n)], dst.at[pl.ds(lo, n)]
        copy = pltpu.make_async_copy(src, dst, self.sems[len(self.copies)])
        copy.start()
        self.copies.append(copy)

    def finish(self):
        if not self.copies:
            self.put()
        for copy in self.copies:
            copy.wait()


class PartOf:
    def __init__(self, out, lo, n):
        self.out, self.lo, self.n = out, lo, n
        self.ref = out.ref.at[pl.ds(lo, n), :]

    def put(self):
        self.out.put(self.lo, self.n)


def call(body, outs, args, flops, scratch=(), smem=(), place=None, window=4, limit=63):
    place = place or {}
    size = lambda v: math.prod(v.shape) * v.dtype.itemsize
    moved = sum(size(v) for v in list(outs) + list(args))
    big_in = [i for i, v in enumerate(args) if i not in smem and size(v) >= BIG]
    held = [i for i in big_in if i not in place]
    big_out = [i for i, v in enumerate(outs) if size(v) >= BIG]
    n_in, n_out = len(args), len(outs)
    def kernel(*refs):
        ins = [Loaded(r) for r in refs[:n_in]]
        res = [Stored(r) for r in refs[n_in : n_in + n_out]]
        rest = refs[n_in + n_out :]
        held_in, rest = rest[: len(held)], rest[len(held) :]
        held_out, rest = rest[: len(big_out)], rest[len(big_out) :]
        extra, (sem_in, sem_out) = rest[:-2], rest[-2:]
        queue = ([], [])
        sem = 0
        for i in big_in:
            if i in place:
                dst, pairs = place[i](refs, extra)
            else:
                dst = held_in[held.index(i)]
                pairs = [(refs[i], dst)]
            copies = []
            for one, two in pairs:
                copies.append(pltpu.make_async_copy(one, two, sem_in.at[sem]))
                sem += 1
            ins[i] = Loaded(dst, copies, queue)
            queue[0].append(ins[i])
        for _ in range(window):
            advance(queue)
        for k, i in enumerate(big_out):
            sems = [sem_out.at[k * CHUNKS + c] for c in range(CHUNKS)]
            res[i] = Stored(held_out[k], refs[n_in + i], sems)
        body(ins, res, extra)
        for item in ins:
            item()
        for item in res:
            item.finish()

    def spec(i, big):
        if i in big:
            return pl.BlockSpec(memory_space=pl.ANY)
        return pl.BlockSpec(memory_space=pltpu.VMEM)

    return pl.pallas_call(
        kernel,
        out_shape=outs,
        in_specs=[
            pl.BlockSpec(memory_space=pltpu.SMEM) if i in smem else spec(i, big_in)
            for i in range(n_in)
        ],
        out_specs=[spec(i, big_out) for i in range(n_out)],
        scratch_shapes=[pltpu.VMEM(args[i].shape, args[i].dtype) for i in held]
        + [pltpu.VMEM(outs[i].shape, outs[i].dtype) for i in big_out]
        + list(scratch)
        + [pltpu.SemaphoreType.DMA((len(big_in) + 3 * len(place) + 1,)), pltpu.SemaphoreType.DMA((max(1, len(big_out)) * CHUNKS,))],
        cost_estimate=pl.CostEstimate(flops=int(flops), bytes_accessed=int(moved), transcendentals=0),
        compiler_params=pltpu.CompilerParams(vmem_limit_bytes=limit * 1024 * 1024),
    )(*args)


def sds(shape, dtype):
    return jax.ShapeDtypeStruct(shape, dtype)


def head_mask(width):
    lane = lax.broadcasted_iota(jnp.int32, (1, width), 1)
    first = jnp.where(lane < width // 2, 1.0, 0.0)
    return first.astype(BF), (1.0 - first).astype(BF)


def doubled(pair, masks):
    return jnp.concatenate([pair * masks[0], pair * masks[1]], axis=0)


def far_places(j_at, first, scratch):
    def place_of(s, k):
        def pairs(refs, extra):
            dst = extra[scratch + s]
            n = dst.shape[0] // 4
            row = pl.multiple_of((refs[j_at][0] ^ k) * n, n)
            return dst, [(refs[first + 4 * s + k], dst.at[pl.ds(row, n), :])]

        return pairs

    return {first + 4 * s + k: place_of(s, k) for s in range(2) for k in range(4)}


class Whole:
    def __init__(self, parts, ref=None):
        self.parts, self.ref = parts, parts[0].ref if ref is None else ref

    def __call__(self):
        for part in self.parts:
            part()
        return self.ref


class Rows:
    def __init__(self, item, lo, n):
        self.item, self.ref = item, item.ref.at[pl.ds(lo, n), :]

    def __call__(self):
        self.item()
        return self.ref


def side_by_side(a_ref, b_ref, row, w):
    a = a_ref[...].astype(F32)
    b = b_ref[...].astype(F32)
    return (a + pltpu.roll(b, w, 1))[row : row + 1, : 2 * w]


def joined(weights, w):
    return jnp.concatenate([q[k * w : (k + 1) * w, :] for k in range(3) for q in weights], axis=0)


def attn_fwd_core(x, weights, outs, biases, len_ref, qkv_ref, p_ref, mix_ref, stored):
    w = outs[0].ref.shape[0]
    rows = x.shape[0]
    seqs = rows // L
    wide = 2 * w
    total = dot(x, joined([q() for q in weights], w), NT)
    qkv_ref[:, :wide] = (total[:, :wide] + side_by_side(*biases, 0, w)).astype(BF)
    qkv_ref[:, wide : 2 * wide] = total[:, wide : 2 * wide].astype(BF)
    qkv_ref[:, 2 * wide :] = (total[:, 2 * wide :] + side_by_side(*biases, 1, w)).astype(BF)
    stored[0].put()
    masks = head_mask(2 * HD)
    key_at = lax.broadcasted_iota(jnp.int32, (L, L), 0)
    pairs = wide // (2 * HD)
    for s in range(seqs):
        at = slice(s * L, (s + 1) * L)
        valid = key_at < len_ref[s]
        for pair in range(pairs):
            lo = pair * 2 * HD
            q = qkv_ref[at, lo : lo + 2 * HD]
            k = qkv_ref[at, wide + lo : wide + lo + 2 * HD]
            v = qkv_ref[at, 2 * wide + lo : 2 * wide + lo + 2 * HD]
            scores = dot(doubled(k, masks), q, NT) * HD ** (-0.5)
            lows = []
            for h in range(2):
                part = jnp.where(valid, scores[h * L : (h + 1) * L], -1e30)
                expo = jnp.exp(part - jnp.max(part, axis=0, keepdims=True))
                prob = expo * (1.0 / jnp.sum(expo, axis=0, keepdims=True))
                p_ref[s * pairs + pair, h * L : (h + 1) * L, :] = prob
                lows.append(prob.astype(BF))
            mixed = dot(jnp.concatenate(lows, axis=0), doubled(v, masks), TN)
            mix_ref[at, lo : lo + 2 * HD] = mixed.astype(BF)
        stored[1].put(s * pairs, pairs)
    stored[2].put()
    return jnp.concatenate([o()[...] for o in outs], axis=0)


def start_of(tok_ref, temb_ref):
    rows, width = tok_ref.shape
    seqs = rows // L
    return [
        tok_ref[s * L : (s + 1) * L, :].astype(F32) + temb_ref[s : s + 1, :] for s in range(seqs)
    ]


def blocks_of(rows):
    n = rows // 3 if rows % (3 * L) == 0 else rows
    return [(slice(lo, lo + n), lo, n) for lo in range(0, rows, n)]


def attn_near_body(ins, res, extra):
    len_r, tok, temb, qa, qb, ba, bb, oa, ob = ins
    x, qkv, p, mix, acc = res
    for s, rows in enumerate(start_of(tok(), temb())):
        x.ref[s * L : (s + 1) * L, :] = rows.astype(BF)
    x.put()
    out = attn_fwd_core(
        x.ref[...], (qa, qb), (oa, ob), (ba(), bb()), len_r(), qkv.ref, p.ref, mix.ref, (qkv, p, mix)
    )
    for at, lo, n in blocks_of(mix.ref.shape[0]):
        acc.ref[at, :] = dot(mix.ref[at, :], out, NN)
        acc.put(lo, n)


def far_weights(pieces):
    both = (Whole(pieces[:4]), Whole(pieces[4:]))
    w = both[0].ref.shape[0] // 4
    return both, tuple(Rows(f, 3 * w, w) for f in both)


def row_mean(value):
    return jnp.mean(value, axis=-1, keepdims=True)


def unit_of(value):
    centred = value - row_mean(value)
    rate = lax.rsqrt(row_mean(centred * centred) + EPS)
    return centred * rate, rate


def attn_far_body(ins, res, extra):
    len_r, j, x, *pieces, ba, bb, near, tok, temb, ob_v, g_v, s_v = ins
    qkv, p, mix, first_o, low = res
    weights, outs = far_weights(pieces)
    out = attn_fwd_core(
        x()[...], weights, outs, (ba(), bb()), len_r(), qkv.ref, p.ref, mix.ref, (qkv, p, mix)
    )
    out_bias, gain, shift = (vector(v) for v in (ob_v, g_v, s_v))
    first_ref = first_o.ref
    near_ref, starts = near(), start_of(tok(), temb())
    for rows, lo, n in blocks_of(mix.ref.shape[0]):
        first_ref[rows, :] = dot(mix.ref[rows, :], out, NN) + near_ref[rows, :] + out_bias
        for s in range(lo // L, (lo + n) // L):
            at = slice(s * L, (s + 1) * L)
            first = first_ref[at, :] + starts[s]
            first_ref[at, :] = first
            unit, _ = unit_of(first)
            low.ref[at, :] = (unit * gain + shift).astype(BF)
        first_o.put(lo, n)
        low.put(lo, n)


def vector(item):
    return item()[...].astype(F32).reshape(1, -1)


def gelu_pair(pre):
    cdf = 0.5 * (1.0 + lax.erf(pre * 0.7071067811865476))
    pdf = jnp.exp(-0.5 * pre * pre) * 0.3989422804014327
    return pre * cdf, cdf + pre * pdf


def mlp_fwd_core(x_ref, ups, downs, biases, act_ref, slope_ref, acc_ref, done=None):
    rows = x_ref.shape[0]
    hid = ups[0].ref.shape[0]
    block = 256 if rows % 256 == 0 else rows
    for r in range(len(ups)):
        cols = slice(r * hid, (r + 1) * hid)
        up = ups[r]()[...]
        down = downs[r]() if downs is not None else None
        bias = biases[r].astype(F32)
        for m in range(rows // block):
            at = slice(m * block, (m + 1) * block)
            act, slope = gelu_pair(dot(x_ref[at, :], up, NT) + bias)
            low = act.astype(BF)
            if act_ref is not None:
                act_ref[at, cols] = low
                slope_ref[at, cols] = slope
            if acc_ref is None:
                continue
            part = dot(low, down[...], NN)
            if r == 0:
                acc_ref[at, :] = part
            else:
                acc_ref[at, :] += part
            if done is not None and r == len(ups) - 1:
                done(m * block, block)


def mlp_near_body(ins, res, extra):
    x, ua, ub, da, db, ba, bb = ins
    (acc,) = res
    mlp_fwd_core(
        x(), (ua, ub), (da, db), (ba()[2:3, :], bb()[2:3, :]), None, None, acc.ref, acc.put
    )


def mlp_far_body(ins, res, extra):
    j, x, *pieces, ba, bb, near, first, cot, g1_v, s1_v, b_v, g2_v, s2_v = ins
    fa, fb = Whole(pieces[:4]), Whole(pieces[4:])
    dub, ddb, dua, dda, bsb, bsa, out, low, sums, grad = res
    _, _, up_ref, down_ref, act_ref, slope_ref, acc_ref = extra
    hid = fa.ref.shape[0] // 2
    ups = tuple(Rows(f, 0, hid) for f in (fa, fb))
    downs = tuple(Rows(f, hid, hid) for f in (fa, fb))
    mlp_fwd_core(
        x(), ups, downs, (ba()[2:3, :], bb()[2:3, :]), act_ref, slope_ref, acc_ref
    )
    rows, width = x().shape
    first_ref, near_ref, cot_ref, sums_ref = first(), near(), cot(), sums.ref
    gain1, shift1, bias, gain, shift = [vector(v) for v in (g1_v, s1_v, b_v, g2_v, s2_v)]
    sums_ref[...] = jnp.zeros_like(sums_ref)
    for s in range(rows // L):
        at = slice(s * L, (s + 1) * L)
        unit1, _ = unit_of(first_ref[at, :])
        normed = unit1 * gain1 + shift1
        second = normed + acc_ref[at, :] + near_ref[at, :] + bias
        unit, rate = unit_of(second)
        out.ref[at, :] = (unit * gain + shift).astype(BF)
        grad_out = cot_ref[at, :].astype(F32)
        inner = grad_out * gain
        lower = rate * (inner - row_mean(inner) - unit * row_mean(inner * unit))
        grad.ref[at, :] = lower
        low.ref[at, :] = lower.astype(BF)
        sums_ref[0:1, :] += jnp.sum(grad_out * unit, axis=0, keepdims=True)
        sums_ref[1:2, :] += jnp.sum(grad_out, axis=0, keepdims=True)
        sums_ref[2:3, :] += jnp.sum(lower, axis=0, keepdims=True)
    out.put()
    low.put()
    for r in range(2):
        at = slice(r * hid, (r + 1) * hid)
        up_ref[at, :] = ups[r]()[...]
        down_ref[at, :] = downs[r]()[...]
    grad.ref[...] += mlp_bwd_core(
        x, low.ref, lambda: up_ref, lambda: down_ref, lambda: act_ref, lambda: slope_ref,
        (dua, dub), (dda, ddb), (bsa, bsb),
    )


def mlp_bwd_core(x, gl_ref, up, down, act, slope, dus, dds, bsums):
    hid = dus[0].ref.shape[0]
    total = dot(act()[...], gl_ref[...], TN)
    for r in (1, 0):
        dds[r].ref[...] = total[r * hid : (r + 1) * hid].astype(dds[r].ref.dtype)
        dds[r].put()
    gp = (dot(gl_ref[...], down()[...], NT) * slope()[...]).astype(BF)
    total = dot(gp, x()[...], TN)
    for r in (1, 0):
        dus[r].ref[...] = total[r * hid : (r + 1) * hid].astype(dus[r].ref.dtype)
        dus[r].put()
    sums = jnp.sum(gp.astype(F32), axis=0, keepdims=True)
    for r in range(2):
        bsums[r].ref[...] = sums[:, r * hid : (r + 1) * hid]
    return dot(gp, up()[...], NN)


def mlp_bwd_near_body(ins, res, extra):
    x, ua, ub, low, da, db, prev, first, g_v, ba, bb = ins
    up_ref, down_ref, act_ref, slope_ref = extra
    dub, ddb, dua, dda, bsb, bsa, gf, gl, sums = res
    gf_ref, sums_ref = gf.ref, sums.ref
    mlp_fwd_core(
        x(), (ua, ub), None, (ba()[2:3, :], bb()[2:3, :]), act_ref, slope_ref, None
    )
    gf_ref[...] = mlp_bwd_core(
        x, low(), lambda: up_ref, Whole((da, db), down_ref), lambda: act_ref, lambda: slope_ref,
        (dua, dub), (dda, ddb), (bsa, bsb),
    )
    rows = x().shape[0]
    prev_ref, first_ref = prev(), first()
    gain = vector(g_v)
    sums_ref[...] = jnp.zeros_like(sums_ref)
    for s in range(rows // L):
        at = slice(s * L, (s + 1) * L)
        unit, rate = unit_of(first_ref[at, :])
        upper = gf_ref[at, :] + prev_ref[at, :]
        inner = upper * gain
        lower = rate * (inner - row_mean(inner) - unit * row_mean(inner * unit))
        gf_ref[at, :] = lower
        gl.ref[at, :] = lower.astype(BF)
        gl.put(s * L, L)
        gf.put(s * L, L)
        sums_ref[0:1, :] += jnp.sum(upper * unit, axis=0, keepdims=True)
        sums_ref[1:2, :] += jnp.sum(upper, axis=0, keepdims=True)
        sums_ref[2:3, :] += jnp.sum(lower, axis=0, keepdims=True)


def near_places(first, scratch):
    def place_of(s):
        def pairs(refs, extra):
            n = extra[scratch].shape[0] // 2
            dst = extra[scratch].at[pl.ds(s * n, n), :]
            return dst, [(refs[first + s], dst)]

        return pairs

    return {first + s: place_of(s) for s in range(2)}


def attn_bwd_core(x, gl, weights, outs, qkv, p, mix, da, db, bsum_ref, gm_ref, dj_ref):
    rows = gl.shape[0]
    seqs = rows // L
    w = outs[0].ref.shape[0]
    wide = 2 * w
    gm_ref[...] = dot(gl, jnp.concatenate([o()[...] for o in outs], axis=0), NT).astype(BF)
    dout = dot(mix()[...], gl, TN)
    da.ref[3 * w : 4 * w, :] = dout[:w].astype(da.ref.dtype)
    db.ref[3 * w : 4 * w, :] = dout[w:].astype(db.ref.dtype)
    masks = head_mask(2 * HD)
    half = lax.broadcasted_iota(jnp.int32, (L, 2 * HD), 1) < HD
    pairs = wide // (2 * HD)
    scale = HD ** (-0.5)
    qkv_ref, p_ref = qkv(), p()

    for s in range(seqs):
        at = slice(s * L, (s + 1) * L)
        for pair in range(pairs):
            lo = pair * 2 * HD
            q = qkv_ref[at, lo : lo + 2 * HD]
            k = qkv_ref[at, wide + lo : wide + lo + 2 * HD]
            v = qkv_ref[at, 2 * wide + lo : 2 * wide + lo + 2 * HD]
            go = gm_ref[at, lo : lo + 2 * HD]
            prob = p_ref[s * pairs + pair]
            dv = dot(prob.astype(BF), go, NN)
            dp = dot(doubled(v, masks), go, NT)
            lows = []
            for h in range(2):
                ph = prob[h * L : (h + 1) * L]
                dh = dp[h * L : (h + 1) * L]
                delta = jnp.sum(ph * dh, axis=0, keepdims=True)
                lows.append((ph * (dh - delta)).astype(BF))
            ds = jnp.concatenate(lows, axis=0)
            dk = dot(ds, q, NN)
            dq = dot(ds, doubled(k, masks), TN) * scale
            dj_ref[at, lo : lo + 2 * HD] = dq.astype(BF)
            dj_ref[at, wide + lo : wide + lo + 2 * HD] = (
                jnp.where(half, dk[:L], dk[L:]) * scale
            ).astype(BF)
            dj_ref[at, 2 * wide + lo : 2 * wide + lo + 2 * HD] = jnp.where(
                half, dv[:L], dv[L:]
            ).astype(BF)

    dj = dj_ref[...]
    grads = dot(dj, x()[...], TN)
    for k in range(3):
        lo = k * wide
        da.ref[k * w : (k + 1) * w, :] = grads[lo : lo + w].astype(da.ref.dtype)
        db.ref[k * w : (k + 1) * w, :] = grads[lo + w : lo + wide].astype(db.ref.dtype)
    db.put()
    da.put()
    bsum_ref[...] = jnp.zeros_like(bsum_ref)
    bsum_ref[0:1, :] = jnp.sum(dj[:, :wide].astype(F32), axis=0, keepdims=True)
    bsum_ref[1:2, :] = jnp.sum(dj[:, 2 * wide :].astype(F32), axis=0, keepdims=True)
    return dj, joined([q() for q in weights], w)


def attn_bwd_far_body(ins, res, extra):
    j, g, *pieces, mix, qkv, p, x = ins
    db, da, bsum, acc = res
    _, _, gm_ref, dj_ref = extra
    weights, outs = far_weights(pieces)
    dj, big = attn_bwd_core(
        x, g()[...], weights, outs, qkv, p, mix, da, db, bsum.ref, gm_ref, dj_ref
    )
    for at, lo, n in blocks_of(dj.shape[0]):
        acc.ref[at, :] = dot(dj[at, :], big, NN)
        acc.put(lo, n)


def attn_bwd_near_body(ins, res, extra):
    t, g, oa, ob, mix, qkv, p, x, qa, qb, far, g_full, sums2, sums1, b0, b1, b2, b3, far_bsum, steps = ins
    db, da, gt, pack = res
    gm_ref, dj_ref, bsum_ref = extra
    bsum = Loaded(bsum_ref)
    gl = g()[...]
    dj, big = attn_bwd_core(
        x, gl, (qa, qb), (oa, ob), qkv, p, mix, da, db, bsum.ref, gm_ref, dj_ref
    )
    far_ref, full_ref = far(), g_full()
    for at, lo, n in blocks_of(gl.shape[0]):
        gt.ref[at, :] = dot(dj[at, :], big, NN) + far_ref[at, :] + full_ref[at, :]
        gt.put(lo, n)
    pack_ref = pack.ref
    pack_ref[...] = jnp.zeros_like(pack_ref)
    pack_ref[0:3, :] = sums2()[0:3, :]
    pack_ref[3:6, :] = sums1()[0:3, :]
    wide = far_bsum.ref.shape[1]
    for r, bias in enumerate((b0, b1, b2, b3)):
        at = t()[0] ^ r
        pack_ref[pl.ds(8 + at, 1), :] = bias()[...]
        sums = (bsum_ref if r < 2 else far_bsum())[...]
        if r % 2:
            sums = pltpu.roll(sums, wide - wide // 2, 1)
        for k in range(2):
            pack_ref[pl.ds(12 + 4 * k + at, 1), :wide] = sums[k : k + 1, :]
    for s in range(gl.shape[0] // L):
        pack_ref[24 + s : 25 + s, :] = jnp.sum(gt.ref[s * L : (s + 1) * L, :], axis=0, keepdims=True)
    pack_ref[31:32, :] = steps()[...]


def halves_at(bit, n):
    keep = pl.multiple_of(bit * n, n)
    send = pl.multiple_of((1 - bit) * n, n)
    return pl.ds(keep, n), pl.ds(send, n)


def cut(refs, bit, keep, send, scale=1):
    n = keep.ref.shape[0]
    for at, out in zip(halves_at(bit, n), (keep, send)):
        total = refs[0][at, :].astype(F32)
        for ref in refs[1:]:
            total = total + ref[at, :].astype(F32)
        out.ref[...] = total.astype(out.ref.dtype)
        out.put()


def pair_sum(one, two, at, out):
    out.ref[...] = (one[at, :].astype(F32) + two[at, :].astype(F32)).astype(out.ref.dtype)


def glue_first_body(ins, res, extra):
    bits, dd, dd2, du, du2 = ins
    d_keep, d_send, u_keep, u_send = res
    cut((dd(), dd2()), bits()[0], d_keep, d_send)
    d_send.put()
    cut((du(), du2()), bits()[1], u_keep, u_send)


def glue_far_body(ins, res, extra):
    bits, df, df_x, uf, uf_z = ins
    df_send, uf_send, uf_keep = res
    pair_sum(df(), df_x(), slice(0, df.ref.shape[0]), df_send)
    df_send.put()
    cut((uf(), uf_z()), bits()[0], uf_keep, uf_send)


def glue_second_body(ins, res, extra):
    bits, dn, dn2, un, un2 = ins
    dn_keep, dn_send, un_keep, un_send = res
    cut((dn(), dn2()), bits()[0], dn_keep, dn_send)
    cut((un(), un2()), bits()[1], un_keep, un_send)


def glue_near_body(ins, res, extra):
    bits, dn, dn_x, df_y, un, un_z, uf, uf_x = ins
    dn_keep, dn_send, un_keep, un_send, uf_sum = res
    cut((dn(), dn_x(), df_y()), bits()[1], dn_keep, dn_send)
    cut((un(), un_z()), bits()[0], un_keep, un_send)
    pair_sum(uf(), uf_x(), slice(0, uf.ref.shape[0]), uf_sum)


def glue_third_body(ins, res, extra):
    bits, da, da2 = ins
    n = res[0].ref.shape[0]
    for k, out in enumerate(res):
        pair_sum(da(), da2(), slice(k * n, (k + 1) * n), out)
        out.put()


def glue_fourth_body(ins, res, extra):
    bits, dn, dn_z, un, un_x, uf_y = ins
    keep, send = res
    n = keep.ref.shape[0] // 2
    cut((dn(), dn_z()), bits()[2], PartOf(keep, 0, n), PartOf(send, 0, n))
    cut((un(), un_x(), uf_y()), bits()[2], PartOf(keep, n, n), PartOf(send, n, n))


def quarter_of(bits, m):
    return (bits[0] ^ (m & 1)) * 2 + (bits[1] ^ (m >> 1))


def glue_fifth_body(which):
    def body(ins, res, extra):
        bits, da, da2, far = ins
        n = res[0].ref.shape[0]
        a, b, far_ref = da(), da2(), far()
        for m in (1, 2, 3, 0):
            out = res[m]
            at = quarter_of(bits(), m)
            rows = pl.ds(pl.multiple_of(which * 4 * n + at * n, n), n)
            part = pl.ds(pl.multiple_of(at * n, n), n)
            total = a[rows, :] + b[rows, :].astype(F32) + far_ref[part, :].astype(F32)
            out.ref[...] = total.astype(out.ref.dtype)
            out.put()

    return body


def join_body(ins, res, extra):
    bits, d_own, d_x, u_own, u_z, *quarters = ins
    d_out, u_out, q_out, o_out = res
    n = d_own.ref.shape[0]
    for own, other, out, bit in ((d_own, d_x, d_out, 0), (u_own, u_z, u_out, 1)):
        for item, at in zip((own, other), halves_at(bits()[bit], n)):
            out.ref[at, :] = item()[...].astype(F32)
        out.put()
    n = quarters[0].ref.shape[0]
    for m, item in enumerate(quarters):
        at = quarter_of(bits(), m)
        half = n // 2
        ref = item()
        q_out.ref[pl.ds(pl.multiple_of(at * half, half), half), :] = ref[:half, :].astype(F32)
        value = ref[half:, :].astype(F32)

        @pl.when(at < 2)
        def _():
            q_out.ref[pl.ds(pl.multiple_of(4 * half + at * half, half), half), :] = value

        @pl.when(at >= 2)
        def _():
            o_out.ref[pl.ds(pl.multiple_of((at - 2) * half, half), half), :] = value


def last_body(ins, res, extra):
    t, feats, inner, ibias, outer, grad, small = ins
    g_inner, g_ibias, g_outer, g_obias, *vectors, own_bup, own_q, own_v = res
    outer_w = outer()[...].astype(F32)
    pre = exact(feats()[...], inner()[...].astype(F32), NN) + vector(ibias)
    gate = 1.0 / (1.0 + jnp.exp(-pre))
    g = grad()[...]
    g_outer.ref[...] = exact(pre * gate, g, TN)
    g_outer.put()
    g_obias.ref[...] = jnp.sum(g, axis=0)
    hidden = exact(g, outer_w, NT) * (gate * (1.0 + pre * (1.0 - gate)))
    g_inner.ref[...] = exact(feats()[...], hidden, TN)
    g_ibias.ref[...] = jnp.sum(hidden, axis=0)
    small_ref = small()
    for i, out in enumerate(vectors):
        out.ref[...] = small_ref[i, :]
    own_bup.ref[...] = small_ref[pl.ds(8 + t()[0], 1), :].reshape(own_bup.ref.shape)
    for k, out in enumerate((own_q, own_v)):
        out.ref[...] = small_ref[pl.ds(12 + 4 * k + t()[0], 1), :]


def time_features(timesteps, width):
    half = width // 2
    frequency = jnp.exp(-math.log(10000.0) * jnp.arange(half, dtype=F32) / half)
    angles = timesteps.astype(F32)[:, None] * frequency[None, :]
    return jnp.concatenate([jnp.cos(angles), jnp.sin(angles)], axis=1)


def swap(value, axis, size, bit):
    return lax.ppermute(value, axis, [(i, i ^ bit) for i in range(size)])


def tie(value, *others):
    return lax.optimization_barrier((value,) + others)[0]


def halves(bit_set, mine, other):
    low = jnp.where(bit_set, other, mine)
    high = jnp.where(bit_set, mine, other)
    return low, high


def tie(value, *others):
    return lax.optimization_barrier((value,) + others)[0]


def sync(*values):
    return lax.optimization_barrier(values)


def local(dp, tensor, *args):
    (
        tokens, timesteps, lengths, time_inner, time_ibias, time_outer, time_obias, qkv_weight,
        qv_bias, out_weight, out_bias, gain_first, shift_first, up_weight, up_bias, down_weight,
        down_bias, gain_second, shift_second, cotangent,
    ) = args
    rows, width = tokens.shape
    seqs = rows // L
    w = qkv_weight.shape[2]
    hid = up_weight.shape[0]
    t = lax.axis_index("tensor")
    d = lax.axis_index("dp")
    high = list(range(3, dp.bit_length() - 1))
    core = lambda v: swap(v, "tensor", tensor, 1)
    across = lambda v: swap(v, "tensor", tensor, 2)

    j0 = (d & 1) == 1
    j1 = ((d >> 1) & 1) == 1
    own_j = (d & 3)[None]
    own_bits = jnp.stack([d & 1, (d >> 1) & 1, (d >> 2) & 1])
    flat_qkv = jnp.transpose(qkv_weight, (1, 2, 0)).reshape(3 * w, width)
    part_a = [flat_qkv[:w], flat_qkv[w : 2 * w], flat_qkv[2 * w :], out_weight]
    h2 = hid // 2
    part_f = [up_weight[:h2], up_weight[h2:], down_weight[:h2], down_weight[h2:]]

    def pick(parts, j0, j1):
        return jnp.where(j1, jnp.where(j0, parts[3], parts[2]), jnp.where(j0, parts[1], parts[0]))

    def spread(got):
        return [swap(got, "dp", dp, m) for m in (1, 2)]

    a_y = across(pick(part_a, j0, j1))
    qkv_core, out_core = core(flat_qkv), core(out_weight)
    bias = jnp.concatenate(
        [
            jnp.pad(qv_bias, ((0, 0), (0, width - w))),
            jnp.pad(up_bias[None], ((0, 13), (0, 0))),
        ],
        axis=0,
    )
    bias_core, bias_y = core(bias), across(bias)

    features = time_features(timesteps, time_inner.shape[0])
    hidden_time = jax.nn.silu(
        exact(features, time_inner.astype(F32), NN) + time_ibias.astype(F32)
    )
    temb = exact(hidden_time, time_outer.astype(F32), NN) + time_obias.astype(F32)
    temb = jnp.pad(temb, ((0, 8 - seqs), (0, 0))) if seqs < 8 else temb
    own_len = lax.dynamic_slice(lengths, (t * seqs,), (seqs,))

    a_y2 = across(pick(part_a, ~j0, ~j1))
    a_others = spread(a_y)
    send_f, a_y2, temb, bias_y, bias_core = sync(
        pick(part_f, j0, j1), a_y2, temb, bias_y, bias_core
    )
    a_others.append(a_y2)
    bias_y2 = core(bias_y)
    f_y = across(send_f)
    wide = 2 * w
    pairs = wide // (2 * HD)
    act_shapes = [
        sds((rows, 3 * wide), BF),
        sds((seqs * pairs, 2 * L, L), F32),
        sds((rows, wide), BF),
    ]
    full = sds((rows, width), F32)
    low_full = sds((rows, width), BF)
    attn_flops = 2 * rows * width * 4 * wide + 4 * rows * L * wide
    x, qkv_n, p_n, mix_n, acc_n = call(
        attn_near_body, [low_full] + act_shapes + [full],
        (own_len, tokens, temb, flat_qkv, qkv_core, bias, bias_core, out_weight, out_core),
        attn_flops, smem=(0,),
    )
    acc_n, bias_y2, f_y, *far_a1 = sync(acc_n, bias_y2, f_y, a_y, *a_others)
    far_a2 = [core(v) for v in far_a1]
    send_f, f_y, acc_n, up_own, down_own, *far_a2 = sync(
        pick(part_f, ~j0, ~j1), f_y, acc_n, up_weight, down_weight, *far_a2
    )
    f_others = spread(f_y)
    f_others.append(across(send_f))
    up_core, down_core = core(up_own), core(down_own)
    wt = pltpu.VMEM((4 * w, width), BF)
    qkv_f, p_f, mix_f, first, normed = call(
        attn_far_body, act_shapes + [full, low_full],
        (
            own_len, own_j, x, *far_a1, *far_a2, bias_y, bias_y2, acc_n,
            tokens, temb, out_bias, gain_first, shift_first,
        ),
        attn_flops, smem=(0, 1), scratch=[wt, wt], place=far_places(1, 3, 0),
    )
    normed, up_core, down_core, *far_f1 = sync(normed, up_core, down_core, f_y, *f_others)
    far_f2 = [core(v) for v in far_f1]
    up_core, down_core = up_core, down_core
    mlp_flops = 2 * rows * width * 4 * hid
    (mlp_n,) = call(
        mlp_near_body, [full],
        (normed, up_weight, up_core, down_weight, down_core, bias, bias_core), mlp_flops,
    )
    mlp_n, *far_f2 = sync(mlp_n, *far_f2)
    mat = pltpu.VMEM((2 * hid, width), BF)
    dw_far = sds((hid, width), BF)
    dw_own = sds((hid, width), F32)
    bsum = sds((1, hid), F32)
    dws = [dw_far, dw_far, dw_own, dw_own, bsum, bsum]
    sums_shape = sds((8, width), F32)
    duf2, ddf2, duf, ddf, bup_f2, bup_f, layer_out, g2_low, sums2, g2 = call(
        mlp_far_body, dws + [low_full, low_full, sums_shape, full],
        (
            own_j, normed, *far_f1, *far_f2, bias_y, bias_y2, mlp_n,
            first, cotangent, gain_first, shift_first, down_bias, gain_second, shift_second,
        ),
        3 * mlp_flops, smem=(0,),
        scratch=[
            mat, mat, mat, mat, pltpu.VMEM((rows, 2 * hid), BF), pltpu.VMEM((rows, 2 * hid), F32),
            pltpu.VMEM((rows, width), F32),
        ],
        place=far_places(0, 2, 0),
    )
    f32 = lambda v: v.astype(F32)

    part = lambda k, dtype: sds((hid // k, width), dtype)

    def glue(body, outs, args):
        return call(body, outs, (own_bits,) + args, 1, smem=(0,), limit=LOW)

    df_keep, df_send, uf_keep, uf_send = glue(
        glue_first_body, [part(2, F32), part(2, BF), part(2, F32), part(2, BF)],
        (ddf, core(ddf2), duf, core(duf2)),
    )
    g2_low, df_keep, df_send, uf_keep, uf_send = sync(g2_low, df_keep, df_send, uf_keep, uf_send)
    along = lambda v, m: swap(v, "dp", dp, m)
    df_x = along(df_send, 1)
    uf_z = along(uf_send, 2)
    dun2, ddn2, dun, ddn, bup_n2, bup_n, g1, g1_low, sums1 = call(
        mlp_bwd_near_body, dws + [full, low_full, sums_shape],
        (
            normed, up_weight, up_core, g2_low, down_weight, down_core, g2, first, gain_first, bias,
            bias_core,
        ),
        2 * mlp_flops, limit=LOW, place={**near_places(1, 0), **near_places(4, 1)},
        scratch=[mat, mat, pltpu.VMEM((rows, 2 * hid), BF), pltpu.VMEM((rows, 2 * hid), F32)],
    )
    dun2, ddn2, df_x, uf_z = sync(dun2, ddn2, df_x, uf_z)
    near2 = core(ddn2), core(dun2)
    df_send, uf_send, uf_keep = glue(
        glue_far_body, [part(2, BF), part(4, BF), part(4, F32)], (df_keep, df_x, uf_keep, uf_z)
    )
    dn_keep, dn_send, un_keep, un_send = glue(
        glue_second_body, [part(2, F32), part(2, BF)] * 2, (ddn, near2[0], dun, near2[1])
    )
    g1_low, dn_keep, dn_send, un_keep, un_send, df_send, uf_keep, uf_send = sync(
        g1_low, dn_keep, dn_send, un_keep, un_send, df_send, uf_keep, uf_send
    )
    dn_x, uf_x = along(dn_send, 1), along(uf_send, 1)
    un_z = along(un_send, 2)
    df_y = across(df_send)
    da_shapes = [sds((4 * w, width), BF), sds((4 * w, width), F32), sds((8, wide), F32)]
    bwd_scratch = [pltpu.VMEM((rows, wide), BF), pltpu.VMEM((rows, 3 * wide), BF)]
    daf2, daf, qvb_f, gin_f = call(
        attn_bwd_far_body, da_shapes + [full],
        (own_j, g1_low, *far_a1, *far_a2, mix_f, qkv_f, p_f, x), 2 * attn_flops, limit=LOW,
        smem=(0,), scratch=[wt, wt] + bwd_scratch, place=far_places(0, 2, 0),
    )
    daf2, gin_f, dn_x, uf_x, un_z, df_y = sync(daf2, gin_f, dn_x, uf_x, un_z, df_y)
    qpart = lambda k, dtype: sds((4 * w // k, width), dtype)
    far_a2nd = core(daf2)
    dn_keep, dn_send, un_keep, un_send, uf_sum = glue(
        glue_near_body, [part(4, F32), part(4, BF)] * 2 + [part(4, BF)],
        (dn_keep, dn_x, df_y, un_keep, un_z, uf_keep, uf_x),
    )
    a_lo, a_hi = glue(glue_third_body, [qpart(2, BF)] * 2, (daf, far_a2nd))
    g1_low, a_lo, a_hi, dn_keep, dn_send, un_keep, un_send, uf_sum = sync(
        g1_low, a_lo, a_hi, dn_keep, dn_send, un_keep, un_send, uf_sum
    )
    a_lo = across(a_lo)
    uf_y = across(uf_sum)
    a_hi = across(a_hi)
    dn_z = along(dn_send, 2)
    un_x = along(un_send, 1)
    steps_row = jnp.pad(timesteps.astype(F32), (0, width - seqs))[None, :]
    dan2, dan, grad_tokens, pack = call(
        attn_bwd_near_body, da_shapes[:2] + [full, sds((32, width), F32)],
        (
            t[None], g1_low, out_weight, out_core, mix_n, qkv_n, p_n, x, flat_qkv, qkv_core, gin_f, g1,
            sums2, sums1, bup_n, bup_n2, bup_f, bup_f2, qvb_f, steps_row,
        ),
        2 * attn_flops, limit=LOW, smem=(0,), scratch=bwd_scratch + [pltpu.VMEM((8, wide), F32)],
    )
    dan2, pack, a_lo, uf_y, dn_z, un_x = sync(dan2, pack, a_lo, uf_y, dn_z, un_x)

    cat = lambda *v: jnp.concatenate(v, axis=0)
    near_a2, pack_c = core(dan2), core(pack)
    du_keep, du_send = glue(
        glue_fourth_body, [part(4, F32), part(4, BF)], (dn_keep, dn_z, un_keep, un_x, uf_y)
    )

    def halve(value, which):
        n = value.shape[0] // 2
        at = jnp.where(((d >> which) & 1) == 1, n, 0)
        keep = lax.dynamic_slice_in_dim(value, at, n, 0)
        return keep, lax.dynamic_slice_in_dim(value, n - at, n, 0).astype(BF)

    def high_sum(value):
        for which in high:
            keep, send = halve(value, which)
            value = keep + f32(along(send, 1 << which))
        return value

    def join_bit(value, which, other=None):
        other = along(value, 1 << which) if other is None else other
        return cat(*halves(((d >> which) & 1) == 1, value, other))

    def high_join(value):
        for which in high[::-1]:
            value = join_bit(value, which)
        return value

    two = lambda f, v: cat(f(v[: v.shape[0] // 2]), f(v[v.shape[0] // 2 :]))
    du_z = along(du_send, 4)
    cut_half = lambda which, far: glue(
        glue_fifth_body(which), [qpart(8, F32)] + [qpart(8, BF)] * 3, (dan, near_a2, far)
    )
    pack, pack_c = sync(pack, pack_c)
    state = [pack[:24] + pack_c[:24], cat(*halves((t & 1) == 1, pack[24:], pack_c[24:]))]

    def small_hop(which):
        small, gath = state
        other = along(cat(small, gath), 1 << which)
        state[:] = [small + other[:24], join_bit(gath, which, other[24:])]

    small_hop(2)
    q_lo = cut_half(0, a_lo)
    got_lo = [along(q_lo[m], m) for m in (1, 2, 3)]
    near_a2, a_hi, du_z, *state[:] = sync(near_a2, a_hi, du_z, *state)

    du = two(high_sum, du_keep + f32(du_z))
    du = two(high_join, du.astype(BF))
    du_z = along(du, 4)
    q_hi = cut_half(1, a_hi)
    got_hi = [along(q_hi[m], m) for m in (1, 2, 3)]
    small_hop(0)
    du, du_z, *rest = sync(du, du_z, *state, *got_hi, *got_lo)
    state[:], got_hi, got_lo = rest[:2], rest[2:5], rest[5:]

    a_sum = cat(
        q_lo[0] + sum(f32(v) for v in got_lo), q_hi[0] + sum(f32(v) for v in got_hi)
    ).astype(BF)
    a_z = along(a_sum, 4)
    n = du.shape[0] // 2
    d_own, u_own = join_bit(du[:n], 2, du_z[:n]), join_bit(du[n:], 2, du_z[n:])
    d_z, u_x = along(d_own, 2), along(u_own, 1)
    small_hop(1)
    a_sum, a_z, d_own, u_own, d_z, u_x, *state[:] = sync(
        a_sum, a_z, d_own, u_own, d_z, u_x, *state
    )
    a_end = (f32(a_sum) + f32(a_z)).astype(BF)
    for which in high:
        a_end = (f32(a_end) + f32(along(a_end, 1 << which))).astype(BF)
        small_hop(which)
    d_own, u_own = join_bit(d_own, 1, d_z), join_bit(u_own, 0, u_x)
    d_x, u_z = along(d_own, 1), along(u_own, 2)
    other = across(cat(*state))
    state[:] = [state[0] + other[:24], cat(*halves((t & 2) == 2, state[1], other[24:]))]
    a_got = [along(a_end, m) for m in (1, 2, 3)]

    small, gath = state
    gath = gath.reshape(dp, tensor, 8, width)
    feats = time_features(gath[:, :, 7, :seqs].reshape(-1), time_inner.shape[0])
    line = sds((width,), F32)
    row = sds((1, width), F32)
    (
        grad_tinner, grad_tibias, grad_touter, grad_tobias, gsecond, ssecond, bdown, gfirst, sfirst,
        bout, own_bup, own_q, own_v,
    ) = call(
        last_body,
        [sds(time_inner.shape, F32), sds(time_ibias.shape, F32), sds(time_outer.shape, F32)]
        + [line] * 8 + [row] * 2,
        (
            t[None], feats, time_inner, time_ibias, time_outer,
            gath[:, :, :seqs].reshape(-1, width), small,
        ),
        1, smem=(0,), window=8, limit=LOW,
    )
    a_end, d_x, u_z, grad_touter, *a_got = sync(a_end, d_x, u_z, grad_touter, *a_got)
    d_all, u_all, q_all, o_all = call(
        join_body, [part(1, F32)] * 2 + [sds((3 * w, width), F32), sds((w, width), F32)],
        (own_bits, d_own, d_x, u_own, u_z, a_end, *a_got), 1, smem=(0,), window=16,
    )

    grad_qkv = jnp.transpose(q_all.reshape(3, w, width), (2, 0, 1))
    return (
        layer_out,
        grad_tokens,
        grad_tinner,
        grad_tibias,
        grad_touter,
        grad_tobias,
        grad_qkv,
        jnp.concatenate([own_q[:, :w], own_v[:, :w]], axis=0),
        o_all,
        bout,
        gfirst,
        sfirst,
        u_all,
        own_bup,
        d_all,
        bdown,
        gsecond,
        ssecond,
    )


def solution(mesh):
    both = ("dp", "tensor")
    placed = (
        P(both, None), P(both), P("dp"), P(), P(), P(), P(), P(None, None, "tensor"),
        P(None, "tensor"), P("tensor", None), P(), P(), P(), P("tensor", None), P("tensor"),
        P("tensor", None), P(), P(), P(), P(both, None),
    )
    return jax.shard_map(
        functools.partial(local, mesh.shape["dp"], mesh.shape["tensor"]),
        mesh=mesh,
        in_specs=placed,
        out_specs=(
            P(both, None), P(both, None), P(), P(), P(), P(), P(None, None, "tensor"),
            P(None, "tensor"), P("tensor", None), P(), P(), P(), P("tensor", None), P("tensor"),
            P("tensor", None), P(), P(), P(),
        ),
        check_vma=False,
    )
```

```python
import functools
import math

import jax
import jax.numpy as jnp
from jax import lax
from jax.experimental import pallas as pl
from jax.experimental.pallas import tpu as pltpu
from jax.sharding import PartitionSpec as P

L = 128
HD = 64
EPS = 1e-05
F32 = jnp.float32
BF = jnp.bfloat16
NN = ((1,), (0,))
NT = ((1,), (1,))
TN = ((0,), (0,))
LOW = 63
BIG = 64 * 1024
CHUNKS = 8


def dot(left, right, dims):
    return lax.dot_general(left, right, (dims, ((), ())), preferred_element_type=F32)


def exact(left, right, dims):
    return lax.dot_general(
        left, right, (dims, ((), ())), precision=lax.Precision.HIGHEST, preferred_element_type=F32
    )


class Loaded:
    def __init__(self, ref, copies=(), queue=None):
        self.ref, self.copies, self.queue = ref, list(copies), queue

    def __call__(self):
        if self.copies:
            while self.queue[0] and self not in self.queue[1]:
                advance(self.queue)
            for copy in self.copies:
                copy.wait()
            self.copies = []
            advance(self.queue)
        return self.ref


def advance(queue):
    if queue[0]:
        item = queue[0].pop(0)
        for copy in item.copies:
            copy.start()
        queue[1].append(item)


class Stored:
    def __init__(self, ref, dst=None, sems=None):
        self.ref, self.dst, self.sems = ref, dst, sems
        self.copies, self.whole = [], False

    def put(self, lo=None, n=None):
        if self.dst is None or self.whole:
            return
        self.whole = lo is None
        src, dst = self.ref, self.dst
        if lo is not None:
            src, dst = src.at[pl.ds(lo, n)], dst.at[pl.ds(lo, n)]
        copy = pltpu.make_async_copy(src, dst, self.sems[len(self.copies)])
        copy.start()
        self.copies.append(copy)

    def finish(self):
        if not self.copies:
            self.put()
        for copy in self.copies:
            copy.wait()


class PartOf:
    def __init__(self, out, lo, n):
        self.out, self.lo, self.n = out, lo, n
        self.ref = out.ref.at[pl.ds(lo, n), :]

    def put(self):
        self.out.put(self.lo, self.n)


def call(body, outs, args, flops, scratch=(), smem=(), place=None, window=4, limit=63):
    place = place or {}
    size = lambda v: math.prod(v.shape) * v.dtype.itemsize
    moved = sum(size(v) for v in list(outs) + list(args))
    big_in = [i for i, v in enumerate(args) if i not in smem and size(v) >= BIG]
    held = [i for i in big_in if i not in place]
    big_out = [i for i, v in enumerate(outs) if size(v) >= BIG]
    n_in, n_out = len(args), len(outs)
    def kernel(*refs):
        ins = [Loaded(r) for r in refs[:n_in]]
        res = [Stored(r) for r in refs[n_in : n_in + n_out]]
        rest = refs[n_in + n_out :]
        held_in, rest = rest[: len(held)], rest[len(held) :]
        held_out, rest = rest[: len(big_out)], rest[len(big_out) :]
        extra, (sem_in, sem_out) = rest[:-2], rest[-2:]
        queue = ([], [])
        sem = 0
        for i in big_in:
            if i in place:
                dst, pairs = place[i](refs, extra)
            else:
                dst = held_in[held.index(i)]
                pairs = [(refs[i], dst)]
            copies = []
            for one, two in pairs:
                copies.append(pltpu.make_async_copy(one, two, sem_in.at[sem]))
                sem += 1
            ins[i] = Loaded(dst, copies, queue)
            queue[0].append(ins[i])
        for _ in range(window):
            advance(queue)
        for k, i in enumerate(big_out):
            sems = [sem_out.at[k * CHUNKS + c] for c in range(CHUNKS)]
            res[i] = Stored(held_out[k], refs[n_in + i], sems)
        body(ins, res, extra)
        for item in ins:
            item()
        for item in res:
            item.finish()

    def spec(i, big):
        if i in big:
            return pl.BlockSpec(memory_space=pl.ANY)
        return pl.BlockSpec(memory_space=pltpu.VMEM)

    return pl.pallas_call(
        kernel,
        out_shape=outs,
        in_specs=[
            pl.BlockSpec(memory_space=pltpu.SMEM) if i in smem else spec(i, big_in)
            for i in range(n_in)
        ],
        out_specs=[spec(i, big_out) for i in range(n_out)],
        scratch_shapes=[pltpu.VMEM(args[i].shape, args[i].dtype) for i in held]
        + [pltpu.VMEM(outs[i].shape, outs[i].dtype) for i in big_out]
        + list(scratch)
        + [pltpu.SemaphoreType.DMA((len(big_in) + 3 * len(place) + 1,)), pltpu.SemaphoreType.DMA((max(1, len(big_out)) * CHUNKS,))],
        cost_estimate=pl.CostEstimate(flops=int(flops), bytes_accessed=int(moved), transcendentals=0),
        compiler_params=pltpu.CompilerParams(vmem_limit_bytes=limit * 1024 * 1024),
    )(*args)


def sds(shape, dtype):
    return jax.ShapeDtypeStruct(shape, dtype)


def head_mask(width):
    lane = lax.broadcasted_iota(jnp.int32, (1, width), 1)
    first = jnp.where(lane < width // 2, 1.0, 0.0)
    return first.astype(BF), (1.0 - first).astype(BF)


def doubled(pair, masks):
    return jnp.concatenate([pair * masks[0], pair * masks[1]], axis=0)


def far_places(j_at, first, scratch):
    def place_of(s, k):
        def pairs(refs, extra):
            dst = extra[scratch + s]
            n = dst.shape[0] // 4
            row = pl.multiple_of((refs[j_at][0] ^ k) * n, n)
            return dst, [(refs[first + 4 * s + k], dst.at[pl.ds(row, n), :])]

        return pairs

    return {first + 4 * s + k: place_of(s, k) for s in range(2) for k in range(4)}


class Whole:
    def __init__(self, parts, ref=None):
        self.parts, self.ref = parts, parts[0].ref if ref is None else ref

    def __call__(self):
        for part in self.parts:
            part()
        return self.ref


class Rows:
    def __init__(self, item, lo, n):
        self.item, self.ref = item, item.ref.at[pl.ds(lo, n), :]

    def __call__(self):
        self.item()
        return self.ref


def side_by_side(a_ref, b_ref, row, w):
    a = a_ref[...].astype(F32)
    b = b_ref[...].astype(F32)
    return (a + pltpu.roll(b, w, 1))[row : row + 1, : 2 * w]


def joined(weights, w):
    return jnp.concatenate([q[k * w : (k + 1) * w, :] for k in range(3) for q in weights], axis=0)


def attn_fwd_core(x, weights, outs, biases, len_ref, qkv_ref, p_ref, mix_ref, stored):
    w = outs[0].ref.shape[0]
    rows = x.shape[0]
    seqs = rows // L
    wide = 2 * w
    total = dot(x, joined([q() for q in weights], w), NT)
    qkv_ref[:, :wide] = (total[:, :wide] + side_by_side(*biases, 0, w)).astype(BF)
    qkv_ref[:, wide : 2 * wide] = total[:, wide : 2 * wide].astype(BF)
    qkv_ref[:, 2 * wide :] = (total[:, 2 * wide :] + side_by_side(*biases, 1, w)).astype(BF)
    stored[0].put()
    masks = head_mask(2 * HD)
    key_at = lax.broadcasted_iota(jnp.int32, (L, L), 0)
    pairs = wide // (2 * HD)
    for s in range(seqs):
        at = slice(s * L, (s + 1) * L)
        valid = key_at < len_ref[s]
        for pair in range(pairs):
            lo = pair * 2 * HD
            q = qkv_ref[at, lo : lo + 2 * HD]
            k = qkv_ref[at, wide + lo : wide + lo + 2 * HD]
            v = qkv_ref[at, 2 * wide + lo : 2 * wide + lo + 2 * HD]
            scores = dot(doubled(k, masks), q, NT) * HD ** (-0.5)
            lows = []
            for h in range(2):
                part = jnp.where(valid, scores[h * L : (h + 1) * L], -1e30)
                expo = jnp.exp(part - jnp.max(part, axis=0, keepdims=True))
                prob = expo * (1.0 / jnp.sum(expo, axis=0, keepdims=True))
                p_ref[s * pairs + pair, h * L : (h + 1) * L, :] = prob
                lows.append(prob.astype(BF))
            mixed = dot(jnp.concatenate(lows, axis=0), doubled(v, masks), TN)
            mix_ref[at, lo : lo + 2 * HD] = mixed.astype(BF)
        stored[1].put(s * pairs, pairs)
    stored[2].put()
    return jnp.concatenate([o()[...] for o in outs], axis=0)


def start_of(tok_ref, temb_ref):
    rows, width = tok_ref.shape
    seqs = rows // L
    return [
        tok_ref[s * L : (s + 1) * L, :].astype(F32) + temb_ref[s : s + 1, :] for s in range(seqs)
    ]


def blocks_of(rows):
    n = rows // 3 if rows % (3 * L) == 0 else rows
    return [(slice(lo, lo + n), lo, n) for lo in range(0, rows, n)]


def attn_near_body(ins, res, extra):
    len_r, tok, temb, qa, qb, ba, bb, oa, ob = ins
    x, qkv, p, mix, acc = res
    for s, rows in enumerate(start_of(tok(), temb())):
        x.ref[s * L : (s + 1) * L, :] = rows.astype(BF)
    x.put()
    out = attn_fwd_core(
        x.ref[...], (qa, qb), (oa, ob), (ba(), bb()), len_r(), qkv.ref, p.ref, mix.ref, (qkv, p, mix)
    )
    for at, lo, n in blocks_of(mix.ref.shape[0]):
        acc.ref[at, :] = dot(mix.ref[at, :], out, NN)
        acc.put(lo, n)


def far_weights(pieces):
    both = (Whole(pieces[:4]), Whole(pieces[4:]))
    w = both[0].ref.shape[0] // 4
    return both, tuple(Rows(f, 3 * w, w) for f in both)


def row_mean(value):
    return jnp.mean(value, axis=-1, keepdims=True)


def unit_of(value):
    centred = value - row_mean(value)
    rate = lax.rsqrt(row_mean(centred * centred) + EPS)
    return centred * rate, rate


def attn_far_body(ins, res, extra):
    len_r, j, x, *pieces, ba, bb, near, tok, temb, ob_v, g_v, s_v = ins
    qkv, p, mix, first_o, low = res
    weights, outs = far_weights(pieces)
    out = attn_fwd_core(
        x()[...], weights, outs, (ba(), bb()), len_r(), qkv.ref, p.ref, mix.ref, (qkv, p, mix)
    )
    out_bias, gain, shift = (vector(v) for v in (ob_v, g_v, s_v))
    first_ref = first_o.ref
    near_ref, starts = near(), start_of(tok(), temb())
    for rows, lo, n in blocks_of(mix.ref.shape[0]):
        first_ref[rows, :] = dot(mix.ref[rows, :], out, NN) + near_ref[rows, :] + out_bias
        for s in range(lo // L, (lo + n) // L):
            at = slice(s * L, (s + 1) * L)
            first = first_ref[at, :] + starts[s]
            first_ref[at, :] = first
            unit, _ = unit_of(first)
            low.ref[at, :] = (unit * gain + shift).astype(BF)
        first_o.put(lo, n)
        low.put(lo, n)


def vector(item):
    return item()[...].astype(F32).reshape(1, -1)


def gelu_pair(pre):
    cdf = 0.5 * (1.0 + lax.erf(pre * 0.7071067811865476))
    pdf = jnp.exp(-0.5 * pre * pre) * 0.3989422804014327
    return pre * cdf, cdf + pre * pdf


def mlp_fwd_core(x_ref, ups, downs, biases, act_ref, slope_ref, acc_ref, done=None):
    rows = x_ref.shape[0]
    hid = ups[0].ref.shape[0]
    block = 256 if rows % 256 == 0 else rows
    for r in range(len(ups)):
        cols = slice(r * hid, (r + 1) * hid)
        up = ups[r]()[...]
        down = downs[r]() if downs is not None else None
        bias = biases[r].astype(F32)
        for m in range(rows // block):
            at = slice(m * block, (m + 1) * block)
            act, slope = gelu_pair(dot(x_ref[at, :], up, NT) + bias)
            low = act.astype(BF)
            if act_ref is not None:
                act_ref[at, cols] = low
                slope_ref[at, cols] = slope
            if acc_ref is None:
                continue
            part = dot(low, down[...], NN)
            if r == 0:
                acc_ref[at, :] = part
            else:
                acc_ref[at, :] += part
            if done is not None and r == len(ups) - 1:
                done(m * block, block)


def mlp_near_body(ins, res, extra):
    x, ua, ub, da, db, ba, bb = ins
    (acc,) = res
    mlp_fwd_core(
        x(), (ua, ub), (da, db), (ba()[2:3, :], bb()[2:3, :]), None, None, acc.ref, acc.put
    )


def mlp_far_body(ins, res, extra):
    j, x, *pieces, ba, bb, near, first, cot, g1_v, s1_v, b_v, g2_v, s2_v = ins
    fa, fb = Whole(pieces[:4]), Whole(pieces[4:])
    dub, ddb, dua, dda, bsb, bsa, out, low, sums, grad = res
    _, _, up_ref, down_ref, act_ref, slope_ref, acc_ref = extra
    hid = fa.ref.shape[0] // 2
    ups = tuple(Rows(f, 0, hid) for f in (fa, fb))
    downs = tuple(Rows(f, hid, hid) for f in (fa, fb))
    mlp_fwd_core(
        x(), ups, downs, (ba()[2:3, :], bb()[2:3, :]), act_ref, slope_ref, acc_ref
    )
    rows, width = x().shape
    first_ref, near_ref, cot_ref, sums_ref = first(), near(), cot(), sums.ref
    gain1, shift1, bias, gain, shift = [vector(v) for v in (g1_v, s1_v, b_v, g2_v, s2_v)]
    sums_ref[...] = jnp.zeros_like(sums_ref)
    for s in range(rows // L):
        at = slice(s * L, (s + 1) * L)
        unit1, _ = unit_of(first_ref[at, :])
        normed = unit1 * gain1 + shift1
        second = normed + acc_ref[at, :] + near_ref[at, :] + bias
        unit, rate = unit_of(second)
        out.ref[at, :] = (unit * gain + shift).astype(BF)
        grad_out = cot_ref[at, :].astype(F32)
        inner = grad_out * gain
        lower = rate * (inner - row_mean(inner) - unit * row_mean(inner * unit))
        grad.ref[at, :] = lower
        low.ref[at, :] = lower.astype(BF)
        sums_ref[0:1, :] += jnp.sum(grad_out * unit, axis=0, keepdims=True)
        sums_ref[1:2, :] += jnp.sum(grad_out, axis=0, keepdims=True)
        sums_ref[2:3, :] += jnp.sum(lower, axis=0, keepdims=True)
    out.put()
    low.put()
    for r in range(2):
        at = slice(r * hid, (r + 1) * hid)
        up_ref[at, :] = ups[r]()[...]
        down_ref[at, :] = downs[r]()[...]
    gp, up = mlp_bwd_core(
        x, low.ref, lambda: up_ref, lambda: down_ref, lambda: act_ref, lambda: slope_ref,
        (dua, dub), (dda, ddb), (bsa, bsb),
    )
    for at, lo, n in blocks_of(rows):
        grad.ref[at, :] += dot(gp[at], up, NN)
        grad.put(lo, n)


def mlp_bwd_core(x, gl_ref, up, down, act, slope, dus, dds, bsums):
    hid = dus[0].ref.shape[0]
    total = dot(act()[...], gl_ref[...], TN)
    for r in (1, 0):
        dds[r].ref[...] = total[r * hid : (r + 1) * hid].astype(dds[r].ref.dtype)
        dds[r].put()
    gp = (dot(gl_ref[...], down()[...], NT) * slope()[...]).astype(BF)
    total = dot(gp, x()[...], TN)
    for r in (1, 0):
        dus[r].ref[...] = total[r * hid : (r + 1) * hid].astype(dus[r].ref.dtype)
        dus[r].put()
    sums = jnp.sum(gp.astype(F32), axis=0, keepdims=True)
    for r in range(2):
        bsums[r].ref[...] = sums[:, r * hid : (r + 1) * hid]
    return gp, up()[...]


def mlp_bwd_near_body(ins, res, extra):
    x, ua, ub, low, da, db, prev, first, g_v, ba, bb = ins
    up_ref, down_ref, act_ref, slope_ref = extra
    dub, ddb, dua, dda, bsb, bsa, gf, gl, sums = res
    gf_ref, sums_ref = gf.ref, sums.ref
    mlp_fwd_core(
        x(), (ua, ub), None, (ba()[2:3, :], bb()[2:3, :]), act_ref, slope_ref, None
    )
    gp, up = mlp_bwd_core(
        x, low(), lambda: up_ref, Whole((da, db), down_ref), lambda: act_ref, lambda: slope_ref,
        (dua, dub), (dda, ddb), (bsa, bsb),
    )
    prev_ref, first_ref = prev(), first()
    gain = vector(g_v)
    sums_ref[...] = jnp.zeros_like(sums_ref)
    for rows, lo, n in blocks_of(x().shape[0]):
        block = dot(gp[rows], up, NN) + prev_ref[rows, :]
        for s in range(n // L):
            at = slice(lo + s * L, lo + (s + 1) * L)
            unit, rate = unit_of(first_ref[at, :])
            upper = block[s * L : (s + 1) * L]
            inner = upper * gain
            lower = rate * (inner - row_mean(inner) - unit * row_mean(inner * unit))
            gf_ref[at, :] = lower
            gl.ref[at, :] = lower.astype(BF)
            sums_ref[0:1, :] += jnp.sum(upper * unit, axis=0, keepdims=True)
            sums_ref[1:2, :] += jnp.sum(upper, axis=0, keepdims=True)
            sums_ref[2:3, :] += jnp.sum(lower, axis=0, keepdims=True)
        gl.put(lo, n)
        gf.put(lo, n)


def near_places(first, scratch):
    def place_of(s):
        def pairs(refs, extra):
            n = extra[scratch].shape[0] // 2
            dst = extra[scratch].at[pl.ds(s * n, n), :]
            return dst, [(refs[first + s], dst)]

        return pairs

    return {first + s: place_of(s) for s in range(2)}


def attn_bwd_core(x, gl, weights, outs, qkv, p, mix, da, db, bsum_ref, gm_ref, dj_ref):
    rows = gl.shape[0]
    seqs = rows // L
    w = outs[0].ref.shape[0]
    wide = 2 * w
    gm_ref[...] = dot(gl, jnp.concatenate([o()[...] for o in outs], axis=0), NT).astype(BF)
    dout = dot(mix()[...], gl, TN)
    da.ref[3 * w : 4 * w, :] = dout[:w].astype(da.ref.dtype)
    db.ref[3 * w : 4 * w, :] = dout[w:].astype(db.ref.dtype)
    masks = head_mask(2 * HD)
    half = lax.broadcasted_iota(jnp.int32, (L, 2 * HD), 1) < HD
    pairs = wide // (2 * HD)
    scale = HD ** (-0.5)
    qkv_ref, p_ref = qkv(), p()

    for s in range(seqs):
        at = slice(s * L, (s + 1) * L)
        for pair in range(pairs):
            lo = pair * 2 * HD
            q = qkv_ref[at, lo : lo + 2 * HD]
            k = qkv_ref[at, wide + lo : wide + lo + 2 * HD]
            v = qkv_ref[at, 2 * wide + lo : 2 * wide + lo + 2 * HD]
            go = gm_ref[at, lo : lo + 2 * HD]
            prob = p_ref[s * pairs + pair]
            dv = dot(prob.astype(BF), go, NN)
            dp = dot(doubled(v, masks), go, NT)
            lows = []
            for h in range(2):
                ph = prob[h * L : (h + 1) * L]
                dh = dp[h * L : (h + 1) * L]
                delta = jnp.sum(ph * dh, axis=0, keepdims=True)
                lows.append((ph * (dh - delta)).astype(BF))
            ds = jnp.concatenate(lows, axis=0)
            dk = dot(ds, q, NN)
            dq = dot(ds, doubled(k, masks), TN) * scale
            dj_ref[at, lo : lo + 2 * HD] = dq.astype(BF)
            dj_ref[at, wide + lo : wide + lo + 2 * HD] = (
                jnp.where(half, dk[:L], dk[L:]) * scale
            ).astype(BF)
            dj_ref[at, 2 * wide + lo : 2 * wide + lo + 2 * HD] = jnp.where(
                half, dv[:L], dv[L:]
            ).astype(BF)

    dj = dj_ref[...]
    grads = dot(dj, x()[...], TN)
    for k in range(3):
        lo = k * wide
        da.ref[k * w : (k + 1) * w, :] = grads[lo : lo + w].astype(da.ref.dtype)
        db.ref[k * w : (k + 1) * w, :] = grads[lo + w : lo + wide].astype(db.ref.dtype)
    db.put()
    da.put()
    bsum_ref[...] = jnp.zeros_like(bsum_ref)
    bsum_ref[0:1, :] = jnp.sum(dj[:, :wide].astype(F32), axis=0, keepdims=True)
    bsum_ref[1:2, :] = jnp.sum(dj[:, 2 * wide :].astype(F32), axis=0, keepdims=True)
    return dj, joined([q() for q in weights], w)


def attn_bwd_far_body(ins, res, extra):
    j, g, *pieces, mix, qkv, p, x = ins
    db, da, bsum, acc = res
    _, _, gm_ref, dj_ref = extra
    weights, outs = far_weights(pieces)
    dj, big = attn_bwd_core(
        x, g()[...], weights, outs, qkv, p, mix, da, db, bsum.ref, gm_ref, dj_ref
    )
    for at, lo, n in blocks_of(dj.shape[0]):
        acc.ref[at, :] = dot(dj[at, :], big, NN)
        acc.put(lo, n)


def attn_bwd_near_body(ins, res, extra):
    t, g, oa, ob, mix, qkv, p, x, qa, qb, far, g_full, sums2, sums1, b0, b1, b2, b3, far_bsum, steps = ins
    db, da, gt, pack = res
    gm_ref, dj_ref, bsum_ref = extra
    bsum = Loaded(bsum_ref)
    gl = g()[...]
    dj, big = attn_bwd_core(
        x, gl, (qa, qb), (oa, ob), qkv, p, mix, da, db, bsum.ref, gm_ref, dj_ref
    )
    far_ref, full_ref = far(), g_full()
    for at, lo, n in blocks_of(gl.shape[0]):
        gt.ref[at, :] = dot(dj[at, :], big, NN) + far_ref[at, :] + full_ref[at, :]
        gt.put(lo, n)
    pack_ref = pack.ref
    pack_ref[...] = jnp.zeros_like(pack_ref)
    pack_ref[0:3, :] = sums2()[0:3, :]
    pack_ref[3:6, :] = sums1()[0:3, :]
    wide = far_bsum.ref.shape[1]
    for r, bias in enumerate((b0, b1, b2, b3)):
        at = t()[0] ^ r
        pack_ref[pl.ds(8 + at, 1), :] = bias()[...]
        sums = (bsum_ref if r < 2 else far_bsum())[...]
        if r % 2:
            sums = pltpu.roll(sums, wide - wide // 2, 1)
        for k in range(2):
            pack_ref[pl.ds(12 + 4 * k + at, 1), :wide] = sums[k : k + 1, :]
    for s in range(gl.shape[0] // L):
        pack_ref[24 + s : 25 + s, :] = jnp.sum(gt.ref[s * L : (s + 1) * L, :], axis=0, keepdims=True)
    pack_ref[31:32, :] = steps()[...]


def halves_at(bit, n):
    keep = pl.multiple_of(bit * n, n)
    send = pl.multiple_of((1 - bit) * n, n)
    return pl.ds(keep, n), pl.ds(send, n)


def cut(refs, bit, keep, send, scale=1):
    n = keep.ref.shape[0]
    for at, out in zip(halves_at(bit, n), (keep, send)):
        total = refs[0][at, :].astype(F32)
        for ref in refs[1:]:
            total = total + ref[at, :].astype(F32)
        out.ref[...] = total.astype(out.ref.dtype)
        out.put()


def pair_sum(one, two, at, out):
    out.ref[...] = (one[at, :].astype(F32) + two[at, :].astype(F32)).astype(out.ref.dtype)


def glue_first_body(ins, res, extra):
    bits, dd, dd2, du, du2 = ins
    d_keep, d_send, u_keep, u_send = res
    cut((dd(), dd2()), bits()[0], d_keep, d_send)
    d_send.put()
    cut((du(), du2()), bits()[1], u_keep, u_send)


def glue_far_body(ins, res, extra):
    bits, df, df_x, uf, uf_z = ins
    df_send, uf_send, uf_keep = res
    pair_sum(df(), df_x(), slice(0, df.ref.shape[0]), df_send)
    df_send.put()
    cut((uf(), uf_z()), bits()[0], uf_keep, uf_send)


def glue_second_body(ins, res, extra):
    bits, dn, dn2, un, un2 = ins
    dn_keep, dn_send, un_keep, un_send = res
    cut((dn(), dn2()), bits()[0], dn_keep, dn_send)
    cut((un(), un2()), bits()[1], un_keep, un_send)


def glue_near_body(ins, res, extra):
    bits, dn, dn_x, df_y, un, un_z, uf, uf_x = ins
    dn_keep, dn_send, un_keep, un_send, uf_sum = res
    cut((dn(), dn_x(), df_y()), bits()[1], dn_keep, dn_send)
    cut((un(), un_z()), bits()[0], un_keep, un_send)
    pair_sum(uf(), uf_x(), slice(0, uf.ref.shape[0]), uf_sum)


def glue_third_body(ins, res, extra):
    bits, da, da2 = ins
    n = res[0].ref.shape[0]
    for k, out in enumerate(res):
        pair_sum(da(), da2(), slice(k * n, (k + 1) * n), out)
        out.put()


def glue_fourth_body(ins, res, extra):
    bits, dn, dn_z, un, un_x, uf_y = ins
    keep, send = res
    n = keep.ref.shape[0] // 2
    cut((dn(), dn_z()), bits()[2], PartOf(keep, 0, n), PartOf(send, 0, n))
    cut((un(), un_x(), uf_y()), bits()[2], PartOf(keep, n, n), PartOf(send, n, n))


def quarter_of(bits, m):
    return (bits[0] ^ (m & 1)) * 2 + (bits[1] ^ (m >> 1))


def glue_fifth_body(which):
    def body(ins, res, extra):
        bits, da, da2, far = ins
        n = res[0].ref.shape[0]
        a, b, far_ref = da(), da2(), far()
        for m in (1, 2, 3, 0):
            out = res[m]
            at = quarter_of(bits(), m)
            rows = pl.ds(pl.multiple_of(which * 4 * n + at * n, n), n)
            part = pl.ds(pl.multiple_of(at * n, n), n)
            total = a[rows, :] + b[rows, :].astype(F32) + far_ref[part, :].astype(F32)
            out.ref[...] = total.astype(out.ref.dtype)
            out.put()

    return body


def join_body(ins, res, extra):
    bits, d_own, d_x, u_own, u_z, *quarters = ins
    d_out, u_out, q_out, o_out = res
    n = d_own.ref.shape[0]
    for own, other, out, bit in ((d_own, d_x, d_out, 0), (u_own, u_z, u_out, 1)):
        for item, at in zip((own, other), halves_at(bits()[bit], n)):
            out.ref[at, :] = item()[...].astype(F32)
        out.put()
    n = quarters[0].ref.shape[0]
    for m, item in enumerate(quarters):
        at = quarter_of(bits(), m)
        half = n // 2
        ref = item()
        q_out.ref[pl.ds(pl.multiple_of(at * half, half), half), :] = ref[:half, :].astype(F32)
        value = ref[half:, :].astype(F32)

        @pl.when(at < 2)
        def _():
            q_out.ref[pl.ds(pl.multiple_of(4 * half + at * half, half), half), :] = value

        @pl.when(at >= 2)
        def _():
            o_out.ref[pl.ds(pl.multiple_of((at - 2) * half, half), half), :] = value


def last_body(ins, res, extra):
    t, feats, inner, ibias, outer, grad, small = ins
    g_inner, g_ibias, g_outer, g_obias, *vectors, own_bup, own_q, own_v = res
    outer_w = outer()[...].astype(F32)
    pre = exact(feats()[...], inner()[...].astype(F32), NN) + vector(ibias)
    gate = 1.0 / (1.0 + jnp.exp(-pre))
    g = grad()[...]
    g_outer.ref[...] = exact(pre * gate, g, TN)
    g_outer.put()
    g_obias.ref[...] = jnp.sum(g, axis=0)
    hidden = exact(g, outer_w, NT) * (gate * (1.0 + pre * (1.0 - gate)))
    g_inner.ref[...] = exact(feats()[...], hidden, TN)
    g_ibias.ref[...] = jnp.sum(hidden, axis=0)
    small_ref = small()
    for i, out in enumerate(vectors):
        out.ref[...] = small_ref[i, :]
    own_bup.ref[...] = small_ref[pl.ds(8 + t()[0], 1), :].reshape(own_bup.ref.shape)
    for k, out in enumerate((own_q, own_v)):
        out.ref[...] = small_ref[pl.ds(12 + 4 * k + t()[0], 1), :]


def time_features(timesteps, width):
    half = width // 2
    frequency = jnp.exp(-math.log(10000.0) * jnp.arange(half, dtype=F32) / half)
    angles = timesteps.astype(F32)[:, None] * frequency[None, :]
    return jnp.concatenate([jnp.cos(angles), jnp.sin(angles)], axis=1)


def swap(value, axis, size, bit):
    return lax.ppermute(value, axis, [(i, i ^ bit) for i in range(size)])


def tie(value, *others):
    return lax.optimization_barrier((value,) + others)[0]


def halves(bit_set, mine, other):
    low = jnp.where(bit_set, other, mine)
    high = jnp.where(bit_set, mine, other)
    return low, high


def tie(value, *others):
    return lax.optimization_barrier((value,) + others)[0]


def sync(*values):
    return lax.optimization_barrier(values)


def local(dp, tensor, *args):
    (
        tokens, timesteps, lengths, time_inner, time_ibias, time_outer, time_obias, qkv_weight,
        qv_bias, out_weight, out_bias, gain_first, shift_first, up_weight, up_bias, down_weight,
        down_bias, gain_second, shift_second, cotangent,
    ) = args
    rows, width = tokens.shape
    seqs = rows // L
    w = qkv_weight.shape[2]
    hid = up_weight.shape[0]
    t = lax.axis_index("tensor")
    d = lax.axis_index("dp")
    high = list(range(3, dp.bit_length() - 1))
    core = lambda v: swap(v, "tensor", tensor, 1)
    across = lambda v: swap(v, "tensor", tensor, 2)

    j0 = (d & 1) == 1
    j1 = ((d >> 1) & 1) == 1
    own_j = (d & 3)[None]
    own_bits = jnp.stack([d & 1, (d >> 1) & 1, (d >> 2) & 1])
    flat_qkv = jnp.transpose(qkv_weight, (1, 2, 0)).reshape(3 * w, width)
    part_a = [flat_qkv[:w], flat_qkv[w : 2 * w], flat_qkv[2 * w :], out_weight]
    h2 = hid // 2
    part_f = [up_weight[:h2], up_weight[h2:], down_weight[:h2], down_weight[h2:]]

    def pick(parts, j0, j1):
        return jnp.where(j1, jnp.where(j0, parts[3], parts[2]), jnp.where(j0, parts[1], parts[0]))

    def spread(got):
        return [swap(got, "dp", dp, m) for m in (1, 2)]

    a_y = across(pick(part_a, j0, j1))
    qkv_core, out_core = core(flat_qkv), core(out_weight)
    bias = jnp.concatenate(
        [
            jnp.pad(qv_bias, ((0, 0), (0, width - w))),
            jnp.pad(up_bias[None], ((0, 13), (0, 0))),
        ],
        axis=0,
    )
    bias_core, bias_y = core(bias), across(bias)

    features = time_features(timesteps, time_inner.shape[0])
    hidden_time = jax.nn.silu(
        exact(features, time_inner.astype(F32), NN) + time_ibias.astype(F32)
    )
    temb = exact(hidden_time, time_outer.astype(F32), NN) + time_obias.astype(F32)
    temb = jnp.pad(temb, ((0, 8 - seqs), (0, 0))) if seqs < 8 else temb
    own_len = lax.dynamic_slice(lengths, (t * seqs,), (seqs,))

    a_y2 = across(pick(part_a, ~j0, ~j1))
    a_others = spread(a_y)
    send_f, a_y2, temb, bias_y, bias_core = sync(
        pick(part_f, j0, j1), a_y2, temb, bias_y, bias_core
    )
    a_others.append(a_y2)
    bias_y2 = core(bias_y)
    f_y = across(send_f)
    wide = 2 * w
    pairs = wide // (2 * HD)
    act_shapes = [
        sds((rows, 3 * wide), BF),
        sds((seqs * pairs, 2 * L, L), F32),
        sds((rows, wide), BF),
    ]
    full = sds((rows, width), F32)
    low_full = sds((rows, width), BF)
    attn_flops = 2 * rows * width * 4 * wide + 4 * rows * L * wide
    x, qkv_n, p_n, mix_n, acc_n = call(
        attn_near_body, [low_full] + act_shapes + [full],
        (own_len, tokens, temb, flat_qkv, qkv_core, bias, bias_core, out_weight, out_core),
        attn_flops, smem=(0,),
    )
    acc_n, bias_y2, f_y, *far_a1 = sync(acc_n, bias_y2, f_y, a_y, *a_others)
    far_a2 = [core(v) for v in far_a1]
    send_f, f_y, acc_n, up_own, down_own, *far_a2 = sync(
        pick(part_f, ~j0, ~j1), f_y, acc_n, up_weight, down_weight, *far_a2
    )
    f_others = spread(f_y)
    f_others.append(across(send_f))
    up_core, down_core = core(up_own), core(down_own)
    wt = pltpu.VMEM((4 * w, width), BF)
    qkv_f, p_f, mix_f, first, normed = call(
        attn_far_body, act_shapes + [full, low_full],
        (
            own_len, own_j, x, *far_a1, *far_a2, bias_y, bias_y2, acc_n,
            tokens, temb, out_bias, gain_first, shift_first,
        ),
        attn_flops, smem=(0, 1), scratch=[wt, wt], place=far_places(1, 3, 0),
    )
    normed, up_core, down_core, *far_f1 = sync(normed, up_core, down_core, f_y, *f_others)
    far_f2 = [core(v) for v in far_f1]
    up_core, down_core = up_core, down_core
    mlp_flops = 2 * rows * width * 4 * hid
    (mlp_n,) = call(
        mlp_near_body, [full],
        (normed, up_weight, up_core, down_weight, down_core, bias, bias_core), mlp_flops,
    )
    mlp_n, *far_f2 = sync(mlp_n, *far_f2)
    mat = pltpu.VMEM((2 * hid, width), BF)
    dw_far = sds((hid, width), BF)
    dw_own = sds((hid, width), F32)
    bsum = sds((1, hid), F32)
    dws = [dw_far, dw_far, dw_own, dw_own, bsum, bsum]
    sums_shape = sds((8, width), F32)
    duf2, ddf2, duf, ddf, bup_f2, bup_f, layer_out, g2_low, sums2, g2 = call(
        mlp_far_body, dws + [low_full, low_full, sums_shape, full],
        (
            own_j, normed, *far_f1, *far_f2, bias_y, bias_y2, mlp_n,
            first, cotangent, gain_first, shift_first, down_bias, gain_second, shift_second,
        ),
        3 * mlp_flops, smem=(0,),
        scratch=[
            mat, mat, mat, mat, pltpu.VMEM((rows, 2 * hid), BF), pltpu.VMEM((rows, 2 * hid), F32),
            pltpu.VMEM((rows, width), F32),
        ],
        place=far_places(0, 2, 0),
    )
    f32 = lambda v: v.astype(F32)

    part = lambda k, dtype: sds((hid // k, width), dtype)

    def glue(body, outs, args):
        return call(body, outs, (own_bits,) + args, 1, smem=(0,), limit=LOW, window=8)

    df_keep, df_send, uf_keep, uf_send = glue(
        glue_first_body, [part(2, F32), part(2, BF), part(2, F32), part(2, BF)],
        (ddf, core(ddf2), duf, core(duf2)),
    )
    g2_low, df_keep, df_send, uf_keep, uf_send = sync(g2_low, df_keep, df_send, uf_keep, uf_send)
    along = lambda v, m: swap(v, "dp", dp, m)
    df_x = along(df_send, 1)
    uf_z = along(uf_send, 2)
    dun2, ddn2, dun, ddn, bup_n2, bup_n, g1, g1_low, sums1 = call(
        mlp_bwd_near_body, dws + [full, low_full, sums_shape],
        (
            normed, up_weight, up_core, g2_low, down_weight, down_core, g2, first, gain_first, bias,
            bias_core,
        ),
        2 * mlp_flops, limit=LOW, place={**near_places(1, 0), **near_places(4, 1)},
        scratch=[mat, mat, pltpu.VMEM((rows, 2 * hid), BF), pltpu.VMEM((rows, 2 * hid), F32)],
    )
    dun2, ddn2, df_x, uf_z = sync(dun2, ddn2, df_x, uf_z)
    near2 = core(ddn2), core(dun2)
    df_send, uf_send, uf_keep = glue(
        glue_far_body, [part(2, BF), part(4, BF), part(4, F32)], (df_keep, df_x, uf_keep, uf_z)
    )
    dn_keep, dn_send, un_keep, un_send = glue(
        glue_second_body, [part(2, F32), part(2, BF)] * 2, (ddn, near2[0], dun, near2[1])
    )
    g1_low, dn_keep, dn_send, un_keep, un_send, df_send, uf_keep, uf_send = sync(
        g1_low, dn_keep, dn_send, un_keep, un_send, df_send, uf_keep, uf_send
    )
    dn_x, uf_x = along(dn_send, 1), along(uf_send, 1)
    un_z = along(un_send, 2)
    df_y = across(df_send)
    da_shapes = [sds((4 * w, width), BF), sds((4 * w, width), F32), sds((8, wide), F32)]
    bwd_scratch = [pltpu.VMEM((rows, wide), BF), pltpu.VMEM((rows, 3 * wide), BF)]
    daf2, daf, qvb_f, gin_f = call(
        attn_bwd_far_body, da_shapes + [full],
        (own_j, g1_low, *far_a1, *far_a2, mix_f, qkv_f, p_f, x), 2 * attn_flops, limit=LOW,
        smem=(0,), scratch=[wt, wt] + bwd_scratch, place=far_places(0, 2, 0),
    )
    daf2, gin_f, dn_x, uf_x, un_z, df_y = sync(daf2, gin_f, dn_x, uf_x, un_z, df_y)
    qpart = lambda k, dtype: sds((4 * w // k, width), dtype)
    far_a2nd = core(daf2)
    dn_keep, dn_send, un_keep, un_send, uf_sum = glue(
        glue_near_body, [part(4, F32), part(4, BF)] * 2 + [part(4, BF)],
        (dn_keep, dn_x, df_y, un_keep, un_z, uf_keep, uf_x),
    )
    a_lo, a_hi = glue(glue_third_body, [qpart(2, BF)] * 2, (daf, far_a2nd))
    g1_low, a_lo, a_hi, dn_keep, dn_send, un_keep, un_send, uf_sum = sync(
        g1_low, a_lo, a_hi, dn_keep, dn_send, un_keep, un_send, uf_sum
    )
    a_lo = across(a_lo)
    uf_y = across(uf_sum)
    a_hi = across(a_hi)
    dn_z = along(dn_send, 2)
    un_x = along(un_send, 1)
    steps_row = jnp.pad(timesteps.astype(F32), (0, width - seqs))[None, :]
    dan2, dan, grad_tokens, pack = call(
        attn_bwd_near_body, da_shapes[:2] + [full, sds((32, width), F32)],
        (
            t[None], g1_low, out_weight, out_core, mix_n, qkv_n, p_n, x, flat_qkv, qkv_core, gin_f, g1,
            sums2, sums1, bup_n, bup_n2, bup_f, bup_f2, qvb_f, steps_row,
        ),
        2 * attn_flops, limit=LOW, smem=(0,), scratch=bwd_scratch + [pltpu.VMEM((8, wide), F32)],
    )
    dan2, pack, a_lo, uf_y, dn_z, un_x = sync(dan2, pack, a_lo, uf_y, dn_z, un_x)

    cat = lambda *v: jnp.concatenate(v, axis=0)
    near_a2, pack_c = core(dan2), core(pack)
    du_keep, du_send = glue(
        glue_fourth_body, [part(4, F32), part(4, BF)], (dn_keep, dn_z, un_keep, un_x, uf_y)
    )

    def halve(value, which):
        n = value.shape[0] // 2
        at = jnp.where(((d >> which) & 1) == 1, n, 0)
        keep = lax.dynamic_slice_in_dim(value, at, n, 0)
        return keep, lax.dynamic_slice_in_dim(value, n - at, n, 0).astype(BF)

    def high_sum(value):
        for which in high:
            keep, send = halve(value, which)
            value = keep + f32(along(send, 1 << which))
        return value

    def join_bit(value, which, other=None):
        other = along(value, 1 << which) if other is None else other
        return cat(*halves(((d >> which) & 1) == 1, value, other))

    def high_join(value):
        for which in high[::-1]:
            value = join_bit(value, which)
        return value

    two = lambda f, v: cat(f(v[: v.shape[0] // 2]), f(v[v.shape[0] // 2 :]))
    du_z = along(du_send, 4)
    cut_half = lambda which, far: glue(
        glue_fifth_body(which), [qpart(8, F32)] + [qpart(8, BF)] * 3, (dan, near_a2, far)
    )
    pack, pack_c = sync(pack, pack_c)
    state = [pack[:24] + pack_c[:24], cat(*halves((t & 1) == 1, pack[24:], pack_c[24:]))]

    def small_hop(which):
        small, gath = state
        other = along(cat(small, gath), 1 << which)
        state[:] = [small + other[:24], join_bit(gath, which, other[24:])]

    small_hop(2)
    q_lo = cut_half(0, a_lo)
    got_lo = [along(q_lo[m], m) for m in (1, 2, 3)]
    near_a2, a_hi, *rest = sync(near_a2, a_hi, *state, *got_lo)
    state[:], got_lo = rest[:2], rest[2:]

    du = two(high_sum, du_keep + f32(du_z))
    du = two(high_join, du.astype(BF))
    du_z = along(du, 4)
    q_hi = cut_half(1, a_hi)
    got_hi = [along(q_hi[m], m) for m in (1, 2, 3)]
    small_hop(1)
    du, du_z, *rest = sync(du, du_z, *state, *got_hi)
    state[:], got_hi = rest[:2], rest[2:]

    a_sum = cat(
        q_lo[0] + sum(f32(v) for v in got_lo), q_hi[0] + sum(f32(v) for v in got_hi)
    ).astype(BF)
    a_z = along(a_sum, 4)
    n = du.shape[0] // 2
    d_own, u_own = join_bit(du[:n], 2, du_z[:n]), join_bit(du[n:], 2, du_z[n:])
    d_z, u_x = along(d_own, 2), along(u_own, 1)
    small_hop(0)
    a_sum, a_z, d_own, u_own, d_z, u_x, *state[:] = sync(
        a_sum, a_z, d_own, u_own, d_z, u_x, *state
    )
    a_end = (f32(a_sum) + f32(a_z)).astype(BF)
    for which in high:
        a_end = (f32(a_end) + f32(along(a_end, 1 << which))).astype(BF)
        small_hop(which)
    d_own, u_own = join_bit(d_own, 1, d_z), join_bit(u_own, 0, u_x)
    d_x, u_z = along(d_own, 1), along(u_own, 2)
    other = across(cat(*state))
    state[:] = [state[0] + other[:24], cat(*halves((t & 2) == 2, state[1], other[24:]))]
    a_got = [along(a_end, m) for m in (1, 2, 3)]

    small, gath = state
    gath = gath.reshape(dp, tensor, 8, width)
    feats = time_features(gath[:, :, 7, :seqs].reshape(-1), time_inner.shape[0])
    line = sds((width,), F32)
    row = sds((1, width), F32)
    (
        grad_tinner, grad_tibias, grad_touter, grad_tobias, gsecond, ssecond, bdown, gfirst, sfirst,
        bout, own_bup, own_q, own_v,
    ) = call(
        last_body,
        [sds(time_inner.shape, F32), sds(time_ibias.shape, F32), sds(time_outer.shape, F32)]
        + [line] * 8 + [row] * 2,
        (
            t[None], feats, time_inner, time_ibias, time_outer,
            gath[:, :, :seqs].reshape(-1, width), small,
        ),
        1, smem=(0,), window=8, limit=LOW,
    )
    a_end, d_x, u_z, grad_touter, *a_got = sync(a_end, d_x, u_z, grad_touter, *a_got)
    d_all, u_all, q_all, o_all = call(
        join_body, [part(1, F32)] * 2 + [sds((3 * w, width), F32), sds((w, width), F32)],
        (own_bits, d_own, d_x, u_own, u_z, a_end, *a_got), 1, smem=(0,), window=16,
    )

    grad_qkv = jnp.transpose(q_all.reshape(3, w, width), (2, 0, 1))
    return (
        layer_out,
        grad_tokens,
        grad_tinner,
        grad_tibias,
        grad_touter,
        grad_tobias,
        grad_qkv,
        jnp.concatenate([own_q[:, :w], own_v[:, :w]], axis=0),
        o_all,
        bout,
        gfirst,
        sfirst,
        u_all,
        own_bup,
        d_all,
        bdown,
        gsecond,
        ssecond,
    )


def solution(mesh):
    both = ("dp", "tensor")
    placed = (
        P(both, None), P(both), P("dp"), P(), P(), P(), P(), P(None, None, "tensor"),
        P(None, "tensor"), P("tensor", None), P(), P(), P(), P("tensor", None), P("tensor"),
        P("tensor", None), P(), P(), P(), P(both, None),
    )
    return jax.shard_map(
        functools.partial(local, mesh.shape["dp"], mesh.shape["tensor"]),
        mesh=mesh,
        in_specs=placed,
        out_specs=(
            P(both, None), P(both, None), P(), P(), P(), P(), P(None, None, "tensor"),
            P(None, "tensor"), P("tensor", None), P(), P(), P(), P("tensor", None), P("tensor"),
            P("tensor", None), P(), P(), P(),
        ),
        check_vma=False,
    )
```

```python
import functools
import math

import jax
import jax.numpy as jnp
from jax import lax
from jax.experimental import pallas as pl
from jax.experimental.pallas import tpu as pltpu
from jax.sharding import PartitionSpec as P

L = 128
HD = 64
EPS = 1e-05
F32 = jnp.float32
BF = jnp.bfloat16
NN = ((1,), (0,))
NT = ((1,), (1,))
TN = ((0,), (0,))
LOW = 63
BIG = 64 * 1024
CHUNKS = 8


def dot(left, right, dims):
    return lax.dot_general(left, right, (dims, ((), ())), preferred_element_type=F32)


def exact(left, right, dims):
    return lax.dot_general(
        left, right, (dims, ((), ())), precision=lax.Precision.HIGHEST, preferred_element_type=F32
    )


class Loaded:
    def __init__(self, ref, copies=(), queue=None):
        self.ref, self.copies, self.queue = ref, list(copies), queue

    def __call__(self):
        if self.copies:
            while self.queue[0] and self not in self.queue[1]:
                advance(self.queue)
            for copy in self.copies:
                copy.wait()
            self.copies = []
            advance(self.queue)
        return self.ref


def advance(queue):
    if queue[0]:
        item = queue[0].pop(0)
        for copy in item.copies:
            copy.start()
        queue[1].append(item)


class Stored:
    def __init__(self, ref, dst=None, sems=None):
        self.ref, self.dst, self.sems = ref, dst, sems
        self.copies, self.whole = [], False

    def put(self, lo=None, n=None):
        if self.dst is None or self.whole:
            return
        self.whole = lo is None
        src, dst = self.ref, self.dst
        if lo is not None:
            src, dst = src.at[pl.ds(lo, n)], dst.at[pl.ds(lo, n)]
        copy = pltpu.make_async_copy(src, dst, self.sems[len(self.copies)])
        copy.start()
        self.copies.append(copy)

    def finish(self):
        if not self.copies:
            self.put()
        for copy in self.copies:
            copy.wait()


class PartOf:
    def __init__(self, out, lo, n):
        self.out, self.lo, self.n = out, lo, n
        self.ref = out.ref.at[pl.ds(lo, n), :]

    def put(self):
        self.out.put(self.lo, self.n)


def call(body, outs, args, flops, scratch=(), smem=(), place=None, window=6, limit=63):
    place = place or {}
    size = lambda v: math.prod(v.shape) * v.dtype.itemsize
    moved = sum(size(v) for v in list(outs) + list(args))
    big_in = [i for i, v in enumerate(args) if i not in smem and size(v) >= BIG]
    held = [i for i in big_in if i not in place]
    big_out = [i for i, v in enumerate(outs) if size(v) >= BIG]
    n_in, n_out = len(args), len(outs)
    def kernel(*refs):
        ins = [Loaded(r) for r in refs[:n_in]]
        res = [Stored(r) for r in refs[n_in : n_in + n_out]]
        rest = refs[n_in + n_out :]
        held_in, rest = rest[: len(held)], rest[len(held) :]
        held_out, rest = rest[: len(big_out)], rest[len(big_out) :]
        extra, (sem_in, sem_out) = rest[:-2], rest[-2:]
        queue = ([], [])
        sem = 0
        for i in big_in:
            if i in place:
                dst, pairs = place[i](refs, extra)
            else:
                dst = held_in[held.index(i)]
                pairs = [(refs[i], dst)]
            copies = []
            for one, two in pairs:
                copies.append(pltpu.make_async_copy(one, two, sem_in.at[sem]))
                sem += 1
            ins[i] = Loaded(dst, copies, queue)
            queue[0].append(ins[i])
        for _ in range(window):
            advance(queue)
        for k, i in enumerate(big_out):
            sems = [sem_out.at[k * CHUNKS + c] for c in range(CHUNKS)]
            res[i] = Stored(held_out[k], refs[n_in + i], sems)
        body(ins, res, extra)
        for item in ins:
            item()
        for item in res:
            item.finish()

    def spec(i, big):
        if i in big:
            return pl.BlockSpec(memory_space=pl.ANY)
        return pl.BlockSpec(memory_space=pltpu.VMEM)

    return pl.pallas_call(
        kernel,
        out_shape=outs,
        in_specs=[
            pl.BlockSpec(memory_space=pltpu.SMEM) if i in smem else spec(i, big_in)
            for i in range(n_in)
        ],
        out_specs=[spec(i, big_out) for i in range(n_out)],
        scratch_shapes=[pltpu.VMEM(args[i].shape, args[i].dtype) for i in held]
        + [pltpu.VMEM(outs[i].shape, outs[i].dtype) for i in big_out]
        + list(scratch)
        + [pltpu.SemaphoreType.DMA((len(big_in) + 3 * len(place) + 1,)), pltpu.SemaphoreType.DMA((max(1, len(big_out)) * CHUNKS,))],
        cost_estimate=pl.CostEstimate(flops=int(flops), bytes_accessed=int(moved), transcendentals=0),
        compiler_params=pltpu.CompilerParams(vmem_limit_bytes=limit * 1024 * 1024),
    )(*args)


def sds(shape, dtype):
    return jax.ShapeDtypeStruct(shape, dtype)


def head_mask(width):
    lane = lax.broadcasted_iota(jnp.int32, (1, width), 1)
    first = jnp.where(lane < width // 2, 1.0, 0.0)
    return first.astype(BF), (1.0 - first).astype(BF)


def doubled(pair, masks):
    return jnp.concatenate([pair * masks[0], pair * masks[1]], axis=0)


def far_places(j_at, first, scratch):
    def place_of(s, k):
        def pairs(refs, extra):
            dst = extra[scratch + s]
            n = dst.shape[0] // 4
            row = pl.multiple_of((refs[j_at][0] ^ k) * n, n)
            return dst, [(refs[first + 4 * s + k], dst.at[pl.ds(row, n), :])]

        return pairs

    return {first + 4 * s + k: place_of(s, k) for s in range(2) for k in range(4)}


class Whole:
    def __init__(self, parts, ref=None):
        self.parts, self.ref = parts, parts[0].ref if ref is None else ref

    def __call__(self):
        for part in self.parts:
            part()
        return self.ref


class Rows:
    def __init__(self, item, lo, n):
        self.item, self.ref = item, item.ref.at[pl.ds(lo, n), :]

    def __call__(self):
        self.item()
        return self.ref


def side_by_side(a_ref, b_ref, row, w):
    a = a_ref[...].astype(F32)
    b = b_ref[...].astype(F32)
    return (a + pltpu.roll(b, w, 1))[row : row + 1, : 2 * w]


def joined(weights, w):
    return jnp.concatenate([q[k * w : (k + 1) * w, :] for k in range(3) for q in weights], axis=0)


def attn_fwd_core(x, weights, outs, biases, len_ref, qkv_ref, p_ref, mix_ref, stored):
    w = outs[0].ref.shape[0]
    rows = x.shape[0]
    seqs = rows // L
    wide = 2 * w
    total = dot(x, joined([q() for q in weights], w), NT)
    qkv_ref[:, :wide] = (total[:, :wide] + side_by_side(*biases, 0, w)).astype(BF)
    qkv_ref[:, wide : 2 * wide] = total[:, wide : 2 * wide].astype(BF)
    qkv_ref[:, 2 * wide :] = (total[:, 2 * wide :] + side_by_side(*biases, 1, w)).astype(BF)
    stored[0].put()
    masks = head_mask(2 * HD)
    key_at = lax.broadcasted_iota(jnp.int32, (L, L), 0)
    pairs = wide // (2 * HD)
    for s in range(seqs):
        at = slice(s * L, (s + 1) * L)
        valid = key_at < len_ref[s]
        for pair in range(pairs):
            lo = pair * 2 * HD
            q = qkv_ref[at, lo : lo + 2 * HD]
            k = qkv_ref[at, wide + lo : wide + lo + 2 * HD]
            v = qkv_ref[at, 2 * wide + lo : 2 * wide + lo + 2 * HD]
            scores = dot(doubled(k, masks), q, NT) * HD ** (-0.5)
            lows = []
            for h in range(2):
                part = jnp.where(valid, scores[h * L : (h + 1) * L], -1e30)
                expo = jnp.exp(part - jnp.max(part, axis=0, keepdims=True))
                prob = expo * (1.0 / jnp.sum(expo, axis=0, keepdims=True))
                p_ref[s * pairs + pair, h * L : (h + 1) * L, :] = prob
                lows.append(prob.astype(BF))
            mixed = dot(jnp.concatenate(lows, axis=0), doubled(v, masks), TN)
            mix_ref[at, lo : lo + 2 * HD] = mixed.astype(BF)
        stored[1].put(s * pairs, pairs)
    stored[2].put()
    return jnp.concatenate([o()[...] for o in outs], axis=0)


def start_of(tok_ref, temb_ref):
    rows, width = tok_ref.shape
    seqs = rows // L
    return [
        tok_ref[s * L : (s + 1) * L, :].astype(F32) + temb_ref[s : s + 1, :] for s in range(seqs)
    ]


def blocks_of(rows):
    n = rows // 3 if rows % (3 * L) == 0 else rows
    return [(slice(lo, lo + n), lo, n) for lo in range(0, rows, n)]


def attn_near_body(ins, res, extra):
    len_r, tok, temb, qa, qb, ba, bb, oa, ob = ins
    x, qkv, p, mix, acc = res
    for s, rows in enumerate(start_of(tok(), temb())):
        x.ref[s * L : (s + 1) * L, :] = rows.astype(BF)
    x.put()
    out = attn_fwd_core(
        x.ref[...], (qa, qb), (oa, ob), (ba(), bb()), len_r(), qkv.ref, p.ref, mix.ref, (qkv, p, mix)
    )
    for at, lo, n in blocks_of(mix.ref.shape[0]):
        acc.ref[at, :] = dot(mix.ref[at, :], out, NN)
        acc.put(lo, n)


def far_weights(pieces):
    both = (Whole(pieces[:4]), Whole(pieces[4:]))
    w = both[0].ref.shape[0] // 4
    return both, tuple(Rows(f, 3 * w, w) for f in both)


def row_mean(value):
    return jnp.mean(value, axis=-1, keepdims=True)


def unit_of(value):
    centred = value - row_mean(value)
    rate = lax.rsqrt(row_mean(centred * centred) + EPS)
    return centred * rate, rate


def attn_far_body(ins, res, extra):
    len_r, j, x, *pieces, ba, bb, near, tok, temb, ob_v, g_v, s_v = ins
    qkv, p, mix, first_o, low = res
    weights, outs = far_weights(pieces)
    out = attn_fwd_core(
        x()[...], weights, outs, (ba(), bb()), len_r(), qkv.ref, p.ref, mix.ref, (qkv, p, mix)
    )
    out_bias, gain, shift = (vector(v) for v in (ob_v, g_v, s_v))
    first_ref = first_o.ref
    near_ref, starts = near(), start_of(tok(), temb())
    for rows, lo, n in blocks_of(mix.ref.shape[0]):
        first_ref[rows, :] = dot(mix.ref[rows, :], out, NN) + near_ref[rows, :] + out_bias
        for s in range(lo // L, (lo + n) // L):
            at = slice(s * L, (s + 1) * L)
            first = first_ref[at, :] + starts[s]
            first_ref[at, :] = first
            unit, _ = unit_of(first)
            low.ref[at, :] = (unit * gain + shift).astype(BF)
        first_o.put(lo, n)
        low.put(lo, n)


def vector(item):
    return item()[...].astype(F32).reshape(1, -1)


def gelu_pair(pre):
    cdf = 0.5 * (1.0 + lax.erf(pre * 0.7071067811865476))
    pdf = jnp.exp(-0.5 * pre * pre) * 0.3989422804014327
    return pre * cdf, cdf + pre * pdf


def mlp_fwd_core(x_ref, ups, downs, biases, act_ref, slope_ref, acc_ref, done=None):
    rows = x_ref.shape[0]
    hid = ups[0].ref.shape[0]
    block = 256 if rows % 256 == 0 else rows
    for r in range(len(ups)):
        cols = slice(r * hid, (r + 1) * hid)
        up = ups[r]()[...]
        down = downs[r]() if downs is not None else None
        bias = biases[r].astype(F32)
        for m in range(rows // block):
            at = slice(m * block, (m + 1) * block)
            act, slope = gelu_pair(dot(x_ref[at, :], up, NT) + bias)
            low = act.astype(BF)
            if act_ref is not None:
                act_ref[at, cols] = low
                slope_ref[at, cols] = slope
            if acc_ref is None:
                continue
            part = dot(low, down[...], NN)
            if r == 0:
                acc_ref[at, :] = part
            else:
                acc_ref[at, :] += part
            if done is not None and r == len(ups) - 1:
                done(m * block, block)


def mlp_near_body(ins, res, extra):
    x, ua, ub, da, db, ba, bb = ins
    (acc,) = res
    mlp_fwd_core(
        x(), (ua, ub), (da, db), (ba()[2:3, :], bb()[2:3, :]), None, None, acc.ref, acc.put
    )


def mlp_far_body(ins, res, extra):
    j, x, *pieces, ba, bb, near, first, cot, g1_v, s1_v, b_v, g2_v, s2_v = ins
    fa, fb = Whole(pieces[:4]), Whole(pieces[4:])
    dub, ddb, dua, dda, bsb, bsa, out, low, sums, grad = res
    _, _, up_ref, down_ref, act_ref, slope_ref, acc_ref = extra
    hid = fa.ref.shape[0] // 2
    ups = tuple(Rows(f, 0, hid) for f in (fa, fb))
    downs = tuple(Rows(f, hid, hid) for f in (fa, fb))
    mlp_fwd_core(
        x(), ups, downs, (ba()[2:3, :], bb()[2:3, :]), act_ref, slope_ref, acc_ref
    )
    rows, width = x().shape
    first_ref, near_ref, cot_ref, sums_ref = first(), near(), cot(), sums.ref
    gain1, shift1, bias, gain, shift = [vector(v) for v in (g1_v, s1_v, b_v, g2_v, s2_v)]
    sums_ref[...] = jnp.zeros_like(sums_ref)
    for s in range(rows // L):
        at = slice(s * L, (s + 1) * L)
        unit1, _ = unit_of(first_ref[at, :])
        normed = unit1 * gain1 + shift1
        second = normed + acc_ref[at, :] + near_ref[at, :] + bias
        unit, rate = unit_of(second)
        out.ref[at, :] = (unit * gain + shift).astype(BF)
        grad_out = cot_ref[at, :].astype(F32)
        inner = grad_out * gain
        lower = rate * (inner - row_mean(inner) - unit * row_mean(inner * unit))
        grad.ref[at, :] = lower
        low.ref[at, :] = lower.astype(BF)
        sums_ref[0:1, :] += jnp.sum(grad_out * unit, axis=0, keepdims=True)
        sums_ref[1:2, :] += jnp.sum(grad_out, axis=0, keepdims=True)
        sums_ref[2:3, :] += jnp.sum(lower, axis=0, keepdims=True)
    out.put()
    low.put()
    for r in range(2):
        at = slice(r * hid, (r + 1) * hid)
        up_ref[at, :] = ups[r]()[...]
        down_ref[at, :] = downs[r]()[...]
    gp, up = mlp_bwd_core(
        x, low.ref, lambda: up_ref, lambda: down_ref, lambda: act_ref, lambda: slope_ref,
        (dua, dub), (dda, ddb), (bsa, bsb),
    )
    for at, lo, n in blocks_of(rows):
        grad.ref[at, :] += dot(gp[at], up, NN)
        grad.put(lo, n)


def mlp_bwd_core(x, gl_ref, up, down, act, slope, dus, dds, bsums):
    hid = dus[0].ref.shape[0]
    total = dot(act()[...], gl_ref[...], TN)
    for r in (1, 0):
        dds[r].ref[...] = total[r * hid : (r + 1) * hid].astype(dds[r].ref.dtype)
        dds[r].put()
    gp = (dot(gl_ref[...], down()[...], NT) * slope()[...]).astype(BF)
    total = dot(gp, x()[...], TN)
    for r in (1, 0):
        dus[r].ref[...] = total[r * hid : (r + 1) * hid].astype(dus[r].ref.dtype)
        dus[r].put()
    sums = jnp.sum(gp.astype(F32), axis=0, keepdims=True)
    for r in range(2):
        bsums[r].ref[...] = sums[:, r * hid : (r + 1) * hid]
    return gp, up()[...]


def mlp_bwd_near_body(ins, res, extra):
    x, ua, ub, low, da, db, prev, first, g_v, ba, bb = ins
    up_ref, down_ref, act_ref, slope_ref = extra
    dub, ddb, dua, dda, bsb, bsa, gf, gl, sums = res
    gf_ref, sums_ref = gf.ref, sums.ref
    mlp_fwd_core(
        x(), (ua, ub), None, (ba()[2:3, :], bb()[2:3, :]), act_ref, slope_ref, None
    )
    gp, up = mlp_bwd_core(
        x, low(), lambda: up_ref, Whole((da, db), down_ref), lambda: act_ref, lambda: slope_ref,
        (dua, dub), (dda, ddb), (bsa, bsb),
    )
    prev_ref, first_ref = prev(), first()
    gain = vector(g_v)
    sums_ref[...] = jnp.zeros_like(sums_ref)
    for rows, lo, n in blocks_of(x().shape[0]):
        block = dot(gp[rows], up, NN) + prev_ref[rows, :]
        for s in range(n // L):
            at = slice(lo + s * L, lo + (s + 1) * L)
            unit, rate = unit_of(first_ref[at, :])
            upper = block[s * L : (s + 1) * L]
            inner = upper * gain
            lower = rate * (inner - row_mean(inner) - unit * row_mean(inner * unit))
            gf_ref[at, :] = lower
            gl.ref[at, :] = lower.astype(BF)
            sums_ref[0:1, :] += jnp.sum(upper * unit, axis=0, keepdims=True)
            sums_ref[1:2, :] += jnp.sum(upper, axis=0, keepdims=True)
            sums_ref[2:3, :] += jnp.sum(lower, axis=0, keepdims=True)
        gl.put(lo, n)
        gf.put(lo, n)


def near_places(first, scratch):
    def place_of(s):
        def pairs(refs, extra):
            n = extra[scratch].shape[0] // 2
            dst = extra[scratch].at[pl.ds(s * n, n), :]
            return dst, [(refs[first + s], dst)]

        return pairs

    return {first + s: place_of(s) for s in range(2)}


def attn_bwd_core(x, gl, weights, outs, qkv, p, mix, da, db, bsum_ref, gm_ref, dj_ref):
    rows = gl.shape[0]
    seqs = rows // L
    w = outs[0].ref.shape[0]
    wide = 2 * w
    gm_ref[...] = dot(gl, jnp.concatenate([o()[...] for o in outs], axis=0), NT).astype(BF)
    dout = dot(mix()[...], gl, TN)
    da.ref[3 * w : 4 * w, :] = dout[:w].astype(da.ref.dtype)
    db.ref[3 * w : 4 * w, :] = dout[w:].astype(db.ref.dtype)
    masks = head_mask(2 * HD)
    half = lax.broadcasted_iota(jnp.int32, (L, 2 * HD), 1) < HD
    pairs = wide // (2 * HD)
    scale = HD ** (-0.5)
    qkv_ref, p_ref = qkv(), p()

    for s in range(seqs):
        at = slice(s * L, (s + 1) * L)
        for pair in range(pairs):
            lo = pair * 2 * HD
            q = qkv_ref[at, lo : lo + 2 * HD]
            k = qkv_ref[at, wide + lo : wide + lo + 2 * HD]
            v = qkv_ref[at, 2 * wide + lo : 2 * wide + lo + 2 * HD]
            go = gm_ref[at, lo : lo + 2 * HD]
            prob = p_ref[s * pairs + pair]
            dv = dot(prob.astype(BF), go, NN)
            dp = dot(doubled(v, masks), go, NT)
            lows = []
            for h in range(2):
                ph = prob[h * L : (h + 1) * L]
                dh = dp[h * L : (h + 1) * L]
                delta = jnp.sum(ph * dh, axis=0, keepdims=True)
                lows.append((ph * (dh - delta)).astype(BF))
            ds = jnp.concatenate(lows, axis=0)
            dk = dot(ds, q, NN)
            dq = dot(ds, doubled(k, masks), TN) * scale
            dj_ref[at, lo : lo + 2 * HD] = dq.astype(BF)
            dj_ref[at, wide + lo : wide + lo + 2 * HD] = (
                jnp.where(half, dk[:L], dk[L:]) * scale
            ).astype(BF)
            dj_ref[at, 2 * wide + lo : 2 * wide + lo + 2 * HD] = jnp.where(
                half, dv[:L], dv[L:]
            ).astype(BF)

    dj = dj_ref[...]
    grads = dot(dj, x()[...], TN)
    for k in range(3):
        lo = k * wide
        da.ref[k * w : (k + 1) * w, :] = grads[lo : lo + w].astype(da.ref.dtype)
        db.ref[k * w : (k + 1) * w, :] = grads[lo + w : lo + wide].astype(db.ref.dtype)
    db.put()
    da.put()
    bsum_ref[...] = jnp.zeros_like(bsum_ref)
    bsum_ref[0:1, :] = jnp.sum(dj[:, :wide].astype(F32), axis=0, keepdims=True)
    bsum_ref[1:2, :] = jnp.sum(dj[:, 2 * wide :].astype(F32), axis=0, keepdims=True)
    return dj, joined([q() for q in weights], w)


def attn_bwd_far_body(ins, res, extra):
    j, g, *pieces, mix, qkv, p, x = ins
    db, da, bsum, acc = res
    _, _, gm_ref, dj_ref = extra
    weights, outs = far_weights(pieces)
    dj, big = attn_bwd_core(
        x, g()[...], weights, outs, qkv, p, mix, da, db, bsum.ref, gm_ref, dj_ref
    )
    for at, lo, n in blocks_of(dj.shape[0]):
        acc.ref[at, :] = dot(dj[at, :], big, NN)
        acc.put(lo, n)


def attn_bwd_near_body(ins, res, extra):
    t, g, oa, ob, mix, qkv, p, x, qa, qb, far, g_full, sums2, sums1, b0, b1, b2, b3, far_bsum, steps = ins
    db, da, gt, pack = res
    gm_ref, dj_ref, bsum_ref = extra
    bsum = Loaded(bsum_ref)
    gl = g()[...]
    dj, big = attn_bwd_core(
        x, gl, (qa, qb), (oa, ob), qkv, p, mix, da, db, bsum.ref, gm_ref, dj_ref
    )
    far_ref, full_ref = far(), g_full()
    for at, lo, n in blocks_of(gl.shape[0]):
        gt.ref[at, :] = dot(dj[at, :], big, NN) + far_ref[at, :] + full_ref[at, :]
        gt.put(lo, n)
    pack_ref = pack.ref
    pack_ref[...] = jnp.zeros_like(pack_ref)
    pack_ref[0:3, :] = sums2()[0:3, :]
    pack_ref[3:6, :] = sums1()[0:3, :]
    wide = far_bsum.ref.shape[1]
    for r, bias in enumerate((b0, b1, b2, b3)):
        at = t()[0] ^ r
        pack_ref[pl.ds(8 + at, 1), :] = bias()[...]
        sums = (bsum_ref if r < 2 else far_bsum())[...]
        if r % 2:
            sums = pltpu.roll(sums, wide - wide // 2, 1)
        for k in range(2):
            pack_ref[pl.ds(12 + 4 * k + at, 1), :wide] = sums[k : k + 1, :]
    for s in range(gl.shape[0] // L):
        pack_ref[24 + s : 25 + s, :] = jnp.sum(gt.ref[s * L : (s + 1) * L, :], axis=0, keepdims=True)
    pack_ref[31:32, :] = steps()[...]


def halves_at(bit, n):
    keep = pl.multiple_of(bit * n, n)
    send = pl.multiple_of((1 - bit) * n, n)
    return pl.ds(keep, n), pl.ds(send, n)


def cut(refs, bit, keep, send, scale=1):
    n = keep.ref.shape[0]
    for at, out in zip(halves_at(bit, n), (keep, send)):
        total = refs[0][at, :].astype(F32)
        for ref in refs[1:]:
            total = total + ref[at, :].astype(F32)
        out.ref[...] = total.astype(out.ref.dtype)
        out.put()


def pair_sum(one, two, at, out):
    out.ref[...] = (one[at, :].astype(F32) + two[at, :].astype(F32)).astype(out.ref.dtype)


def glue_first_body(ins, res, extra):
    bits, dd, dd2, du, du2 = ins
    d_keep, d_send, u_keep, u_send = res
    cut((dd(), dd2()), bits()[0], d_keep, d_send)
    d_send.put()
    cut((du(), du2()), bits()[1], u_keep, u_send)


def glue_far_body(ins, res, extra):
    bits, df, df_x, uf, uf_z = ins
    df_send, uf_send, uf_keep = res
    pair_sum(df(), df_x(), slice(0, df.ref.shape[0]), df_send)
    df_send.put()
    cut((uf(), uf_z()), bits()[0], uf_keep, uf_send)


def glue_second_body(ins, res, extra):
    bits, dn, dn2, un, un2 = ins
    dn_keep, dn_send, un_keep, un_send = res
    cut((dn(), dn2()), bits()[0], dn_keep, dn_send)
    cut((un(), un2()), bits()[1], un_keep, un_send)


def glue_near_body(ins, res, extra):
    bits, dn, dn_x, df_y, un, un_z, uf, uf_x = ins
    dn_keep, dn_send, un_keep, un_send, uf_sum = res
    cut((dn(), dn_x(), df_y()), bits()[1], dn_keep, dn_send)
    cut((un(), un_z()), bits()[0], un_keep, un_send)
    pair_sum(uf(), uf_x(), slice(0, uf.ref.shape[0]), uf_sum)


def glue_third_body(ins, res, extra):
    bits, da, da2 = ins
    n = res[0].ref.shape[0]
    for k, out in enumerate(res):
        pair_sum(da(), da2(), slice(k * n, (k + 1) * n), out)
        out.put()


def glue_fourth_body(ins, res, extra):
    bits, dn, dn_z, un, un_x, uf_y = ins
    keep, send = res
    n = keep.ref.shape[0] // 2
    cut((dn(), dn_z()), bits()[2], PartOf(keep, 0, n), PartOf(send, 0, n))
    cut((un(), un_x(), uf_y()), bits()[2], PartOf(keep, n, n), PartOf(send, n, n))


def quarter_of(bits, m):
    return (bits[0] ^ (m & 1)) * 2 + (bits[1] ^ (m >> 1))


def glue_fifth_body(which):
    def body(ins, res, extra):
        bits, da, da2, far = ins
        n = res[0].ref.shape[0]
        a, b, far_ref = da(), da2(), far()
        for m in (1, 2, 3, 0):
            out = res[m]
            at = quarter_of(bits(), m)
            rows = pl.ds(pl.multiple_of(which * 4 * n + at * n, n), n)
            part = pl.ds(pl.multiple_of(at * n, n), n)
            total = a[rows, :] + b[rows, :].astype(F32) + far_ref[part, :].astype(F32)
            out.ref[...] = total.astype(out.ref.dtype)
            out.put()

    return body


def join_body(ins, res, extra):
    bits, d_own, d_x, u_own, u_z, *quarters = ins
    d_out, u_out, q_out, o_out = res
    n = d_own.ref.shape[0]
    for own, other, out, bit in ((d_own, d_x, d_out, 0), (u_own, u_z, u_out, 1)):
        for item, at in zip((own, other), halves_at(bits()[bit], n)):
            out.ref[at, :] = item()[...].astype(F32)
        out.put()
    n = quarters[0].ref.shape[0]
    for m, item in enumerate(quarters):
        at = quarter_of(bits(), m)
        half = n // 2
        ref = item()
        q_out.ref[pl.ds(pl.multiple_of(at * half, half), half), :] = ref[:half, :].astype(F32)
        value = ref[half:, :].astype(F32)

        @pl.when(at < 2)
        def _():
            q_out.ref[pl.ds(pl.multiple_of(4 * half + at * half, half), half), :] = value

        @pl.when(at >= 2)
        def _():
            o_out.ref[pl.ds(pl.multiple_of((at - 2) * half, half), half), :] = value


def last_body(ins, res, extra):
    t, feats, inner, ibias, outer, grad, small = ins
    g_inner, g_ibias, g_outer, g_obias, *vectors, own_bup, own_q, own_v = res
    outer_w = outer()[...].astype(F32)
    pre = exact(feats()[...], inner()[...].astype(F32), NN) + vector(ibias)
    gate = 1.0 / (1.0 + jnp.exp(-pre))
    g = grad()[...]
    g_outer.ref[...] = exact(pre * gate, g, TN)
    g_outer.put()
    g_obias.ref[...] = jnp.sum(g, axis=0)
    hidden = exact(g, outer_w, NT) * (gate * (1.0 + pre * (1.0 - gate)))
    g_inner.ref[...] = exact(feats()[...], hidden, TN)
    g_ibias.ref[...] = jnp.sum(hidden, axis=0)
    small_ref = small()
    for i, out in enumerate(vectors):
        out.ref[...] = small_ref[i, :]
    own_bup.ref[...] = small_ref[pl.ds(8 + t()[0], 1), :].reshape(own_bup.ref.shape)
    for k, out in enumerate((own_q, own_v)):
        out.ref[...] = small_ref[pl.ds(12 + 4 * k + t()[0], 1), :]


def time_features(timesteps, width):
    half = width // 2
    frequency = jnp.exp(-math.log(10000.0) * jnp.arange(half, dtype=F32) / half)
    angles = timesteps.astype(F32)[:, None] * frequency[None, :]
    return jnp.concatenate([jnp.cos(angles), jnp.sin(angles)], axis=1)


def swap(value, axis, size, bit):
    return lax.ppermute(value, axis, [(i, i ^ bit) for i in range(size)])


def tie(value, *others):
    return lax.optimization_barrier((value,) + others)[0]


def halves(bit_set, mine, other):
    low = jnp.where(bit_set, other, mine)
    high = jnp.where(bit_set, mine, other)
    return low, high


def tie(value, *others):
    return lax.optimization_barrier((value,) + others)[0]


def sync(*values):
    return lax.optimization_barrier(values)


def local(dp, tensor, *args):
    (
        tokens, timesteps, lengths, time_inner, time_ibias, time_outer, time_obias, qkv_weight,
        qv_bias, out_weight, out_bias, gain_first, shift_first, up_weight, up_bias, down_weight,
        down_bias, gain_second, shift_second, cotangent,
    ) = args
    rows, width = tokens.shape
    seqs = rows // L
    w = qkv_weight.shape[2]
    hid = up_weight.shape[0]
    t = lax.axis_index("tensor")
    d = lax.axis_index("dp")
    high = list(range(3, dp.bit_length() - 1))
    core = lambda v: swap(v, "tensor", tensor, 1)
    across = lambda v: swap(v, "tensor", tensor, 2)

    j0 = (d & 1) == 1
    j1 = ((d >> 1) & 1) == 1
    own_j = (d & 3)[None]
    own_bits = jnp.stack([d & 1, (d >> 1) & 1, (d >> 2) & 1])
    flat_qkv = jnp.transpose(qkv_weight, (1, 2, 0)).reshape(3 * w, width)
    part_a = [flat_qkv[:w], flat_qkv[w : 2 * w], flat_qkv[2 * w :], out_weight]
    h2 = hid // 2
    part_f = [up_weight[:h2], up_weight[h2:], down_weight[:h2], down_weight[h2:]]

    def pick(parts, j0, j1):
        return jnp.where(j1, jnp.where(j0, parts[3], parts[2]), jnp.where(j0, parts[1], parts[0]))

    def spread(got):
        return [swap(got, "dp", dp, m) for m in (1, 2)]

    a_y = across(pick(part_a, j0, j1))
    qkv_core, out_core = core(flat_qkv), core(out_weight)
    bias = jnp.concatenate(
        [
            jnp.pad(qv_bias, ((0, 0), (0, width - w))),
            jnp.pad(up_bias[None], ((0, 13), (0, 0))),
        ],
        axis=0,
    )
    bias_core, bias_y = core(bias), across(bias)

    features = time_features(timesteps, time_inner.shape[0])
    hidden_time = jax.nn.silu(
        exact(features, time_inner.astype(F32), NN) + time_ibias.astype(F32)
    )
    temb = exact(hidden_time, time_outer.astype(F32), NN) + time_obias.astype(F32)
    temb = jnp.pad(temb, ((0, 8 - seqs), (0, 0))) if seqs < 8 else temb
    own_len = lax.dynamic_slice(lengths, (t * seqs,), (seqs,))

    a_y2 = across(pick(part_a, ~j0, ~j1))
    a_others = spread(a_y)
    send_f, a_y2 = sync(pick(part_f, j0, j1), a_y2)
    a_others.append(a_y2)
    bias_y2 = core(bias_y)
    f_y = across(send_f)
    wide = 2 * w
    pairs = wide // (2 * HD)
    act_shapes = [
        sds((rows, 3 * wide), BF),
        sds((seqs * pairs, 2 * L, L), F32),
        sds((rows, wide), BF),
    ]
    full = sds((rows, width), F32)
    low_full = sds((rows, width), BF)
    attn_flops = 2 * rows * width * 4 * wide + 4 * rows * L * wide
    x, qkv_n, p_n, mix_n, acc_n = call(
        attn_near_body, [low_full] + act_shapes + [full],
        (own_len, tokens, temb, flat_qkv, qkv_core, bias, bias_core, out_weight, out_core),
        attn_flops, smem=(0,),
    )
    acc_n, bias_y2, f_y, *far_a1 = sync(acc_n, bias_y2, f_y, a_y, *a_others)
    far_a2 = [core(v) for v in far_a1]
    send_f, f_y, acc_n, up_own, down_own, *far_a2 = sync(
        pick(part_f, ~j0, ~j1), f_y, acc_n, up_weight, down_weight, *far_a2
    )
    f_others = spread(f_y)
    f_others.append(across(send_f))
    up_core, down_core = core(up_own), core(down_own)
    wt = pltpu.VMEM((4 * w, width), BF)
    qkv_f, p_f, mix_f, first, normed = call(
        attn_far_body, act_shapes + [full, low_full],
        (
            own_len, own_j, x, *far_a1, *far_a2, bias_y, bias_y2, acc_n,
            tokens, temb, out_bias, gain_first, shift_first,
        ),
        attn_flops, smem=(0, 1), scratch=[wt, wt], place=far_places(1, 3, 0),
    )
    normed, up_core, down_core, *far_f1 = sync(normed, up_core, down_core, f_y, *f_others)
    far_f2 = [core(v) for v in far_f1]
    up_core, down_core = up_core, down_core
    mlp_flops = 2 * rows * width * 4 * hid
    (mlp_n,) = call(
        mlp_near_body, [full],
        (normed, up_weight, up_core, down_weight, down_core, bias, bias_core), mlp_flops,
    )
    mlp_n, *far_f2 = sync(mlp_n, *far_f2)
    mat = pltpu.VMEM((2 * hid, width), BF)
    dw_far = sds((hid, width), BF)
    dw_own = sds((hid, width), F32)
    bsum = sds((1, hid), F32)
    dws = [dw_far, dw_far, dw_own, dw_own, bsum, bsum]
    sums_shape = sds((8, width), F32)
    duf2, ddf2, duf, ddf, bup_f2, bup_f, layer_out, g2_low, sums2, g2 = call(
        mlp_far_body, dws + [low_full, low_full, sums_shape, full],
        (
            own_j, normed, *far_f1, *far_f2, bias_y, bias_y2, mlp_n,
            first, cotangent, gain_first, shift_first, down_bias, gain_second, shift_second,
        ),
        3 * mlp_flops, smem=(0,),
        scratch=[
            mat, mat, mat, mat, pltpu.VMEM((rows, 2 * hid), BF), pltpu.VMEM((rows, 2 * hid), F32),
            pltpu.VMEM((rows, width), F32),
        ],
        place=far_places(0, 2, 0),
    )
    f32 = lambda v: v.astype(F32)

    part = lambda k, dtype: sds((hid // k, width), dtype)

    def glue(body, outs, args):
        return call(body, outs, (own_bits,) + args, 1, smem=(0,), limit=LOW, window=12)

    df_keep, df_send, uf_keep, uf_send = glue(
        glue_first_body, [part(2, F32), part(2, BF), part(2, F32), part(2, BF)],
        (ddf, core(ddf2), duf, core(duf2)),
    )
    g2_low, df_keep, df_send, uf_keep, uf_send = sync(g2_low, df_keep, df_send, uf_keep, uf_send)
    along = lambda v, m: swap(v, "dp", dp, m)
    df_x = along(df_send, 1)
    uf_z = along(uf_send, 2)
    dun2, ddn2, dun, ddn, bup_n2, bup_n, g1, g1_low, sums1 = call(
        mlp_bwd_near_body, dws + [full, low_full, sums_shape],
        (
            normed, up_weight, up_core, g2_low, down_weight, down_core, g2, first, gain_first, bias,
            bias_core,
        ),
        2 * mlp_flops, limit=LOW, place={**near_places(1, 0), **near_places(4, 1)},
        scratch=[mat, mat, pltpu.VMEM((rows, 2 * hid), BF), pltpu.VMEM((rows, 2 * hid), F32)],
    )
    dun2, ddn2, df_x, uf_z = sync(dun2, ddn2, df_x, uf_z)
    near2 = core(ddn2), core(dun2)
    df_send, uf_send, uf_keep = glue(
        glue_far_body, [part(2, BF), part(4, BF), part(4, F32)], (df_keep, df_x, uf_keep, uf_z)
    )
    dn_keep, dn_send, un_keep, un_send = glue(
        glue_second_body, [part(2, F32), part(2, BF)] * 2, (ddn, near2[0], dun, near2[1])
    )
    g1_low, dn_keep, dn_send, un_keep, un_send, df_send, uf_keep, uf_send = sync(
        g1_low, dn_keep, dn_send, un_keep, un_send, df_send, uf_keep, uf_send
    )
    dn_x, uf_x = along(dn_send, 1), along(uf_send, 1)
    un_z = along(un_send, 2)
    df_y = across(df_send)
    da_shapes = [sds((4 * w, width), BF), sds((4 * w, width), F32), sds((8, wide), F32)]
    bwd_scratch = [pltpu.VMEM((rows, wide), BF), pltpu.VMEM((rows, 3 * wide), BF)]
    daf2, daf, qvb_f, gin_f = call(
        attn_bwd_far_body, da_shapes + [full],
        (own_j, g1_low, *far_a1, *far_a2, mix_f, qkv_f, p_f, x), 2 * attn_flops, limit=LOW,
        smem=(0,), scratch=[wt, wt] + bwd_scratch, place=far_places(0, 2, 0),
    )
    daf2, gin_f, dn_x, uf_x, un_z, df_y = sync(daf2, gin_f, dn_x, uf_x, un_z, df_y)
    qpart = lambda k, dtype: sds((4 * w // k, width), dtype)
    far_a2nd = core(daf2)
    dn_keep, dn_send, un_keep, un_send, uf_sum = glue(
        glue_near_body, [part(4, F32), part(4, BF)] * 2 + [part(4, BF)],
        (dn_keep, dn_x, df_y, un_keep, un_z, uf_keep, uf_x),
    )
    a_lo, a_hi = glue(glue_third_body, [qpart(2, BF)] * 2, (daf, far_a2nd))
    g1_low, a_lo, a_hi, dn_keep, dn_send, un_keep, un_send, uf_sum = sync(
        g1_low, a_lo, a_hi, dn_keep, dn_send, un_keep, un_send, uf_sum
    )
    a_lo = across(a_lo)
    uf_y = across(uf_sum)
    a_hi = across(a_hi)
    dn_z = along(dn_send, 2)
    un_x = along(un_send, 1)
    steps_row = jnp.pad(timesteps.astype(F32), (0, width - seqs))[None, :]
    dan2, dan, grad_tokens, pack = call(
        attn_bwd_near_body, da_shapes[:2] + [full, sds((32, width), F32)],
        (
            t[None], g1_low, out_weight, out_core, mix_n, qkv_n, p_n, x, flat_qkv, qkv_core, gin_f, g1,
            sums2, sums1, bup_n, bup_n2, bup_f, bup_f2, qvb_f, steps_row,
        ),
        2 * attn_flops, limit=LOW, smem=(0,), scratch=bwd_scratch + [pltpu.VMEM((8, wide), F32)],
    )
    dan2, pack, a_lo, uf_y, dn_z, un_x = sync(dan2, pack, a_lo, uf_y, dn_z, un_x)

    cat = lambda *v: jnp.concatenate(v, axis=0)
    near_a2, pack_c = core(dan2), core(pack)
    du_keep, du_send = glue(
        glue_fourth_body, [part(4, F32), part(4, BF)], (dn_keep, dn_z, un_keep, un_x, uf_y)
    )

    def halve(value, which):
        n = value.shape[0] // 2
        at = jnp.where(((d >> which) & 1) == 1, n, 0)
        keep = lax.dynamic_slice_in_dim(value, at, n, 0)
        return keep, lax.dynamic_slice_in_dim(value, n - at, n, 0).astype(BF)

    def high_sum(value):
        for which in high:
            keep, send = halve(value, which)
            value = keep + f32(along(send, 1 << which))
        return value

    def join_bit(value, which, other=None):
        other = along(value, 1 << which) if other is None else other
        return cat(*halves(((d >> which) & 1) == 1, value, other))

    def high_join(value):
        for which in high[::-1]:
            value = join_bit(value, which)
        return value

    two = lambda f, v: cat(f(v[: v.shape[0] // 2]), f(v[v.shape[0] // 2 :]))
    du_z = along(du_send, 4)
    cut_half = lambda which, far: glue(
        glue_fifth_body(which), [qpart(8, F32)] + [qpart(8, BF)] * 3, (dan, near_a2, far)
    )
    pack, pack_c = sync(pack, pack_c)
    state = [pack[:24] + pack_c[:24], cat(*halves((t & 1) == 1, pack[24:], pack_c[24:]))]

    def small_hop(which):
        small, gath = state
        other = along(cat(small, gath), 1 << which)
        state[:] = [small + other[:24], join_bit(gath, which, other[24:])]

    small_hop(2)
    q_lo = cut_half(0, a_lo)
    got_lo = [along(q_lo[m], m) for m in (1, 2, 3)]
    near_a2, a_hi, *rest = sync(near_a2, a_hi, *state, *got_lo)
    state[:], got_lo = rest[:2], rest[2:]

    du = two(high_sum, du_keep + f32(du_z))
    du = two(high_join, du.astype(BF))
    du_z = along(du, 4)
    q_hi = cut_half(1, a_hi)
    got_hi = [along(q_hi[m], m) for m in (1, 2, 3)]
    small_hop(1)
    du, du_z, *rest = sync(du, du_z, *state, *got_hi)
    state[:], got_hi = rest[:2], rest[2:]

    a_sum = cat(
        q_lo[0] + sum(f32(v) for v in got_lo), q_hi[0] + sum(f32(v) for v in got_hi)
    ).astype(BF)
    a_z = along(a_sum, 4)
    n = du.shape[0] // 2
    d_own, u_own = join_bit(du[:n], 2, du_z[:n]), join_bit(du[n:], 2, du_z[n:])
    d_z, u_x = along(d_own, 2), along(u_own, 1)
    small_hop(0)
    a_sum, a_z, d_own, u_own, d_z, u_x, *state[:] = sync(
        a_sum, a_z, d_own, u_own, d_z, u_x, *state
    )
    a_end = (f32(a_sum) + f32(a_z)).astype(BF)
    for which in high:
        a_end = (f32(a_end) + f32(along(a_end, 1 << which))).astype(BF)
        small_hop(which)
    d_own, u_own = join_bit(d_own, 1, d_z), join_bit(u_own, 0, u_x)
    d_x, u_z = along(d_own, 1), along(u_own, 2)
    other = across(cat(*state))
    state[:] = [state[0] + other[:24], cat(*halves((t & 2) == 2, state[1], other[24:]))]
    a_got = [along(a_end, m) for m in (1, 2, 3)]

    small, gath = state
    gath = gath.reshape(dp, tensor, 8, width)
    feats = time_features(gath[:, :, 7, :seqs].reshape(-1), time_inner.shape[0])
    line = sds((width,), F32)
    row = sds((1, width), F32)
    (
        grad_tinner, grad_tibias, grad_touter, grad_tobias, gsecond, ssecond, bdown, gfirst, sfirst,
        bout, own_bup, own_q, own_v,
    ) = call(
        last_body,
        [sds(time_inner.shape, F32), sds(time_ibias.shape, F32), sds(time_outer.shape, F32)]
        + [line] * 8 + [row] * 2,
        (
            t[None], feats, time_inner, time_ibias, time_outer,
            gath[:, :, :seqs].reshape(-1, width), small,
        ),
        1, smem=(0,), window=8, limit=LOW,
    )
    a_end, d_x, u_z, grad_touter, *a_got = sync(a_end, d_x, u_z, grad_touter, *a_got)
    d_all, u_all, q_all, o_all = call(
        join_body, [part(1, F32)] * 2 + [sds((3 * w, width), F32), sds((w, width), F32)],
        (own_bits, d_own, d_x, u_own, u_z, a_end, *a_got), 1, smem=(0,), window=16,
    )

    grad_qkv = jnp.transpose(q_all.reshape(3, w, width), (2, 0, 1))
    return (
        layer_out,
        grad_tokens,
        grad_tinner,
        grad_tibias,
        grad_touter,
        grad_tobias,
        grad_qkv,
        jnp.concatenate([own_q[:, :w], own_v[:, :w]], axis=0),
        o_all,
        bout,
        gfirst,
        sfirst,
        u_all,
        own_bup,
        d_all,
        bdown,
        gsecond,
        ssecond,
    )


def solution(mesh):
    both = ("dp", "tensor")
    placed = (
        P(both, None), P(both), P("dp"), P(), P(), P(), P(), P(None, None, "tensor"),
        P(None, "tensor"), P("tensor", None), P(), P(), P(), P("tensor", None), P("tensor"),
        P("tensor", None), P(), P(), P(), P(both, None),
    )
    return jax.shard_map(
        functools.partial(local, mesh.shape["dp"], mesh.shape["tensor"]),
        mesh=mesh,
        in_specs=placed,
        out_specs=(
            P(both, None), P(both, None), P(), P(), P(), P(), P(None, None, "tensor"),
            P(None, "tensor"), P("tensor", None), P(), P(), P(), P("tensor", None), P("tensor"),
            P("tensor", None), P(), P(), P(),
        ),
        check_vma=False,
    )
```
